32 devices in a mesh: row: 8 (over z, y), col: 4 (over x, core).
Axes of the slice: x: 2, y: 2, z: 4, core: 2. Of those that a mesh axis runs over, the one named last changes fastest.
Arguments:
- blocks: float32 [8, 4, 8, 128, 128], P('row', 'col'), may hold values from -1.2 to 1.2
- block_rows: int32 [8, 4, 8], P('row', 'col'), may hold values from -1 to 63, as said below
- block_cols: int32 [8, 4, 8], P('row', 'col'), may hold values from -1 to 127, as said below
Outputs:
- square_part: float32 [8, 4, 8, 128, 128], P('row', 'col')
The draws below stay inside these ranges and needn't reach their ends.
Inputs may be any that keep to these rules, and one draw needn't show every extreme that they name: Empty slots have -1 in block_rows and block_cols alike; a used slot has a block row below 64; no block is listed twice in one tile. At most 4 used slots of one tile share a block row, and some tile has a block row with exactly 4. Some tile uses all 8 slots, and some tile has empty slots. `block_cols`: the two lists describe the same slots; a used slot has a block column below 128.
All inputs are finite; a program needn't handle non-finite values.
Results may differ from the reference program's by a relative error of at most 0.0003.
Values sent between devices are 32-bit elements; how exact they have to be, the bound alone decides.
No kernel may reach another device: no remote copies, remote signals or barrier semaphores. Data moves between devices by JAX's collectives and lax.ppermute only.
A program may use at most 64 MiB of HBM per device.

```python
import jax
import jax.numpy as jnp
from jax import lax

BS = 128
NBLK = 512
ACT = 2
SECTIONS = 4
TILE_ROWS = 8
TILE_COLS = 4
RB = 64
CB = 128
SLOTS = 8
QMAX = 4
N_ROW = 8
N_COL = 4


def block_pattern(key):
    base = jax.random.fold_in(key, 47)
    keys = jax.random.split(base, 8)
    reach = max(NBLK // 56, 2)
    tile_count = N_ROW * N_COL
    span = RB * CB
    order = jax.random.permutation(keys[0], NBLK).astype(jnp.int32)
    distance = jnp.abs(order[:, None] - order[None, :])
    coin = jax.random.randint(keys[1], (NBLK, NBLK), 0, reach + 1).astype(jnp.int32)
    band = (distance <= reach) & (coin >= distance)
    identity = jnp.arange(NBLK, dtype=jnp.int32)
    diagonal = identity[:, None] == identity[None, :]
    band_tiles = band.reshape(N_ROW, RB, N_COL, CB).transpose(0, 2, 1, 3)
    diagonal_tiles = diagonal.reshape(N_ROW, RB, N_COL, CB).transpose(0, 2, 1, 3)
    forced_flat = jax.random.randint(keys[2], (), 0, tile_count).astype(jnp.int32)
    sparse_flat = (forced_flat + 1 + jax.random.randint(keys[3], (), 0, tile_count - 1).astype(jnp.int32)) % tile_count
    tile_flat = jnp.arange(tile_count, dtype=jnp.int32).reshape(N_ROW, N_COL)
    forced_tile = tile_flat == forced_flat
    first_row = RB - 1 - jax.random.randint(keys[4], (), 0, ACT).astype(jnp.int32)
    local_rows = jnp.arange(RB, dtype=jnp.int32)
    offset_rows = (local_rows - first_row) % RB
    in_forced_row = offset_rows < ACT
    column_perms = jax.vmap(lambda one: jax.random.permutation(one, CB))(jax.random.split(keys[5], ACT)).astype(jnp.int32)
    column_perms = (column_perms + (CB - 1 - column_perms[:, 0:1])) % CB
    column_ranks = jnp.argsort(column_perms, axis=1).astype(jnp.int32)
    row_ranks = column_ranks[jnp.minimum(offset_rows, ACT - 1)]
    forced_local = in_forced_row[:, None] & (row_ranks < QMAX)
    forced = forced_tile[:, :, None, None] & forced_local[None, None, :, :]
    live = band_tiles | forced
    tiebreak = jax.vmap(lambda one: jax.random.permutation(one, span))(jax.random.split(keys[6], tile_count))
    tiebreak = tiebreak.astype(jnp.int32).reshape(N_ROW, N_COL, RB, CB)
    kind = jnp.where(forced, 0, jnp.where(diagonal_tiles, 1, 2)).astype(jnp.int32)
    score = jnp.where(live, kind * span + tiebreak, 3 * span + tiebreak)
    row_order = jnp.argsort(score, axis=-1).astype(jnp.int32)
    row_place = jnp.argsort(row_order, axis=-1).astype(jnp.int32)
    kept = live & (row_place < QMAX)
    tile_score = jnp.where(kept, score, 3 * span + tiebreak).reshape(N_ROW, N_COL, span)
    picked = jnp.argsort(tile_score, axis=-1).astype(jnp.int32)[:, :, :SLOTS]
    used = jnp.take_along_axis(kept.reshape(N_ROW, N_COL, span), picked, axis=-1)
    limit = jnp.where(tile_flat == sparse_flat, SLOTS // 2, SLOTS).astype(jnp.int32)
    used = used & (jnp.arange(SLOTS, dtype=jnp.int32)[None, None, :] < limit[:, :, None])
    rows_out = jnp.where(used, picked // CB, -1).astype(jnp.int32)
    cols_out = jnp.where(used, picked % CB, -1).astype(jnp.int32)
    shuffles = jax.vmap(lambda one: jax.random.permutation(one, SLOTS))(jax.random.split(keys[7], tile_count))
    shuffles = shuffles.astype(jnp.int32).reshape(N_ROW, N_COL, SLOTS)
    return (jnp.take_along_axis(rows_out, shuffles, axis=-1), jnp.take_along_axis(cols_out, shuffles, axis=-1))


def draw_block_rows(key, part):
    return block_pattern(key)[0].astype(jnp.int32)


def draw_block_cols(key, part):
    return block_pattern(key)[1].astype(jnp.int32)


def block_levels(key, extent, cuts, least, top_value):
    def one(axis_at, shards_of):
        draws = jax.random.uniform(jax.random.fold_in(jax.random.fold_in(key, 6), axis_at), (shards_of,), jnp.float32, least / len(cuts), top_value / len(cuts))
        return jnp.repeat(jnp.exp(draws), extent[axis_at] // shards_of).reshape((-1,) + (1,) * (len(extent) - axis_at - 1))

    factor_of = one(*cuts[0])
    for cut in cuts[1:]:
        factor_of = factor_of * one(*cut)
    return factor_of


def scatter_about(key, extent, scale, most, pieces=(), held_as=jnp.bfloat16):
    array = scale * jax.random.normal(key, extent, jnp.float32)
    if pieces:
        array = array * block_levels(key, extent, pieces, -0.22, 0.18)
    return jnp.clip(array, -most, most).astype(held_as)


def setup_inputs(seed: int = 0) -> dict:
    splits = jax.random.split(jax.random.key(seed), 4)
    blocks = scatter_about(splits[0], (TILE_ROWS, TILE_COLS, SLOTS, BS, BS), 0.2, 1.2, ((0, 8), (1, 4)), jnp.float32)
    block_rows = draw_block_rows(jax.random.fold_in(splits[3], 71), 0)
    block_cols = draw_block_cols(jax.random.fold_in(splits[3], 71), 0)
    return {"blocks": blocks, "block_rows": block_rows, "block_cols": block_cols}


def section_product(panel, pair, out_rows, out_cols, depth):
    panel_vals, panel_rows, panel_cols = panel
    pair_vals, pair_inner, pair_cols = pair
    panel_iota = jnp.arange(panel_rows.shape[0], dtype=jnp.int32)
    pair_iota = jnp.arange(pair_inner.shape[0], dtype=jnp.int32)
    depth_iota = jnp.arange(depth, dtype=jnp.int32)
    panel_live = panel_rows >= 0
    earlier = (panel_rows[None, :] == panel_rows[:, None]) & panel_live[None, :] & (panel_iota[None, :] < panel_iota[:, None])
    within = jnp.sum(earlier.astype(jnp.int32), axis=1)
    picked = (panel_rows[None, None, :] == out_rows[:, None, None]) & (within[None, None, :] == depth_iota[None, :, None])
    picked = picked & panel_live[None, None, :] & (out_rows >= 0)[:, None, None]
    picked_int = picked.astype(jnp.int32)
    panel_slot = jnp.sum(picked_int * panel_iota[None, None, :], axis=2)
    found = jnp.sum(picked_int, axis=2) > 0
    inner = jnp.sum(picked_int * panel_cols[None, None, :], axis=2)
    matched = (pair_inner[None, None, :] == inner[:, :, None]) & (pair_cols[None, None, :] == out_cols[:, None, None])
    matched = matched & (pair_inner >= 0)[None, None, :] & found[:, :, None]
    matched_int = matched.astype(jnp.int32)
    pair_slot = jnp.sum(matched_int * pair_iota[None, None, :], axis=2)
    weight = (jnp.sum(matched_int, axis=2) > 0).astype(jnp.float32)
    left = panel_vals[panel_slot] * weight[:, :, None, None]
    right = pair_vals[pair_slot]
    return jnp.einsum("tqij,tqjk->tik", left, right, precision=lax.Precision.HIGHEST, preferred_element_type=jnp.float32)


def make_pair(first, second, row_span):
    inner = jnp.concatenate([first[1], jnp.where(second[1] >= 0, second[1] + row_span, -1)])
    return (jnp.concatenate([first[0], second[0]]), inner, jnp.concatenate([first[2], second[2]]))


def reference(blocks, block_rows, block_cols):
    row_span = NBLK // N_ROW

    def one_tile(flat):
        row_index = flat // N_COL
        col_index = flat % N_COL
        total = jnp.zeros((SLOTS, BS, BS), jnp.float32)
        for section in range(SECTIONS):
            root = (row_index // 2 + section) % N_COL
            panel = (blocks[row_index, root], block_rows[row_index, root], block_cols[row_index, root])
            upper = 2 * root
            first = (blocks[upper, col_index], block_rows[upper, col_index], block_cols[upper, col_index])
            second = (blocks[upper + 1, col_index], block_rows[upper + 1, col_index], block_cols[upper + 1, col_index])
            pair = make_pair(first, second, row_span)
            total = total + section_product(panel, pair, block_rows[row_index, col_index], block_cols[row_index, col_index], 2 * ACT)
        return total

    tiles = lax.map(one_tile, jnp.arange(N_ROW * N_COL, dtype=jnp.int32))
    return tiles.reshape(N_ROW, N_COL, SLOTS, BS, BS)
```

```python
import jax
import jax.numpy as jnp
from jax import lax
from jax.experimental import pallas as pl
from jax.experimental.pallas import tpu as pltpu
from jax.sharding import PartitionSpec as P

NBLK = 512
ACT = 2
SECTIONS = 4
BS = 128
SLOTS = 8
CAP = 8
VMEM_LIMIT = 32 * 1024 * 1024


def from_root(x, axis, root):
    mine = lax.axis_index(axis) == root
    return lax.psum(jnp.where(mine, x, jnp.zeros_like(x)), axis)


def from_partner(x, axis, bit):
    return lax.ppermute(x, axis, [(i, i ^ 1 << bit) for i in range(lax.axis_size(axis))])


def shifted(value, axis, steps):
    count = lax.axis_size(axis)
    pairs = [(source, (source + steps) % count) for source in range(count)]
    return lax.ppermute(value, axis, pairs)


def section_product(panel, pair, out_rows, out_cols, depth):
    panel_vals, panel_rows, panel_cols = panel
    pair_vals, pair_inner, pair_cols = pair
    panel_iota = jnp.arange(panel_rows.shape[0], dtype=jnp.int32)
    pair_iota = jnp.arange(pair_inner.shape[0], dtype=jnp.int32)
    depth_iota = jnp.arange(depth, dtype=jnp.int32)
    panel_live = panel_rows >= 0
    earlier = (
        (panel_rows[None, :] == panel_rows[:, None])
        & panel_live[None, :]
        & (panel_iota[None, :] < panel_iota[:, None])
    )
    within = jnp.sum(earlier.astype(jnp.int32), axis=1)
    picked = (panel_rows[None, None, :] == out_rows[:, None, None]) & (
        within[None, None, :] == depth_iota[None, :, None]
    )
    picked = picked & panel_live[None, None, :] & (out_rows >= 0)[:, None, None]
    picked_int = picked.astype(jnp.int32)
    panel_slot = jnp.sum(picked_int * panel_iota[None, None, :], axis=2)
    found = jnp.sum(picked_int, axis=2) > 0
    inner = jnp.sum(picked_int * panel_cols[None, None, :], axis=2)
    matched = (pair_inner[None, None, :] == inner[:, :, None]) & (
        pair_cols[None, None, :] == out_cols[:, None, None]
    )
    matched = matched & (pair_inner >= 0)[None, None, :] & found[:, :, None]
    matched_int = matched.astype(jnp.int32)
    pair_slot = jnp.sum(matched_int * pair_iota[None, None, :], axis=2)
    weight = (jnp.sum(matched_int, axis=2) > 0).astype(jnp.float32)
    left = panel_vals[panel_slot] * weight[:, :, None, None]
    right = pair_vals[pair_slot]
    return jnp.einsum(
        "tqij,tqjk->tik",
        left,
        right,
        precision=lax.Precision.HIGHEST,
        preferred_element_type=jnp.float32,
    )


def make_pair(first, second, row_span):
    inner = jnp.concatenate([first[1], jnp.where(second[1] >= 0, second[1] + row_span, -1)])
    return (jnp.concatenate([first[0], second[0]]), inner, jnp.concatenate([first[2], second[2]]))


def order_pair(mine, other, is_even, row_span):
    first = tuple((jnp.where(is_even, one, two) for one, two in zip(mine, other)))
    second = tuple((jnp.where(is_even, two, one) for one, two in zip(mine, other)))
    return make_pair(first, second, row_span)


def fetch_panel(tile, row_index, col_count, section):
    root = (row_index // 2 + section) % col_count
    return tuple(from_root(one, "col", root) for one in tile)


def general_body(blocks, block_rows, block_cols):
    tile = (blocks[0, 0], block_rows[0, 0], block_cols[0, 0])
    row_count = lax.axis_size("row")
    col_count = lax.axis_size("col")
    row_span = NBLK // row_count
    row_index = lax.axis_index("row")
    is_even = row_index % 2 == 0
    depth = 2 * ACT
    total = jnp.zeros(blocks.shape[2:], jnp.float32)
    partner = from_partner((tile[0], tile[1], tile[2]), "row", 0)
    current = order_pair(tile, partner, is_even, row_span)
    for section in range(SECTIONS):
        panel = fetch_panel(tile, row_index, col_count, section)
        if section > 0:
            current = shifted((current[0], current[1], current[2]), "row", -2)
        total = total + section_product(panel, current, tile[1], tile[2], depth)
    return total[None, None]


def everything(x, axis):
    return lax.all_to_all(jnp.broadcast_to(x[None], (lax.axis_size(axis),) + x.shape), axis, 0, 0)


def whole_tiles(blocks, block_rows, block_cols):
    tile = (blocks[0, 0], block_rows[0, 0], block_cols[0, 0])
    row_span = NBLK // lax.axis_size("row")
    col_count = lax.axis_size("col")
    row_index = lax.axis_index("row")
    panels = tuple(everything(one, "col") for one in tile)
    column = tuple(everything(one, "row") for one in tile)

    def section(step, total):
        root = (row_index // 2 + step) % col_count
        take = lambda arrays, at: tuple(lax.dynamic_index_in_dim(a, at, 0, False) for a in arrays)
        pair = make_pair(take(column, 2 * root), take(column, 2 * root + 1), row_span)
        return total + section_product(take(panels, root), pair, tile[1], tile[2], 2 * ACT)

    total = lax.fori_loop(0, SECTIONS, section, jnp.zeros(blocks.shape[2:], jnp.float32))
    return total[None, None]


def spread_kernel(blocks_ref, rows_ref, cols_ref, out_ref):
    devices = out_ref.shape[0]
    q = BS // devices
    sub = lax.broadcasted_iota(jnp.int32, (SLOTS, SLOTS), 0)
    lane = lax.broadcasted_iota(jnp.int32, (SLOTS, SLOTS), 1)

    def column(ref):
        one = jnp.broadcast_to(ref[...].astype(jnp.float32), (SLOTS, SLOTS))
        return jnp.sum(jnp.where(sub == lane, one, 0.0), axis=1, keepdims=True)

    lanes = lax.broadcasted_iota(jnp.int32, (SLOTS, BS), 1)
    places = jnp.where(lanes == 0, column(rows_ref), jnp.where(lanes == 1, column(cols_ref), 0.0))
    for p in range(devices):
        for part in range(q):
            out_ref[p, :, part * BS : (part + 1) * BS] = blocks_ref[pl.ds(q * p + part, SLOTS, stride=BS), :]
        out_ref[p, :, q * BS : (q + 1) * BS] = places


def bf(x):
    return x.astype(jnp.bfloat16)


def mm(a, b, transposed=False):
    dims = (((1,), (1 if transposed else 0,)), ((), ()))
    return lax.dot_general(a, b, dims, preferred_element_type=jnp.float32)


def plan_kernel(rows, cols, piece_ref, send_ref, list_ref, most_ref):
    devices = rows * cols
    n = devices * SLOTS
    width = send_ref.shape[1]
    rb = NBLK // rows
    cb = NBLK // cols
    per_row = cols * SLOTS
    my_row, my_col = lax.axis_index("row"), lax.axis_index("col")
    me = my_row * cols + my_col

    idx = piece_ref[:, width : width + BS]
    idx_t = idx.T
    sub = lax.broadcasted_iota(jnp.int32, (n, 1), 0)
    lane = lax.broadcasted_iota(jnp.int32, (1, n), 1)

    def places(row, col, at):
        up = ((at // per_row) * rb).astype(jnp.float32)
        along = (((at // SLOTS) % cols) * cb).astype(jnp.float32)
        return jnp.where(row >= 0, row + up, -1.0), jnp.where(col >= 0, col + along, -2.0)

    row_c, col_c = places(idx[:, 0:1], idx[:, 1:2], sub)
    row_r, col_r = places(idx_t[0:1, :], idx_t[1:2, :], lane)

    same_row = bf(jnp.where(row_c == row_r, 1.0, 0.0))
    slot_r = (lane % SLOTS).astype(jnp.float32)
    same_col = bf(jnp.where(col_c == col_r, 1.0 + 16.0 * slot_r, 0.0))
    hit = mm(same_col, same_row)
    product = (row_c == col_r) & (hit > 0)
    product_b = bf(jnp.where(product, 1.0, 0.0))

    dev = lax.broadcasted_iota(jnp.int32, (devices, 1), 0)
    in_row = (lane // per_row) == (dev // cols)
    in_col = ((lane // SLOTS) % cols) == (dev % cols)
    own = (lane // SLOTS) == dev
    as_left = mm(bf(jnp.where(in_col, 1.0, 0.0)), product_b)
    as_right = mm(bf(jnp.where(in_row, 1.0, 0.0)), product_b, transposed=True)
    need = ((in_row & (as_left > 0)) | (in_col & (as_right > 0))) & jnp.logical_not(own)
    need_f = jnp.where(need, 1.0, 0.0)
    before = bf(jnp.where(sub < lane, 1.0, 0.0))
    pos = jnp.where(need, mm(bf(need_f), before), -1.0)
    most_ref[0, 0] = jnp.max(jnp.sum(need_f, axis=1, keepdims=True)).astype(jnp.int32)

    dev_r = lax.broadcasted_iota(jnp.int32, (1, devices), 1)
    repeat = bf(jnp.where((sub // CAP) == dev_r, 1.0, 0.0))
    chosen = bf(jnp.where(mm(repeat, bf(pos)) == (sub % CAP).astype(jnp.float32), 1.0, 0.0))
    data = piece_ref[:, :width]
    high = bf(data)
    low = bf(data - high.astype(jnp.float32))
    send_ref[...] = mm(chosen, high) + mm(chosen, low)

    my_pos = jnp.sum(jnp.where(dev == me, pos, 0.0), axis=0, keepdims=True)
    held_r = jnp.where((lane // SLOTS) == me, slot_r, SLOTS + my_pos)
    held_c = jnp.sum(jnp.where(sub == lane, held_r, 0.0), axis=1, keepdims=True)
    mine = product & (((sub // SLOTS) % cols) == my_col) & ((lane // per_row) == my_row)
    earlier = bf(jnp.where(lane < sub, 1.0, 0.0))
    rank = mm(earlier, bf(jnp.where(mine, 1.0, 0.0)))
    code = (hit - 1.0) * 16.0 + held_r * 16.0 + held_c + 1.0
    out_sub = lax.broadcasted_iota(jnp.int32, (list_ref.shape[0], 1), 0)
    listed = jnp.zeros(list_ref.shape, jnp.float32)
    for k in range(2 * ACT):
        one = jnp.sum(jnp.where(mine & (rank == k), code, 0.0), axis=0, keepdims=True)
        listed = jnp.where(out_sub == k, one, listed)
    list_ref[...] = listed.astype(jnp.int32) - 1


def product_kernel(rows, cols, list_ref, blocks_ref, piece_ref, out_ref, held_ref):
    devices = rows * cols
    q = BS // devices
    per_row = cols * SLOTS
    first = lax.axis_index("row") * per_row
    held_ref[: SLOTS * BS, :] = blocks_ref[...]
    for p in range(devices):
        for part in range(q):
            held_ref[pl.ds(SLOTS * BS + q * p + part, CAP, stride=BS), :] = piece_ref[
                p * CAP : (p + 1) * CAP, part * BS : (part + 1) * BS
            ]
    out_ref[...] = jnp.zeros_like(out_ref)

    def block(at):
        x = held_ref[pl.ds(pl.multiple_of(at * BS, BS), BS), :]
        high = bf(x)
        return high, bf(x - high.astype(jnp.float32))

    def entry(i, carry):
        for k in range(2 * ACT):
            code = list_ref[k, first + i]

            @pl.when(code >= 0)
            def _():
                a_high, a_low = block((code // 16) % 16)
                b_high, b_low = block(code % 16)
                at = pl.ds(pl.multiple_of((code // 256) * BS, BS), BS)
                out_ref[at, :] += mm(a_high, b_high) + (mm(a_high, b_low) + mm(a_low, b_high))

        return carry

    lax.fori_loop(0, per_row, entry, 0)


def packed_body(blocks, block_rows, block_cols):
    rows, cols = lax.axis_size("row"), lax.axis_size("col")
    devices = rows * cols
    n = devices * SLOTS
    q = BS // devices
    flat = blocks.reshape(SLOTS * BS, BS)
    params = pltpu.CompilerParams(vmem_limit_bytes=VMEM_LIMIT)
    vmem = pl.BlockSpec(memory_space=pltpu.VMEM)
    smem = pl.BlockSpec(memory_space=pltpu.SMEM)
    spread = pl.pallas_call(
        spread_kernel,
        out_shape=jax.ShapeDtypeStruct((devices, SLOTS, (q + 1) * BS), jnp.float32),
        in_specs=[vmem] * 3,
        out_specs=vmem,
        compiler_params=params,
        name="spread",
    )(flat, block_rows[0], block_cols[0])
    pieces = lax.all_to_all(spread, ("row", "col"), 0, 0).reshape(n, (q + 1) * BS)
    send, listed, most = pl.pallas_call(
        lambda *refs: plan_kernel(rows, cols, *refs),
        out_shape=(
            jax.ShapeDtypeStruct((devices * CAP, q * BS), jnp.float32),
            jax.ShapeDtypeStruct((8, n), jnp.int32),
            jax.ShapeDtypeStruct((1, 1), jnp.int32),
        ),
        in_specs=[vmem],
        out_specs=(vmem, vmem, smem),
        compiler_params=params,
        name="plan",
    )(pieces)

    def packed():
        got = lax.all_to_all(send.reshape(devices, CAP, q * BS), ("row", "col"), 0, 0)
        out = pl.pallas_call(
            lambda *refs: product_kernel(rows, cols, *refs),
            out_shape=jax.ShapeDtypeStruct((SLOTS * BS, BS), jnp.float32),
            in_specs=[smem, vmem, vmem],
            out_specs=vmem,
            scratch_shapes=[pltpu.VMEM(((SLOTS + CAP) * BS, BS), jnp.float32)],
            compiler_params=params,
            name="products",
        )(listed, flat, got.reshape(devices * CAP, q * BS))
        return out.reshape(blocks.shape)

    return lax.cond(most[0, 0] <= CAP, packed, lambda: whole_tiles(blocks, block_rows, block_cols))


def solution(mesh):
    small = mesh.shape["col"] == SECTIONS and mesh.devices.size * SLOTS <= 256
    return jax.shard_map(
        packed_body if small else general_body,
        mesh=mesh,
        in_specs=(P("row", "col", None, None, None), P("row", "col", None), P("row", "col", None)),
        out_specs=P("row", "col", None, None, None),
        check_vma=False,
    )
```

```python
import jax
import jax.numpy as jnp
from jax import lax
from jax.experimental import pallas as pl
from jax.experimental.pallas import tpu as pltpu
from jax.sharding import PartitionSpec as P

NBLK = 512
ACT = 2
SECTIONS = 4
BS = 128
SLOTS = 8
CAP = 8
ZCAP = 8
VMEM_LIMIT = 32 * 1024 * 1024


def from_root(x, axis, root):
    mine = lax.axis_index(axis) == root
    return lax.psum(jnp.where(mine, x, jnp.zeros_like(x)), axis)


def from_partner(x, axis, bit):
    return lax.ppermute(x, axis, [(i, i ^ 1 << bit) for i in range(lax.axis_size(axis))])


def shifted(value, axis, steps):
    count = lax.axis_size(axis)
    pairs = [(source, (source + steps) % count) for source in range(count)]
    return lax.ppermute(value, axis, pairs)


def section_product(panel, pair, out_rows, out_cols, depth):
    panel_vals, panel_rows, panel_cols = panel
    pair_vals, pair_inner, pair_cols = pair
    panel_iota = jnp.arange(panel_rows.shape[0], dtype=jnp.int32)
    pair_iota = jnp.arange(pair_inner.shape[0], dtype=jnp.int32)
    depth_iota = jnp.arange(depth, dtype=jnp.int32)
    panel_live = panel_rows >= 0
    earlier = (
        (panel_rows[None, :] == panel_rows[:, None])
        & panel_live[None, :]
        & (panel_iota[None, :] < panel_iota[:, None])
    )
    within = jnp.sum(earlier.astype(jnp.int32), axis=1)
    picked = (panel_rows[None, None, :] == out_rows[:, None, None]) & (
        within[None, None, :] == depth_iota[None, :, None]
    )
    picked = picked & panel_live[None, None, :] & (out_rows >= 0)[:, None, None]
    picked_int = picked.astype(jnp.int32)
    panel_slot = jnp.sum(picked_int * panel_iota[None, None, :], axis=2)
    found = jnp.sum(picked_int, axis=2) > 0
    inner = jnp.sum(picked_int * panel_cols[None, None, :], axis=2)
    matched = (pair_inner[None, None, :] == inner[:, :, None]) & (
        pair_cols[None, None, :] == out_cols[:, None, None]
    )
    matched = matched & (pair_inner >= 0)[None, None, :] & found[:, :, None]
    matched_int = matched.astype(jnp.int32)
    pair_slot = jnp.sum(matched_int * pair_iota[None, None, :], axis=2)
    weight = (jnp.sum(matched_int, axis=2) > 0).astype(jnp.float32)
    left = panel_vals[panel_slot] * weight[:, :, None, None]
    right = pair_vals[pair_slot]
    return jnp.einsum(
        "tqij,tqjk->tik",
        left,
        right,
        precision=lax.Precision.HIGHEST,
        preferred_element_type=jnp.float32,
    )


def make_pair(first, second, row_span):
    inner = jnp.concatenate([first[1], jnp.where(second[1] >= 0, second[1] + row_span, -1)])
    return (jnp.concatenate([first[0], second[0]]), inner, jnp.concatenate([first[2], second[2]]))


def order_pair(mine, other, is_even, row_span):
    first = tuple((jnp.where(is_even, one, two) for one, two in zip(mine, other)))
    second = tuple((jnp.where(is_even, two, one) for one, two in zip(mine, other)))
    return make_pair(first, second, row_span)


def fetch_panel(tile, row_index, col_count, section):
    root = (row_index // 2 + section) % col_count
    return tuple(from_root(one, "col", root) for one in tile)


def general_body(blocks, block_rows, block_cols):
    tile = (blocks[0, 0], block_rows[0, 0], block_cols[0, 0])
    row_count = lax.axis_size("row")
    col_count = lax.axis_size("col")
    row_span = NBLK // row_count
    row_index = lax.axis_index("row")
    is_even = row_index % 2 == 0
    depth = 2 * ACT
    total = jnp.zeros(blocks.shape[2:], jnp.float32)
    partner = from_partner((tile[0], tile[1], tile[2]), "row", 0)
    current = order_pair(tile, partner, is_even, row_span)
    for section in range(SECTIONS):
        panel = fetch_panel(tile, row_index, col_count, section)
        if section > 0:
            current = shifted((current[0], current[1], current[2]), "row", -2)
        total = total + section_product(panel, current, tile[1], tile[2], depth)
    return total[None, None]


def everything(x, axis):
    return lax.all_to_all(jnp.broadcast_to(x[None], (lax.axis_size(axis),) + x.shape), axis, 0, 0)


def whole_tiles(blocks, block_rows, block_cols):
    tile = (blocks[0, 0], block_rows[0, 0], block_cols[0, 0])
    row_span = NBLK // lax.axis_size(("z", "y"))
    col_count = lax.axis_size("col")
    row_index = lax.axis_index(("z", "y"))
    panels = tuple(everything(one, "col") for one in tile)
    column = tuple(everything(one, ("z", "y")) for one in tile)

    def section(step, total):
        root = (row_index // 2 + step) % col_count
        take = lambda arrays, at: tuple(lax.dynamic_index_in_dim(a, at, 0, False) for a in arrays)
        pair = make_pair(take(column, 2 * root), take(column, 2 * root + 1), row_span)
        return total + section_product(take(panels, root), pair, tile[1], tile[2], 2 * ACT)

    total = lax.fori_loop(0, SECTIONS, section, jnp.zeros(blocks.shape[2:], jnp.float32))
    return total[None, None]


def bf(x):
    return x.astype(jnp.bfloat16)


def ind(x):
    return bf(jnp.where(x, 1.0, 0.0))


def mm(a, b, transposed=False):
    dims = (((1,), (1 if transposed else 0,)), ((), ()))
    return lax.dot_general(a, b, dims, preferred_element_type=jnp.float32)


def plan_kernel(rows, cols, idx_ref, cross_ref, give_ref, list_ref, most_ref):
    devices = rows * cols
    planes = rows // 2
    plane = 2 * cols
    n = devices * SLOTS
    in_plane = plane * SLOTS
    rb = NBLK // rows
    cb = NBLK // cols
    per_row = cols * SLOTS
    my_plane = lax.axis_index("z")
    my_row = 2 * my_plane + lax.axis_index("y")
    my_col = lax.axis_index("col")
    me = my_row * cols + my_col

    sub = lax.broadcasted_iota(jnp.int32, (n, 1), 0)
    lane = lax.broadcasted_iota(jnp.int32, (1, n), 1)
    dev = lax.broadcasted_iota(jnp.int32, (devices, 1), 0)
    dev_r = lax.broadcasted_iota(jnp.int32, (1, devices), 1)
    slot = lax.broadcasted_iota(jnp.int32, (1, SLOTS), 1)
    diagonal = sub == lane

    def as_row(column):
        return jnp.sum(jnp.where(diagonal, column, 0.0), axis=0, keepdims=True)

    def as_column(row):
        return jnp.sum(jnp.where(diagonal, row, 0.0), axis=1, keepdims=True)

    repeat = ind((sub // SLOTS) == dev_r)

    def column(k):
        values = mm(repeat, bf(idx_ref[:, k, :].astype(jnp.float32)))
        return jnp.sum(jnp.where((sub % SLOTS) == slot, values, 0.0), axis=1, keepdims=True)

    up = ((sub // per_row) * rb).astype(jnp.float32)
    along = (((sub // SLOTS) % cols) * cb).astype(jnp.float32)
    row_c, col_c = column(0), column(1)
    row_c = jnp.where(row_c >= 0, row_c + up, -1.0)
    col_c = jnp.where(col_c >= 0, col_c + along, -2.0)
    row_r, col_r = as_row(row_c), as_row(col_c)

    slot_r = (lane % SLOTS).astype(jnp.float32)
    hit = mm(bf(jnp.where(col_c == col_r, 1.0 + 16.0 * slot_r, 0.0)), ind(row_c == row_r))
    product = (row_c == col_r) & (hit > 0)
    product_b = ind(product)

    in_row = (lane // per_row) == (dev // cols)
    in_col = ((lane // SLOTS) % cols) == (dev % cols)
    as_left = mm(ind(in_col), product_b)
    as_right = mm(ind(in_row), product_b, transposed=True)
    need = (in_row & (as_left > 0)) | (in_col & (as_right > 0))
    need = need & ((lane // SLOTS) != dev)
    before = sub < lane
    pos = jnp.where(need, mm(ind(need), ind(before)), -1.0)

    zed = lax.broadcasted_iota(jnp.int32, (8, 1), 0)
    zneed = (mm(ind((dev_r // plane) == zed), ind(need)) > 0) & ((lane // in_plane) != zed)
    same_plane = (sub // in_plane) == (lane // in_plane)
    zpos = jnp.where(zneed, mm(ind(zneed), ind(before & same_plane)), -1.0)

    over = jnp.maximum(jnp.max(pos) - (CAP - 1), jnp.max(zpos) - (ZCAP - 1))
    most_ref[0, 0] = over.astype(jnp.int32)

    lanes = lax.broadcasted_iota(jnp.int32, (1, BS), 1)
    mine_z = (lane // in_plane) == my_plane
    local = (lane % in_plane).astype(jnp.float32)
    cross = jnp.zeros(cross_ref.shape, jnp.float32)
    for m in range(ZCAP):
        one = jnp.sum(jnp.where(mine_z & (zpos == m), local, 0.0), axis=1, keepdims=True)
        cross = jnp.where(lanes == m, one, cross)
    cross_ref[...] = cross.astype(jnp.int32)

    from_z = jnp.sum(jnp.where(zed == my_plane, zpos, 0.0), axis=0, keepdims=True)
    source = jnp.where(mine_z, local, in_plane + ZCAP * (lane // in_plane).astype(jnp.float32) + from_z)
    pick = lax.broadcasted_iota(jnp.int32, (plane, 1), 0) + plane * my_plane
    pos_p = mm(ind(pick == dev_r), bf(pos))
    give = jnp.zeros(give_ref.shape, jnp.float32)
    for m in range(CAP):
        one = jnp.sum(jnp.where(pos_p == m, source, 0.0), axis=1, keepdims=True)
        give = jnp.where(lanes == m, one, give)
    give_ref[...] = give.astype(jnp.int32)

    my_pos = jnp.sum(jnp.where(dev == me, pos, 0.0), axis=0, keepdims=True)
    held_r = jnp.where((lane // SLOTS) == me, slot_r, SLOTS + my_pos)
    held_c = as_column(held_r)
    mine = product & (((sub // SLOTS) % cols) == my_col) & ((lane // per_row) == my_row)
    rank = mm(ind(lane < sub), ind(mine))
    code = (hit - 1.0) * 16.0 + held_r * 16.0 + held_c + 1.0
    out_sub = lax.broadcasted_iota(jnp.int32, (list_ref.shape[0], 1), 0)
    listed = jnp.zeros(list_ref.shape, jnp.float32)
    for k in range(2 * ACT):
        one = jnp.sum(jnp.where(mine & (rank == k), code, 0.0), axis=0, keepdims=True)
        listed = jnp.where(out_sub == k, one, listed)
    list_ref[...] = listed.astype(jnp.int32) - 1


def cross_kernel(planes, piece, cross_ref, held_ref, out_ref):
    for z in range(planes):
        for m in range(ZCAP):
            at = pl.ds(pl.multiple_of(cross_ref[z, m] * piece, piece), piece)
            out_ref[pl.ds((z * ZCAP + m) * piece, piece), :] = held_ref[at, :]


def give_kernel(plane, piece, give_ref, held_ref, crossed_ref, out_ref):
    count = held_ref.shape[0] // piece
    for p in range(plane):
        for m in range(CAP):
            at = give_ref[p, m]
            here = pl.ds(pl.multiple_of(jnp.minimum(at, count - 1) * piece, piece), piece)
            there = pl.ds(pl.multiple_of(jnp.maximum(at - count, 0) * piece, piece), piece)
            out_ref[pl.ds((p * CAP + m) * piece, piece), :] = jnp.where(
                at < count, held_ref[here, :], crossed_ref[there, :]
            )


def product_kernel(cols, plane, piece, list_ref, blocks_ref, got_ref, out_ref, held_ref):
    per_row = cols * SLOTS
    first = (2 * lax.axis_index("z") + lax.axis_index("y")) * per_row
    held_ref[: SLOTS * BS, :] = blocks_ref[...]
    for p in range(plane):
        for m in range(CAP):
            held_ref[pl.ds((SLOTS + m) * BS + p * piece, piece), :] = got_ref[pl.ds((p * CAP + m) * piece, piece), :]
    out_ref[...] = jnp.zeros_like(out_ref)

    def block(at):
        x = held_ref[pl.ds(pl.multiple_of(at * BS, BS), BS), :]
        high = bf(x)
        return high, bf(x - high.astype(jnp.float32))

    def entry(i, carry):
        for k in range(2 * ACT):
            code = list_ref[k, first + i]

            @pl.when(code >= 0)
            def _():
                a_high, a_low = block((code // 16) % 16)
                b_high, b_low = block(code % 16)
                at = pl.ds(pl.multiple_of((code // 256) * BS, BS), BS)
                out_ref[at, :] += mm(a_high, b_high) + (mm(a_high, b_low) + mm(a_low, b_high))

        return carry

    lax.fori_loop(0, per_row, entry, 0)


def packed_body(blocks, block_rows, block_cols):
    planes, cols = lax.axis_size("z"), lax.axis_size("col")
    rows = 2 * planes
    plane = 2 * cols
    devices = rows * cols
    n = devices * SLOTS
    piece = BS // plane
    flat = blocks.reshape(SLOTS * BS, BS)
    params = pltpu.CompilerParams(vmem_limit_bytes=VMEM_LIMIT)
    vmem = pl.BlockSpec(memory_space=pltpu.VMEM)
    smem = pl.BlockSpec(memory_space=pltpu.SMEM)

    idx = jnp.concatenate([block_rows[0], block_cols[0]])
    idx = lax.all_to_all(jnp.broadcast_to(idx[None], (devices, 2, SLOTS)), ("z", "y", "col"), 0, 0)
    spread = blocks.reshape(SLOTS, plane, piece, BS).transpose(1, 0, 2, 3)
    held = lax.all_to_all(spread, ("y", "col"), 0, 0).reshape(plane * SLOTS * piece, BS)
    cross, give, listed, most = pl.pallas_call(
        lambda *refs: plan_kernel(rows, cols, *refs),
        out_shape=(
            jax.ShapeDtypeStruct((8, BS), jnp.int32),
            jax.ShapeDtypeStruct((plane, BS), jnp.int32),
            jax.ShapeDtypeStruct((8, n), jnp.int32),
            jax.ShapeDtypeStruct((1, 1), jnp.int32),
        ),
        in_specs=[vmem],
        out_specs=(vmem, vmem, vmem, smem),
        compiler_params=params,
        name="plan",
    )(idx)

    def packed():
        out = pl.pallas_call(
            lambda *refs: cross_kernel(planes, piece, *refs),
            out_shape=jax.ShapeDtypeStruct((planes * ZCAP * piece, BS), jnp.float32),
            in_specs=[smem, vmem],
            out_specs=vmem,
            compiler_params=params,
            name="cross",
        )(cross, held)
        crossed = lax.all_to_all(out.reshape(planes, ZCAP, piece, BS), "z", 0, 0)
        out = pl.pallas_call(
            lambda *refs: give_kernel(plane, piece, *refs),
            out_shape=jax.ShapeDtypeStruct((plane * CAP * piece, BS), jnp.float32),
            in_specs=[smem, vmem, vmem],
            out_specs=vmem,
            compiler_params=params,
            name="give",
        )(give, held, crossed.reshape(planes * ZCAP * piece, BS))
        got = lax.all_to_all(out.reshape(plane, CAP, piece, BS), ("y", "col"), 0, 0)
        out = pl.pallas_call(
            lambda *refs: product_kernel(cols, plane, piece, *refs),
            out_shape=jax.ShapeDtypeStruct((SLOTS * BS, BS), jnp.float32),
            in_specs=[smem, vmem, vmem],
            out_specs=vmem,
            scratch_shapes=[pltpu.VMEM(((SLOTS + CAP) * BS, BS), jnp.float32)],
            compiler_params=params,
            name="products",
        )(listed, flat, got.reshape(plane * CAP * piece, BS))
        return out.reshape(blocks.shape)

    return lax.cond(most[0, 0] <= 0, packed, lambda: whole_tiles(blocks, block_rows, block_cols))


def solution(mesh):
    rows, cols = mesh.devices.shape
    if cols == SECTIONS and rows == 2 * SECTIONS:
        body, row = packed_body, ("z", "y")
        mesh = jax.sharding.Mesh(mesh.devices.reshape(rows // 2, 2, cols), ("z", "y", "col"))
    else:
        body, row = general_body, "row"
    return jax.shard_map(
        body,
        mesh=mesh,
        in_specs=(P(row, "col", None, None, None), P(row, "col", None), P(row, "col", None)),
        out_specs=P(row, "col", None, None, None),
        check_vma=False,
    )
```

```python
import jax
import jax.numpy as jnp
from jax import lax
from jax.experimental import pallas as pl
from jax.experimental.pallas import tpu as pltpu
from jax.sharding import PartitionSpec as P

NBLK = 512
ACT = 2
SECTIONS = 4
BS = 128
SLOTS = 8
CAP = 8
ZCAP = 8
VMEM_LIMIT = 32 * 1024 * 1024


def from_root(x, axis, root):
    mine = lax.axis_index(axis) == root
    return lax.psum(jnp.where(mine, x, jnp.zeros_like(x)), axis)


def from_partner(x, axis, bit):
    return lax.ppermute(x, axis, [(i, i ^ 1 << bit) for i in range(lax.axis_size(axis))])


def shifted(value, axis, steps):
    count = lax.axis_size(axis)
    pairs = [(source, (source + steps) % count) for source in range(count)]
    return lax.ppermute(value, axis, pairs)


def section_product(panel, pair, out_rows, out_cols, depth):
    panel_vals, panel_rows, panel_cols = panel
    pair_vals, pair_inner, pair_cols = pair
    panel_iota = jnp.arange(panel_rows.shape[0], dtype=jnp.int32)
    pair_iota = jnp.arange(pair_inner.shape[0], dtype=jnp.int32)
    depth_iota = jnp.arange(depth, dtype=jnp.int32)
    panel_live = panel_rows >= 0
    earlier = (
        (panel_rows[None, :] == panel_rows[:, None])
        & panel_live[None, :]
        & (panel_iota[None, :] < panel_iota[:, None])
    )
    within = jnp.sum(earlier.astype(jnp.int32), axis=1)
    picked = (panel_rows[None, None, :] == out_rows[:, None, None]) & (
        within[None, None, :] == depth_iota[None, :, None]
    )
    picked = picked & panel_live[None, None, :] & (out_rows >= 0)[:, None, None]
    picked_int = picked.astype(jnp.int32)
    panel_slot = jnp.sum(picked_int * panel_iota[None, None, :], axis=2)
    found = jnp.sum(picked_int, axis=2) > 0
    inner = jnp.sum(picked_int * panel_cols[None, None, :], axis=2)
    matched = (pair_inner[None, None, :] == inner[:, :, None]) & (
        pair_cols[None, None, :] == out_cols[:, None, None]
    )
    matched = matched & (pair_inner >= 0)[None, None, :] & found[:, :, None]
    matched_int = matched.astype(jnp.int32)
    pair_slot = jnp.sum(matched_int * pair_iota[None, None, :], axis=2)
    weight = (jnp.sum(matched_int, axis=2) > 0).astype(jnp.float32)
    left = panel_vals[panel_slot] * weight[:, :, None, None]
    right = pair_vals[pair_slot]
    return jnp.einsum(
        "tqij,tqjk->tik",
        left,
        right,
        precision=lax.Precision.HIGHEST,
        preferred_element_type=jnp.float32,
    )


def make_pair(first, second, row_span):
    inner = jnp.concatenate([first[1], jnp.where(second[1] >= 0, second[1] + row_span, -1)])
    return (jnp.concatenate([first[0], second[0]]), inner, jnp.concatenate([first[2], second[2]]))


def order_pair(mine, other, is_even, row_span):
    first = tuple((jnp.where(is_even, one, two) for one, two in zip(mine, other)))
    second = tuple((jnp.where(is_even, two, one) for one, two in zip(mine, other)))
    return make_pair(first, second, row_span)


def fetch_panel(tile, row_index, col_count, section):
    root = (row_index // 2 + section) % col_count
    return tuple(from_root(one, "col", root) for one in tile)


def general_body(blocks, block_rows, block_cols):
    tile = (blocks[0, 0], block_rows[0, 0], block_cols[0, 0])
    row_count = lax.axis_size("row")
    col_count = lax.axis_size("col")
    row_span = NBLK // row_count
    row_index = lax.axis_index("row")
    is_even = row_index % 2 == 0
    depth = 2 * ACT
    total = jnp.zeros(blocks.shape[2:], jnp.float32)
    partner = from_partner((tile[0], tile[1], tile[2]), "row", 0)
    current = order_pair(tile, partner, is_even, row_span)
    for section in range(SECTIONS):
        panel = fetch_panel(tile, row_index, col_count, section)
        if section > 0:
            current = shifted((current[0], current[1], current[2]), "row", -2)
        total = total + section_product(panel, current, tile[1], tile[2], depth)
    return total[None, None]


def everything(x, axis):
    return lax.all_to_all(jnp.broadcast_to(x[None], (lax.axis_size(axis),) + x.shape), axis, 0, 0)


def whole_tiles(blocks, block_rows, block_cols):
    tile = (blocks[0, 0], block_rows[0, 0], block_cols[0, 0])
    row_span = NBLK // lax.axis_size(("z", "y"))
    col_count = lax.axis_size("col")
    row_index = lax.axis_index(("z", "y"))
    panels = tuple(everything(one, "col") for one in tile)
    column = tuple(everything(one, ("z", "y")) for one in tile)

    def section(step, total):
        root = (row_index // 2 + step) % col_count
        take = lambda arrays, at: tuple(lax.dynamic_index_in_dim(a, at, 0, False) for a in arrays)
        pair = make_pair(take(column, 2 * root), take(column, 2 * root + 1), row_span)
        return total + section_product(take(panels, root), pair, tile[1], tile[2], 2 * ACT)

    total = lax.fori_loop(0, SECTIONS, section, jnp.zeros(blocks.shape[2:], jnp.float32))
    return total[None, None]


def bf(x):
    return x.astype(jnp.bfloat16)


def ind(x):
    return bf(jnp.where(x, 1.0, 0.0))


def mm(a, b, transposed=False):
    dims = (((1,), (1 if transposed else 0,)), ((), ()))
    return lax.dot_general(a, b, dims, preferred_element_type=jnp.float32)


def plan_kernel(rows, cols, *refs):
    planes = rows // 2
    idx_refs = refs[: 2 * cols]
    cross_ref, give_ref, list_ref, most_ref = refs[2 * cols :]
    devices = rows * cols
    plane = 2 * cols
    n = devices * SLOTS
    in_plane = plane * SLOTS
    rb = NBLK // rows
    cb = NBLK // cols
    per_row = cols * SLOTS
    my_plane, my_p = lax.axis_index("z"), lax.axis_index(("y", "col"))
    my_row = 2 * my_plane + lax.axis_index("y")
    my_col = lax.axis_index("col")
    me = my_row * cols + my_col

    sub = lax.broadcasted_iota(jnp.int32, (n, 1), 0)
    lane = lax.broadcasted_iota(jnp.int32, (1, n), 1)
    dev = lax.broadcasted_iota(jnp.int32, (devices, 1), 0)
    dev_r = lax.broadcasted_iota(jnp.int32, (1, devices), 1)
    slot = lax.broadcasted_iota(jnp.int32, (1, BS), 1)
    diagonal = sub == lane

    def as_row(column):
        return jnp.sum(jnp.where(diagonal, column, 0.0), axis=0, keepdims=True)

    def as_column(row):
        return jnp.sum(jnp.where(diagonal, row, 0.0), axis=1, keepdims=True)

    told = jnp.concatenate([ref[ref.shape[0] - 8 :, :] for ref in idx_refs])
    at = lax.broadcasted_iota(jnp.int32, (1, 8 * plane), 1)
    from_p = (at // 8) ^ my_p
    from_plane = (at % 8) ^ my_plane
    repeat = ind(((sub // SLOTS) == from_plane * plane + from_p) & (at % 8 < planes))
    values = mm(repeat, bf(told))

    def column(k):
        return jnp.sum(jnp.where((sub % SLOTS) == slot - k * SLOTS, values, 0.0), axis=1, keepdims=True)

    up = ((sub // per_row) * rb).astype(jnp.float32)
    along = (((sub // SLOTS) % cols) * cb).astype(jnp.float32)
    row_c, col_c = column(0), column(1)
    row_c = jnp.where(row_c >= 0, row_c + up, -1.0)
    col_c = jnp.where(col_c >= 0, col_c + along, -2.0)
    row_r, col_r = as_row(row_c), as_row(col_c)

    slot_r = (lane % SLOTS).astype(jnp.float32)
    hit = mm(bf(jnp.where(col_c == col_r, 1.0 + 16.0 * slot_r, 0.0)), ind(row_c == row_r))
    product = (row_c == col_r) & (hit > 0)
    product_b = ind(product)

    in_row = (lane // per_row) == (dev // cols)
    in_col = ((lane // SLOTS) % cols) == (dev % cols)
    as_left = mm(ind(in_col), product_b)
    as_right = mm(ind(in_row), product_b, transposed=True)
    need = (in_row & (as_left > 0)) | (in_col & (as_right > 0))
    need = need & ((lane // SLOTS) != dev)
    before = sub < lane
    pos = jnp.where(need, mm(ind(need), ind(before)), -1.0)

    zed = lax.broadcasted_iota(jnp.int32, (8, 1), 0)
    zneed = (mm(ind((dev_r // plane) == zed), ind(need)) > 0) & ((lane // in_plane) != zed)
    same_plane = (sub // in_plane) == (lane // in_plane)
    zpos = jnp.where(zneed, mm(ind(zneed), ind(before & same_plane)), -1.0)

    over = jnp.maximum(jnp.max(pos) - (CAP - 1), jnp.max(zpos) - (ZCAP - 1))
    most_ref[0, 0] = over.astype(jnp.int32)

    lanes = lax.broadcasted_iota(jnp.int32, (1, BS), 1)
    mine_z = (lane // in_plane) == my_plane
    local = ((((lane // SLOTS) % plane) ^ my_p) * SLOTS + lane % SLOTS).astype(jnp.float32)
    away = in_plane + ZCAP * (((lane // in_plane) ^ my_plane) - 1)
    cross = jnp.zeros(cross_ref.shape, jnp.float32)
    for m in range(ZCAP):
        one = jnp.sum(jnp.where(mine_z & (zpos == m), local, 0.0), axis=1, keepdims=True)
        cross = jnp.where(lanes == m, one, cross)
    cross_ref[...] = cross.astype(jnp.int32)

    from_z = jnp.sum(jnp.where(zed == my_plane, zpos, 0.0), axis=0, keepdims=True)
    source = jnp.where(mine_z, local, away.astype(jnp.float32) + from_z)
    pick = lax.broadcasted_iota(jnp.int32, (plane, 1), 0) + plane * my_plane
    pos_p = mm(ind(pick == dev_r), bf(pos))
    give = jnp.zeros(give_ref.shape, jnp.float32)
    for m in range(CAP):
        one = jnp.sum(jnp.where(pos_p == m, source, 0.0), axis=1, keepdims=True)
        give = jnp.where(lanes == m, one, give)
    give_ref[...] = give.astype(jnp.int32)

    my_pos = jnp.sum(jnp.where(dev == me, pos, 0.0), axis=0, keepdims=True)
    held_r = jnp.where((lane // SLOTS) == me, slot_r, SLOTS + my_pos)
    held_c = as_column(held_r)
    mine = product & (((sub // SLOTS) % cols) == my_col) & ((lane // per_row) == my_row)
    rank = mm(ind(lane < sub), ind(mine))
    code = (hit - 1.0) * 16.0 + held_r * 16.0 + held_c + 1.0
    out_sub = lax.broadcasted_iota(jnp.int32, (list_ref.shape[0], 1), 0)
    listed = jnp.zeros(list_ref.shape, jnp.float32)
    for k in range(2 * ACT):
        one = jnp.sum(jnp.where(mine & (rank == k), code, 0.0), axis=0, keepdims=True)
        listed = jnp.where(out_sub == k, one, listed)
    list_ref[...] = listed.astype(jnp.int32) - 1


def spread_kernel(plane, piece, blocks_ref, *refs):
    idx_refs, outs = refs[:-plane], refs[-plane:]
    my_p = lax.axis_index(("y", "col"))
    sub = lax.broadcasted_iota(jnp.int32, (8, BS), 0)
    lane = lax.broadcasted_iota(jnp.int32, (8, BS), 1)
    wide = lax.broadcasted_iota(jnp.int32, (SLOTS, BS), 1)
    shift = lax.broadcasted_iota(jnp.int32, (SLOTS, BS), 0)
    told = jnp.zeros((8, BS), jnp.float32)
    for k, ref in enumerate(idx_refs):
        for half in range(2):
            place = ind(wide == shift + half * SLOTS)
            row = jnp.broadcast_to(ref[half : half + 1, :].astype(jnp.float32), (8, SLOTS))
            told = jnp.where(
                (sub == k) & (lane // SLOTS == half), mm(bf(row), place), told
            )
    for m, out_ref in enumerate(outs):
        p = my_p ^ m
        for t in range(SLOTS):
            at = pl.ds(pl.multiple_of(t * BS + p * piece, piece), piece)
            out_ref[t * piece : (t + 1) * piece, :] = blocks_ref[at, :]
        out_ref[SLOTS * piece :, :] = told


def cross_kernel(planes, plane, piece, cross_ref, *refs):
    piece_refs, outs, held_ref = refs[:plane], refs[plane:-1], refs[-1]
    size = SLOTS * piece
    for m, ref in enumerate(piece_refs):
        held_ref[m * size : (m + 1) * size, :] = ref[:size, :]
    my_plane = lax.axis_index("z")
    for m, out_ref in enumerate(outs):
        z = my_plane ^ (m + 1)
        for k in range(ZCAP):
            at = pl.ds(pl.multiple_of(cross_ref[z, k] * piece, piece), piece)
            out_ref[k * piece : (k + 1) * piece, :] = held_ref[at, :]


def give_kernel(planes, plane, piece, give_ref, held_ref, *refs):
    crossed_refs, outs, all_ref = refs[: planes - 1], refs[planes - 1 : -1], refs[-1]
    here = held_ref.shape[0]
    size = ZCAP * piece
    all_ref[:here, :] = held_ref[...]
    for m, ref in enumerate(crossed_refs):
        all_ref[here + m * size : here + (m + 1) * size, :] = ref[...]
    my_p = lax.axis_index(("y", "col"))
    for m, out_ref in enumerate(outs):
        p = my_p ^ m
        for k in range(CAP):
            at = pl.ds(pl.multiple_of(give_ref[p, k] * piece, piece), piece)
            out_ref[k * piece : (k + 1) * piece, :] = all_ref[at, :]


def product_kernel(cols, plane, piece, list_ref, blocks_ref, *refs):
    got_refs, out_ref, held_ref = refs[:plane], refs[plane], refs[plane + 1]
    per_row = cols * SLOTS
    first = (2 * lax.axis_index("z") + lax.axis_index("y")) * per_row
    my_p = lax.axis_index(("y", "col"))
    held_ref[: SLOTS * BS, :] = blocks_ref[...]
    for m, ref in enumerate(got_refs):
        p = my_p ^ m
        for k in range(CAP):
            at = pl.ds(pl.multiple_of((SLOTS + k) * BS + p * piece, piece), piece)
            held_ref[at, :] = ref[k * piece : (k + 1) * piece, :]
    out_ref[...] = jnp.zeros_like(out_ref)

    def block(at):
        x = held_ref[pl.ds(pl.multiple_of(at * BS, BS), BS), :]
        high = bf(x)
        return high, bf(x - high.astype(jnp.float32))

    def entry(i, carry):
        for k in range(2 * ACT):
            code = list_ref[k, first + i]

            @pl.when(code >= 0)
            def _():
                a_high, a_low = block((code // 16) % 16)
                b_high, b_low = block(code % 16)
                at = pl.ds(pl.multiple_of((code // 256) * BS, BS), BS)
                out_ref[at, :] += mm(a_high, b_high) + (mm(a_high, b_low) + mm(a_low, b_high))

        return carry

    lax.fori_loop(0, per_row, entry, 0)


def swapped(arrays, axis):
    count = lax.axis_size(axis)
    swap = lambda x, m: lax.ppermute(x, axis, [(i, i ^ m) for i in range(count)])
    return arrays[:1] + [swap(x, m) for m, x in enumerate(arrays) if m]


def packed_body(blocks, block_rows, block_cols):
    planes, cols = lax.axis_size("z"), lax.axis_size("col")
    rows = 2 * planes
    plane = 2 * cols
    n = rows * cols * SLOTS
    piece = BS // plane
    in_plane = ("y", "col")
    flat = blocks.reshape(SLOTS * BS, BS)
    params = pltpu.CompilerParams(vmem_limit_bytes=VMEM_LIMIT)
    vmem = pl.BlockSpec(memory_space=pltpu.VMEM)
    smem = pl.BlockSpec(memory_space=pltpu.SMEM)

    def floats(height):
        return jax.ShapeDtypeStruct((height, BS), jnp.float32)

    def call(kernel, name, ins, outs, scratch=(), specs=None):
        return pl.pallas_call(
            kernel,
            out_shape=outs,
            in_specs=ins,
            out_specs=[vmem] * len(outs) if specs is None else specs,
            scratch_shapes=scratch,
            compiler_params=params,
            name=name,
        )

    idx = jnp.concatenate([block_rows[0], block_cols[0]])
    line = swapped([idx] * planes, "z")
    spread = call(
        lambda *refs: spread_kernel(plane, piece, *refs),
        "spread",
        [vmem] * (1 + planes),
        [floats(SLOTS * piece + 8)] * plane,
    )(flat, *line)
    pieces = swapped(list(spread), in_plane)
    cross, give, listed, most = call(
        lambda *refs: plan_kernel(rows, cols, *refs),
        "plan",
        [vmem] * plane,
        (
            jax.ShapeDtypeStruct((8, BS), jnp.int32),
            jax.ShapeDtypeStruct((plane, BS), jnp.int32),
            jax.ShapeDtypeStruct((8, n), jnp.int32),
            jax.ShapeDtypeStruct((1, 1), jnp.int32),
        ),
        specs=(vmem, vmem, vmem, smem),
    )(*pieces)

    def packed():
        *crossing, held = call(
            lambda *refs: cross_kernel(planes, plane, piece, *refs),
            "cross",
            [smem] + [vmem] * plane,
            [floats(ZCAP * piece)] * (planes - 1) + [floats(plane * SLOTS * piece)],
        )(cross, *pieces)
        crossed = swapped([held] + crossing, "z")[1:]
        giving = call(
            lambda *refs: give_kernel(planes, plane, piece, *refs),
            "give",
            [smem] + [vmem] * planes,
            [floats(CAP * piece)] * plane,
            [pltpu.VMEM(((plane * SLOTS + (planes - 1) * ZCAP) * piece, BS), jnp.float32)],
        )(give, held, *crossed)
        got = swapped(list(giving), in_plane)
        out = call(
            lambda *refs: product_kernel(cols, plane, piece, *refs),
            "products",
            [smem] + [vmem] * (1 + plane),
            [floats(SLOTS * BS)],
            [pltpu.VMEM(((SLOTS + CAP) * BS, BS), jnp.float32)],
        )(listed, flat, *got)
        return out[0].reshape(blocks.shape)

    return lax.cond(most[0, 0] <= 0, packed, lambda: whole_tiles(blocks, block_rows, block_cols))


def solution(mesh):
    rows, cols = mesh.devices.shape
    if cols == SECTIONS and rows == 2 * SECTIONS:
        body, row = packed_body, ("z", "y")
        mesh = jax.sharding.Mesh(mesh.devices.reshape(rows // 2, 2, cols), ("z", "y", "col"))
    else:
        body, row = general_body, "row"
    return jax.shard_map(
        body,
        mesh=mesh,
        in_specs=(P(row, "col", None, None, None), P(row, "col", None), P(row, "col", None)),
        out_specs=P(row, "col", None, None, None),
        check_vma=False,
    )
```

```python
import jax
import jax.numpy as jnp
from jax import lax
from jax.experimental import pallas as pl
from jax.experimental.pallas import tpu as pltpu
from jax.sharding import PartitionSpec as P

NBLK = 512
ACT = 2
SECTIONS = 4
BS = 128
SLOTS = 8
LCAP = 5
RCAP = 5
ZCAP = 6
VMEM_LIMIT = 32 * 1024 * 1024


def from_root(x, axis, root):
    mine = lax.axis_index(axis) == root
    return lax.psum(jnp.where(mine, x, jnp.zeros_like(x)), axis)


def from_partner(x, axis, bit):
    return lax.ppermute(x, axis, [(i, i ^ 1 << bit) for i in range(lax.axis_size(axis))])


def shifted(value, axis, steps):
    count = lax.axis_size(axis)
    pairs = [(source, (source + steps) % count) for source in range(count)]
    return lax.ppermute(value, axis, pairs)


def section_product(panel, pair, out_rows, out_cols, depth):
    panel_vals, panel_rows, panel_cols = panel
    pair_vals, pair_inner, pair_cols = pair
    panel_iota = jnp.arange(panel_rows.shape[0], dtype=jnp.int32)
    pair_iota = jnp.arange(pair_inner.shape[0], dtype=jnp.int32)
    depth_iota = jnp.arange(depth, dtype=jnp.int32)
    panel_live = panel_rows >= 0
    earlier = (
        (panel_rows[None, :] == panel_rows[:, None])
        & panel_live[None, :]
        & (panel_iota[None, :] < panel_iota[:, None])
    )
    within = jnp.sum(earlier.astype(jnp.int32), axis=1)
    picked = (panel_rows[None, None, :] == out_rows[:, None, None]) & (
        within[None, None, :] == depth_iota[None, :, None]
    )
    picked = picked & panel_live[None, None, :] & (out_rows >= 0)[:, None, None]
    picked_int = picked.astype(jnp.int32)
    panel_slot = jnp.sum(picked_int * panel_iota[None, None, :], axis=2)
    found = jnp.sum(picked_int, axis=2) > 0
    inner = jnp.sum(picked_int * panel_cols[None, None, :], axis=2)
    matched = (pair_inner[None, None, :] == inner[:, :, None]) & (
        pair_cols[None, None, :] == out_cols[:, None, None]
    )
    matched = matched & (pair_inner >= 0)[None, None, :] & found[:, :, None]
    matched_int = matched.astype(jnp.int32)
    pair_slot = jnp.sum(matched_int * pair_iota[None, None, :], axis=2)
    weight = (jnp.sum(matched_int, axis=2) > 0).astype(jnp.float32)
    left = panel_vals[panel_slot] * weight[:, :, None, None]
    right = pair_vals[pair_slot]
    return jnp.einsum(
        "tqij,tqjk->tik",
        left,
        right,
        precision=lax.Precision.HIGHEST,
        preferred_element_type=jnp.float32,
    )


def make_pair(first, second, row_span):
    inner = jnp.concatenate([first[1], jnp.where(second[1] >= 0, second[1] + row_span, -1)])
    return (jnp.concatenate([first[0], second[0]]), inner, jnp.concatenate([first[2], second[2]]))


def order_pair(mine, other, is_even, row_span):
    first = tuple((jnp.where(is_even, one, two) for one, two in zip(mine, other)))
    second = tuple((jnp.where(is_even, two, one) for one, two in zip(mine, other)))
    return make_pair(first, second, row_span)


def fetch_panel(tile, row_index, col_count, section):
    root = (row_index // 2 + section) % col_count
    return tuple(from_root(one, "col", root) for one in tile)


def general_body(blocks, block_rows, block_cols):
    tile = (blocks[0, 0], block_rows[0, 0], block_cols[0, 0])
    row_count = lax.axis_size("row")
    col_count = lax.axis_size("col")
    row_span = NBLK // row_count
    row_index = lax.axis_index("row")
    is_even = row_index % 2 == 0
    depth = 2 * ACT
    total = jnp.zeros(blocks.shape[2:], jnp.float32)
    partner = from_partner((tile[0], tile[1], tile[2]), "row", 0)
    current = order_pair(tile, partner, is_even, row_span)
    for section in range(SECTIONS):
        panel = fetch_panel(tile, row_index, col_count, section)
        if section > 0:
            current = shifted((current[0], current[1], current[2]), "row", -2)
        total = total + section_product(panel, current, tile[1], tile[2], depth)
    return total[None, None]


def everything(x, axis):
    return lax.all_to_all(jnp.broadcast_to(x[None], (lax.axis_size(axis),) + x.shape), axis, 0, 0)


def whole_tiles(blocks, block_rows, block_cols):
    tile = (blocks[0, 0], block_rows[0, 0], block_cols[0, 0])
    row_span = NBLK // lax.axis_size(("z", "y"))
    col_count = lax.axis_size("col")
    row_index = lax.axis_index(("z", "y"))
    panels = tuple(everything(one, "col") for one in tile)
    column = tuple(everything(one, ("z", "y")) for one in tile)

    def section(step, total):
        root = (row_index // 2 + step) % col_count
        take = lambda arrays, at: tuple(lax.dynamic_index_in_dim(a, at, 0, False) for a in arrays)
        pair = make_pair(take(column, 2 * root), take(column, 2 * root + 1), row_span)
        return total + section_product(take(panels, root), pair, tile[1], tile[2], 2 * ACT)

    total = lax.fori_loop(0, SECTIONS, section, jnp.zeros(blocks.shape[2:], jnp.float32))
    return total[None, None]


GROUP = (0, 4)


def piece_of(p):
    return p // 4


def group_of(p):
    return p % 4


def bf(x):
    return x.astype(jnp.bfloat16)


def ind(x):
    return bf(jnp.where(x, 1.0, 0.0))


def mm(a, b, transposed=False):
    dims = (((1,), (1 if transposed else 0,)), ((), ()))
    return lax.dot_general(a, b, dims, preferred_element_type=jnp.float32)


def plan_kernel(rows, cols, idx_ref, table_ref, list_ref, over_ref):
    devices = rows * cols
    plane = 2 * cols
    n = devices * SLOTS
    in_plane = plane * SLOTS
    rb = NBLK // rows
    cb = NBLK // cols
    per_row = cols * SLOTS
    lefts = (cols - 1) * LCAP
    my_plane, my_p = lax.axis_index("z"), lax.axis_index(("y", "col"))
    my_row = 2 * my_plane + lax.axis_index("y")
    my_col = lax.axis_index("col")
    me = my_row * cols + my_col

    sub = lax.broadcasted_iota(jnp.int32, (n, 1), 0)
    lane = lax.broadcasted_iota(jnp.int32, (1, n), 1)
    dev = lax.broadcasted_iota(jnp.int32, (devices, 1), 0)
    dev_r = lax.broadcasted_iota(jnp.int32, (1, devices), 1)
    slot = lax.broadcasted_iota(jnp.int32, (1, 2 * SLOTS), 1)
    diagonal = sub == lane

    def as_row(column):
        return jnp.sum(jnp.where(diagonal, column, 0.0), axis=0, keepdims=True)

    def as_column(row):
        return jnp.sum(jnp.where(diagonal, row, 0.0), axis=1, keepdims=True)

    values = mm(ind((sub // SLOTS) == dev_r), bf(idx_ref[...].astype(jnp.float32)))

    def column(k):
        return jnp.sum(jnp.where((sub % SLOTS) == slot - k * SLOTS, values, 0.0), axis=1, keepdims=True)

    up = ((sub // per_row) * rb).astype(jnp.float32)
    along = (((sub // SLOTS) % cols) * cb).astype(jnp.float32)
    row_c, col_c = column(0), column(1)
    row_c = jnp.where(row_c >= 0, row_c + up, -1.0)
    col_c = jnp.where(col_c >= 0, col_c + along, -2.0)
    row_r, col_r = as_row(row_c), as_row(col_c)

    slot_r = (lane % SLOTS).astype(jnp.float32)
    hit = mm(bf(jnp.where(col_c == col_r, 1.0 + 16.0 * slot_r, 0.0)), ind(row_c == row_r))
    product = (row_c == col_r) & (hit > 0)
    product_b = ind(product)

    in_row = (lane // per_row) == (dev // cols)
    in_col = ((lane // SLOTS) % cols) == (dev % cols)
    other = (lane // SLOTS) != dev
    left = in_row & other & (mm(ind(in_col), product_b) > 0)
    right = in_col & other & (mm(ind(in_row), product_b, transposed=True) > 0)
    before = sub < lane
    same_device = (sub // SLOTS) == (lane // SLOTS)
    left_at = jnp.where(left, mm(ind(left), ind(before & same_device)), -1.0)
    right_at = jnp.where(right, mm(ind(right), ind(before)), -1.0)

    zed = lax.broadcasted_iota(jnp.int32, (8, 1), 0)
    cross = (mm(ind((dev_r // plane) == zed), ind(right)) > 0) & ((lane // in_plane) != zed)
    together = ((sub // in_plane) == (lane // in_plane)) & (
        group_of((sub // SLOTS) % plane) == group_of((lane // SLOTS) % plane)
    )
    cross_at = jnp.where(cross, mm(ind(cross), ind(before & together)), -1.0)

    over = jnp.maximum(jnp.max(left_at) - (LCAP - 1), jnp.max(right_at) - (RCAP - 1))
    over_ref[0, 0] = jnp.maximum(over, jnp.max(cross_at) - (ZCAP - 1)).astype(jnp.int32)

    lanes = lax.broadcasted_iota(jnp.int32, (1, BS), 1)

    def table(first, at, value, most):
        out = jnp.zeros((8, BS), jnp.float32)
        for k in range(most):
            one = jnp.sum(jnp.where(at == k, value, 0.0), axis=1, keepdims=True)
            out = jnp.where(lanes == k, one, out)
        table_ref[first : first + 8, :] = out.astype(jnp.int32)

    mine = (lane // SLOTS) == me
    to_col = mm(ind(my_row * cols + zed % cols == dev_r), bf(left_at))
    table(0, jnp.where(mine, to_col, -1.0), slot_r, LCAP)
    here = ((lane // in_plane) == my_plane) & (group_of((lane // SLOTS) % plane) == group_of(my_p))
    partner = piece_of((lane // SLOTS) % plane) ^ piece_of(my_p)
    local = (partner * SLOTS + lane % SLOTS).astype(jnp.float32)
    table(8, jnp.where(here, cross_at, -1.0), local, ZCAP)
    came = jnp.sum(jnp.where(zed == my_plane, cross_at, 0.0), axis=0, keepdims=True)
    away = len(GROUP) * SLOTS + ZCAP * (((lane // in_plane) ^ my_plane) - 1)
    source = jnp.where((lane // in_plane) == my_plane, local, away.astype(jnp.float32) + came)
    partners = jnp.zeros((8, devices), jnp.bool_)
    for g, mask in enumerate(GROUP):
        partners = partners | ((zed == g) & (dev_r == my_plane * plane + (my_p ^ mask)))
    table(16, mm(ind(partners), bf(right_at)), source, RCAP)

    left_me = jnp.sum(jnp.where(dev == me, left_at, 0.0), axis=0, keepdims=True)
    right_me = jnp.sum(jnp.where(dev == me, right_at, 0.0), axis=0, keepdims=True)
    from_col = ((lane // SLOTS) % cols) ^ my_col
    held_a = jnp.where(mine, slot_r, (SLOTS + LCAP * (from_col - 1)).astype(jnp.float32) + left_me)
    held_b = as_column(jnp.where(mine, slot_r, SLOTS + lefts + right_me))
    my_product = product & (((sub // SLOTS) % cols) == my_col) & ((lane // per_row) == my_row)
    rank = mm(ind(lane < sub), ind(my_product))
    code = (hit - 1.0) * 64.0 + held_a * 32.0 + held_b + 1.0
    out_sub = lax.broadcasted_iota(jnp.int32, (list_ref.shape[0], 1), 0)
    listed = jnp.zeros(list_ref.shape, jnp.float32)
    for k in range(2 * ACT):
        one = jnp.sum(jnp.where(my_product & (rank == k), code, 0.0), axis=0, keepdims=True)
        listed = jnp.where(out_sub == k, one, listed)
    list_ref[...] = listed.astype(jnp.int32) - 1


def spread_kernel(piece, blocks_ref, *outs):
    mine = piece_of(lax.axis_index(("y", "col")))
    for g, out_ref in enumerate(outs):
        for t in range(SLOTS):
            at = pl.ds(pl.multiple_of(t * BS + (mine ^ (g + 1)) * piece, piece), piece)
            out_ref[t * piece : (t + 1) * piece, :] = blocks_ref[at, :]


def cross_kernel(planes, cols, piece, table_ref, blocks_ref, *refs):
    partners = len(GROUP) - 1
    piece_refs, left_refs = refs[:partners], refs[partners : partners + cols - 1]
    cross_refs, held_ref = refs[partners + cols - 1 : -1], refs[-1]
    mine = piece_of(lax.axis_index(("y", "col")))
    for t in range(SLOTS):
        at = pl.ds(pl.multiple_of(t * BS + mine * piece, piece), piece)
        held_ref[t * piece : (t + 1) * piece, :] = blocks_ref[at, :]
    size = SLOTS * piece
    for g, ref in enumerate(piece_refs):
        held_ref[(g + 1) * size : (g + 2) * size, :] = ref[...]
    for m, out_ref in enumerate(cross_refs):
        z = lax.axis_index("z") ^ (m + 1)
        for k in range(ZCAP):
            at = pl.ds(pl.multiple_of(table_ref[8 + z, k] * piece, piece), piece)
            out_ref[k * piece : (k + 1) * piece, :] = held_ref[at, :]
    for m, out_ref in enumerate(left_refs):
        col = lax.axis_index("col") ^ (m + 1)
        for k in range(LCAP):
            at = pl.ds(pl.multiple_of(table_ref[col, k] * BS, BS), BS)
            out_ref[k * BS : (k + 1) * BS, :] = blocks_ref[at, :]


def give_kernel(planes, piece, table_ref, held_ref, *refs):
    crossed_refs, outs, all_ref = refs[: planes - 1], refs[planes - 1 : -1], refs[-1]
    here = held_ref.shape[0]
    size = ZCAP * piece
    all_ref[:here, :] = held_ref[...]
    for m, ref in enumerate(crossed_refs):
        all_ref[here + m * size : here + (m + 1) * size, :] = ref[...]
    for g, out_ref in enumerate(outs):
        for k in range(RCAP):
            at = pl.ds(pl.multiple_of(table_ref[16 + g, k] * piece, piece), piece)
            out_ref[k * piece : (k + 1) * piece, :] = all_ref[at, :]


def add_products(per_row, list_ref, held_ref, out_ref, wanted):
    first = (2 * lax.axis_index("z") + lax.axis_index("y")) * per_row

    def block(at):
        x = held_ref[pl.ds(pl.multiple_of(at * BS, BS), BS), :]
        high = bf(x)
        return high, bf(x - high.astype(jnp.float32))

    def entry(i, carry):
        for k in range(2 * ACT):
            code = list_ref[k, first + i]
            a, b = (code // 32) % 32, code % 32

            @pl.when((code >= 0) & wanted(a, b))
            def _():
                a_high, a_low = block(a)
                b_high, b_low = block(b)
                at = pl.ds(pl.multiple_of((code // 1024) * BS, BS), BS)
                out_ref[at, :] += mm(a_high, b_high) + (mm(a_high, b_low) + mm(a_low, b_high))

        return carry

    lax.fori_loop(0, per_row, entry, 0)


def own_kernel(per_row, list_ref, blocks_ref, out_ref):
    out_ref[...] = jnp.zeros_like(out_ref)
    add_products(per_row, list_ref, blocks_ref, out_ref, lambda a, b: (a < SLOTS) & (b < SLOTS))


def product_kernel(cols, piece, list_ref, blocks_ref, start_ref, *refs):
    lefts, group = cols - 1, len(GROUP)
    left_refs, right_refs = refs[:lefts], refs[lefts : lefts + group]
    out_ref, held_ref = refs[lefts + group :]
    mine = piece_of(lax.axis_index(("y", "col")))
    out_ref[...] = start_ref[...]
    held_ref[: SLOTS * BS, :] = blocks_ref[...]
    at = SLOTS * BS
    for ref in left_refs:
        held_ref[at : at + LCAP * BS, :] = ref[...]
        at += LCAP * BS
    for g, ref in enumerate(right_refs):
        for k in range(RCAP):
            to = pl.ds(pl.multiple_of(at + k * BS + (mine ^ g) * piece, piece), piece)
            held_ref[to, :] = ref[k * piece : (k + 1) * piece, :]
    add_products(cols * SLOTS, list_ref, held_ref, out_ref, lambda a, b: (a >= SLOTS) | (b >= SLOTS))


def swapped(x, axis, mask):
    return lax.ppermute(x, axis, [(i, i ^ mask) for i in range(lax.axis_size(axis))])


def packed_body(blocks, block_rows, block_cols):
    planes, cols = lax.axis_size("z"), lax.axis_size("col")
    rows = 2 * planes
    plane = 2 * cols
    devices = rows * cols
    n = devices * SLOTS
    group = len(GROUP)
    piece = BS // group
    in_plane = ("y", "col")
    flat = blocks.reshape(SLOTS * BS, BS)
    params = pltpu.CompilerParams(vmem_limit_bytes=VMEM_LIMIT)
    vmem = pl.BlockSpec(memory_space=pltpu.VMEM)
    smem = pl.BlockSpec(memory_space=pltpu.SMEM)

    def floats(height):
        return jax.ShapeDtypeStruct((height, BS), jnp.float32)

    def ints(*shape):
        return jax.ShapeDtypeStruct(shape, jnp.int32)

    def call(kernel, name, ins, outs, scratch=(), specs=None):
        return pl.pallas_call(
            kernel,
            out_shape=outs,
            in_specs=ins,
            out_specs=[vmem] * len(outs) if specs is None else specs,
            scratch_shapes=scratch,
            compiler_params=params,
            name=name,
        )

    spread = call(
        lambda *refs: spread_kernel(piece, *refs), "spread", [vmem], [floats(SLOTS * piece)] * (group - 1)
    )(flat)
    pieces = [swapped(x, in_plane, mask) for x, mask in zip(spread, GROUP[1:])]
    me = lax.axis_index(("z", "y", "col"))
    idx = jnp.concatenate([block_rows[0], block_cols[0]], axis=1)
    idx = lax.psum(jnp.where(jnp.arange(devices)[:, None] == me, idx, 0), ("z", "y", "col"))
    table, listed, over = call(
        lambda *refs: plan_kernel(rows, cols, *refs),
        "plan",
        [vmem],
        [ints(24, BS), ints(8, n), ints(1, 1)],
        specs=[vmem, vmem, smem],
    )(idx)

    def packed():
        *outgoing, held = call(
            lambda *refs: cross_kernel(planes, cols, piece, *refs),
            "cross",
            [smem] + [vmem] * group,
            [floats(LCAP * BS)] * (cols - 1) + [floats(ZCAP * piece)] * (planes - 1) + [floats(group * SLOTS * piece)],
        )(table, flat, *pieces)
        crossed = [swapped(x, "z", m + 1) for m, x in enumerate(outgoing[cols - 1 :])]
        lefts = [swapped(x, "col", m + 1) for m, x in enumerate(outgoing[: cols - 1])]
        own = call(
            lambda *refs: own_kernel(cols * SLOTS, *refs), "own", [smem, vmem], [floats(SLOTS * BS)]
        )(listed, flat)
        giving = call(
            lambda *refs: give_kernel(planes, piece, *refs),
            "give",
            [smem] + [vmem] * planes,
            [floats(RCAP * piece)] * group,
            [pltpu.VMEM(((group * SLOTS + (planes - 1) * ZCAP) * piece, BS), jnp.float32)],
        )(table, held, *crossed)
        rights = [swapped(x, in_plane, mask) if mask else x for x, mask in zip(giving, GROUP)]
        out = call(
            lambda *refs: product_kernel(cols, piece, *refs),
            "products",
            [smem] + [vmem] * (2 + cols - 1 + group),
            [floats(SLOTS * BS)],
            [pltpu.VMEM(((SLOTS + (cols - 1) * LCAP + RCAP) * BS, BS), jnp.float32)],
        )(listed, flat, *own, *lefts, *rights)
        return out[0].reshape(blocks.shape)

    return lax.cond(over[0, 0] <= 0, packed, lambda: whole_tiles(blocks, block_rows, block_cols))


def solution(mesh):
    rows, cols = mesh.devices.shape
    if cols == SECTIONS and rows == 2 * SECTIONS:
        body, row = packed_body, ("z", "y")
        mesh = jax.sharding.Mesh(mesh.devices.reshape(rows // 2, 2, cols), ("z", "y", "col"))
    else:
        body, row = general_body, "row"
    return jax.shard_map(
        body,
        mesh=mesh,
        in_specs=(P(row, "col", None, None, None), P(row, "col", None), P(row, "col", None)),
        out_specs=P(row, "col", None, None, None),
        check_vma=False,
    )
```

```python
import jax
import jax.numpy as jnp
from jax import lax
from jax.experimental import pallas as pl
from jax.experimental.pallas import tpu as pltpu
from jax.sharding import PartitionSpec as P

NBLK = 512
ACT = 2
SECTIONS = 4
BS = 128
SLOTS = 8
LCAP = 5
RCAP = 5
ZCAP = 6
VMEM_LIMIT = 32 * 1024 * 1024


def from_root(x, axis, root):
    mine = lax.axis_index(axis) == root
    return lax.psum(jnp.where(mine, x, jnp.zeros_like(x)), axis)


def from_partner(x, axis, bit):
    return lax.ppermute(x, axis, [(i, i ^ 1 << bit) for i in range(lax.axis_size(axis))])


def shifted(value, axis, steps):
    count = lax.axis_size(axis)
    pairs = [(source, (source + steps) % count) for source in range(count)]
    return lax.ppermute(value, axis, pairs)


def section_product(panel, pair, out_rows, out_cols, depth):
    panel_vals, panel_rows, panel_cols = panel
    pair_vals, pair_inner, pair_cols = pair
    panel_iota = jnp.arange(panel_rows.shape[0], dtype=jnp.int32)
    pair_iota = jnp.arange(pair_inner.shape[0], dtype=jnp.int32)
    depth_iota = jnp.arange(depth, dtype=jnp.int32)
    panel_live = panel_rows >= 0
    earlier = (
        (panel_rows[None, :] == panel_rows[:, None])
        & panel_live[None, :]
        & (panel_iota[None, :] < panel_iota[:, None])
    )
    within = jnp.sum(earlier.astype(jnp.int32), axis=1)
    picked = (panel_rows[None, None, :] == out_rows[:, None, None]) & (
        within[None, None, :] == depth_iota[None, :, None]
    )
    picked = picked & panel_live[None, None, :] & (out_rows >= 0)[:, None, None]
    picked_int = picked.astype(jnp.int32)
    panel_slot = jnp.sum(picked_int * panel_iota[None, None, :], axis=2)
    found = jnp.sum(picked_int, axis=2) > 0
    inner = jnp.sum(picked_int * panel_cols[None, None, :], axis=2)
    matched = (pair_inner[None, None, :] == inner[:, :, None]) & (
        pair_cols[None, None, :] == out_cols[:, None, None]
    )
    matched = matched & (pair_inner >= 0)[None, None, :] & found[:, :, None]
    matched_int = matched.astype(jnp.int32)
    pair_slot = jnp.sum(matched_int * pair_iota[None, None, :], axis=2)
    weight = (jnp.sum(matched_int, axis=2) > 0).astype(jnp.float32)
    left = panel_vals[panel_slot] * weight[:, :, None, None]
    right = pair_vals[pair_slot]
    return jnp.einsum(
        "tqij,tqjk->tik",
        left,
        right,
        precision=lax.Precision.HIGHEST,
        preferred_element_type=jnp.float32,
    )


def make_pair(first, second, row_span):
    inner = jnp.concatenate([first[1], jnp.where(second[1] >= 0, second[1] + row_span, -1)])
    return (jnp.concatenate([first[0], second[0]]), inner, jnp.concatenate([first[2], second[2]]))


def order_pair(mine, other, is_even, row_span):
    first = tuple((jnp.where(is_even, one, two) for one, two in zip(mine, other)))
    second = tuple((jnp.where(is_even, two, one) for one, two in zip(mine, other)))
    return make_pair(first, second, row_span)


def fetch_panel(tile, row_index, col_count, section):
    root = (row_index // 2 + section) % col_count
    return tuple(from_root(one, "col", root) for one in tile)


def general_body(blocks, block_rows, block_cols):
    tile = (blocks[0, 0], block_rows[0, 0], block_cols[0, 0])
    row_count = lax.axis_size("row")
    col_count = lax.axis_size("col")
    row_span = NBLK // row_count
    row_index = lax.axis_index("row")
    is_even = row_index % 2 == 0
    depth = 2 * ACT
    total = jnp.zeros(blocks.shape[2:], jnp.float32)
    partner = from_partner((tile[0], tile[1], tile[2]), "row", 0)
    current = order_pair(tile, partner, is_even, row_span)
    for section in range(SECTIONS):
        panel = fetch_panel(tile, row_index, col_count, section)
        if section > 0:
            current = shifted((current[0], current[1], current[2]), "row", -2)
        total = total + section_product(panel, current, tile[1], tile[2], depth)
    return total[None, None]


def everything(x, axis):
    return lax.all_to_all(jnp.broadcast_to(x[None], (lax.axis_size(axis),) + x.shape), axis, 0, 0)


def whole_tiles(blocks, block_rows, block_cols):
    tile = (blocks[0, 0], block_rows[0, 0], block_cols[0, 0])
    row_span = NBLK // lax.axis_size(("z", "y"))
    col_count = lax.axis_size("col")
    row_index = lax.axis_index(("z", "y"))
    panels = tuple(everything(one, "col") for one in tile)
    column = tuple(everything(one, ("z", "y")) for one in tile)

    def section(step, total):
        root = (row_index // 2 + step) % col_count
        take = lambda arrays, at: tuple(lax.dynamic_index_in_dim(a, at, 0, False) for a in arrays)
        pair = make_pair(take(column, 2 * root), take(column, 2 * root + 1), row_span)
        return total + section_product(take(panels, root), pair, tile[1], tile[2], 2 * ACT)

    total = lax.fori_loop(0, SECTIONS, section, jnp.zeros(blocks.shape[2:], jnp.float32))
    return total[None, None]


GROUP = (0, 4)


def piece_of(p):
    return p // 4


def group_of(p):
    return p % 4


def bf(x):
    return x.astype(jnp.bfloat16)


def ind(x):
    return bf(jnp.where(x, 1.0, 0.0))


def mm(a, b, transposed=False):
    dims = (((1,), (1 if transposed else 0,)), ((), ()))
    return lax.dot_general(a, b, dims, preferred_element_type=jnp.float32)


def plan_kernel(rows, cols, idx_ref, table_ref, list_ref, over_ref):
    devices = rows * cols
    plane = 2 * cols
    n = devices * SLOTS
    in_plane = plane * SLOTS
    rb = NBLK // rows
    cb = NBLK // cols
    per_row = cols * SLOTS
    lefts = (cols - 1) * LCAP
    my_plane, my_p = lax.axis_index("z"), lax.axis_index(("y", "col"))
    my_row = 2 * my_plane + lax.axis_index("y")
    my_col = lax.axis_index("col")
    me = my_row * cols + my_col

    sub = lax.broadcasted_iota(jnp.int32, (n, 1), 0)
    lane = lax.broadcasted_iota(jnp.int32, (1, n), 1)
    dev = lax.broadcasted_iota(jnp.int32, (devices, 1), 0)
    dev_r = lax.broadcasted_iota(jnp.int32, (1, devices), 1)
    slot = lax.broadcasted_iota(jnp.int32, (1, SLOTS), 1)
    diagonal = sub == lane

    def as_row(column):
        return jnp.sum(jnp.where(diagonal, column, 0.0), axis=0, keepdims=True)

    def as_column(row):
        return jnp.sum(jnp.where(diagonal, row, 0.0), axis=1, keepdims=True)

    repeat = ind((sub // SLOTS) == dev_r)

    def column(k):
        values = mm(repeat, bf(idx_ref[:, k, :].astype(jnp.float32)))
        return jnp.sum(jnp.where((sub % SLOTS) == slot, values, 0.0), axis=1, keepdims=True)

    up = ((sub // per_row) * rb).astype(jnp.float32)
    along = (((sub // SLOTS) % cols) * cb).astype(jnp.float32)
    row_c, col_c = column(0), column(1)
    row_c = jnp.where(row_c >= 0, row_c + up, -1.0)
    col_c = jnp.where(col_c >= 0, col_c + along, -2.0)
    row_r, col_r = as_row(row_c), as_row(col_c)

    slot_r = (lane % SLOTS).astype(jnp.float32)
    hit = mm(bf(jnp.where(col_c == col_r, 1.0 + 16.0 * slot_r, 0.0)), ind(row_c == row_r))
    product = (row_c == col_r) & (hit > 0)
    product_b = ind(product)

    in_row = (lane // per_row) == (dev // cols)
    in_col = ((lane // SLOTS) % cols) == (dev % cols)
    other = (lane // SLOTS) != dev
    left = in_row & other & (mm(ind(in_col), product_b) > 0)
    right = in_col & other & (mm(ind(in_row), product_b, transposed=True) > 0)
    before = sub < lane
    same_device = (sub // SLOTS) == (lane // SLOTS)
    left_at = jnp.where(left, mm(ind(left), ind(before & same_device)), -1.0)
    right_at = jnp.where(right, mm(ind(right), ind(before)), -1.0)

    zed = lax.broadcasted_iota(jnp.int32, (8, 1), 0)
    cross = (mm(ind((dev_r // plane) == zed), ind(right)) > 0) & ((lane // in_plane) != zed)
    together = ((sub // in_plane) == (lane // in_plane)) & (
        group_of((sub // SLOTS) % plane) == group_of((lane // SLOTS) % plane)
    )
    cross_at = jnp.where(cross, mm(ind(cross), ind(before & together)), -1.0)

    over = jnp.maximum(jnp.max(left_at) - (LCAP - 1), jnp.max(right_at) - (RCAP - 1))
    over_ref[0, 0] = jnp.maximum(over, jnp.max(cross_at) - (ZCAP - 1)).astype(jnp.int32)

    lanes = lax.broadcasted_iota(jnp.int32, (1, BS), 1)

    def table(first, at, value, most):
        out = jnp.zeros((8, BS), jnp.float32)
        for k in range(most):
            one = jnp.sum(jnp.where(at == k, value + 1.0, 0.0), axis=1, keepdims=True)
            out = jnp.where(lanes == k, one, out)
        table_ref[first : first + 8, :] = out.astype(jnp.int32) - 1

    mine = (lane // SLOTS) == me
    to_col = mm(ind(my_row * cols + zed % cols == dev_r), bf(left_at))
    table(0, jnp.where(mine, to_col, -1.0), slot_r, LCAP)
    here = ((lane // in_plane) == my_plane) & (group_of((lane // SLOTS) % plane) == group_of(my_p))
    partner = piece_of((lane // SLOTS) % plane) ^ piece_of(my_p)
    local = (partner * SLOTS + lane % SLOTS).astype(jnp.float32)
    table(8, jnp.where(here, cross_at, -1.0), local, ZCAP)
    came = jnp.sum(jnp.where(zed == my_plane, cross_at, 0.0), axis=0, keepdims=True)
    away = len(GROUP) * SLOTS + ZCAP * (((lane // in_plane) ^ my_plane) - 1)
    source = jnp.where((lane // in_plane) == my_plane, local, away.astype(jnp.float32) + came)
    partners = jnp.zeros((8, devices), jnp.bool_)
    for g, mask in enumerate(GROUP):
        partners = partners | ((zed == g) & (dev_r == my_plane * plane + (my_p ^ mask)))
    table(16, mm(ind(partners), bf(right_at)), source, RCAP)

    left_me = jnp.sum(jnp.where(dev == me, left_at, 0.0), axis=0, keepdims=True)
    right_me = jnp.sum(jnp.where(dev == me, right_at, 0.0), axis=0, keepdims=True)
    from_col = ((lane // SLOTS) % cols) ^ my_col
    held_a = jnp.where(mine, slot_r, (SLOTS + LCAP * (from_col - 1)).astype(jnp.float32) + left_me)
    held_b = as_column(jnp.where(mine, slot_r, SLOTS + lefts + right_me))
    my_product = product & (((sub // SLOTS) % cols) == my_col) & ((lane // per_row) == my_row)
    rank = mm(ind(lane < sub), ind(my_product))
    code = (hit - 1.0) * 64.0 + held_a * 32.0 + held_b + 1.0
    out_sub = lax.broadcasted_iota(jnp.int32, (list_ref.shape[0], 1), 0)
    listed = jnp.zeros(list_ref.shape, jnp.float32)
    for k in range(2 * ACT):
        one = jnp.sum(jnp.where(my_product & (rank == k), code, 0.0), axis=0, keepdims=True)
        listed = jnp.where(out_sub == k, one, listed)
    list_ref[...] = listed.astype(jnp.int32) - 1


def copy_listed(table_ref, row, most, height, from_ref, to_ref):
    for k in range(most):
        at = table_ref[row, k]

        @pl.when(at >= 0)
        def _():
            here = pl.ds(pl.multiple_of(at * height, height), height)
            to_ref[k * height : (k + 1) * height, :] = from_ref[here, :]


def spread_kernel(piece, blocks_ref, *outs):
    mine = piece_of(lax.axis_index(("y", "col")))
    for g, out_ref in enumerate(outs):
        for t in range(SLOTS):
            at = pl.ds(pl.multiple_of(t * BS + (mine ^ (g + 1)) * piece, piece), piece)
            out_ref[t * piece : (t + 1) * piece, :] = blocks_ref[at, :]


def cross_kernel(planes, cols, piece, table_ref, blocks_ref, *refs):
    partners = len(GROUP) - 1
    piece_refs, left_refs = refs[:partners], refs[partners : partners + cols - 1]
    cross_refs, held_ref = refs[partners + cols - 1 : -1], refs[-1]
    mine = piece_of(lax.axis_index(("y", "col")))
    for t in range(SLOTS):
        at = pl.ds(pl.multiple_of(t * BS + mine * piece, piece), piece)
        held_ref[t * piece : (t + 1) * piece, :] = blocks_ref[at, :]
    size = SLOTS * piece
    for g, ref in enumerate(piece_refs):
        held_ref[(g + 1) * size : (g + 2) * size, :] = ref[...]
    for m, out_ref in enumerate(cross_refs):
        copy_listed(table_ref, 8 + (lax.axis_index("z") ^ (m + 1)), ZCAP, piece, held_ref, out_ref)
    for m, out_ref in enumerate(left_refs):
        copy_listed(table_ref, lax.axis_index("col") ^ (m + 1), LCAP, BS, blocks_ref, out_ref)


def give_kernel(planes, piece, table_ref, held_ref, *refs):
    crossed_refs, outs, all_ref = refs[: planes - 1], refs[planes - 1 : -1], refs[-1]
    here = held_ref.shape[0]
    size = ZCAP * piece
    all_ref[:here, :] = held_ref[...]
    for m, ref in enumerate(crossed_refs):
        all_ref[here + m * size : here + (m + 1) * size, :] = ref[...]
    for g, out_ref in enumerate(outs):
        copy_listed(table_ref, 16 + g, RCAP, piece, all_ref, out_ref)


def add_products(per_row, list_ref, held_ref, out_ref, wanted):
    first = (2 * lax.axis_index("z") + lax.axis_index("y")) * per_row

    def block(at):
        x = held_ref[pl.ds(pl.multiple_of(at * BS, BS), BS), :]
        high = bf(x)
        return high, bf(x - high.astype(jnp.float32))

    def one(i, k):
        code = list_ref[k, first + i]
        a, b = (code // 32) % 32, code % 32

        @pl.when((code >= 0) & wanted(a, b))
        def _():
            a_high, a_low = block(a)
            b_high, b_low = block(b)
            at = pl.ds(pl.multiple_of((code // 1024) * BS, BS), BS)
            out_ref[at, :] += mm(
                jnp.concatenate([a_high, a_high, a_low], axis=1), jnp.concatenate([b_high, b_low, b_high], axis=0)
            )

        if k + 1 < 2 * ACT:

            @pl.when(code >= 0)
            def _():
                one(i, k + 1)

    def entry(i, carry):
        one(i, 0)
        return carry

    lax.fori_loop(0, per_row, entry, 0)


def own_kernel(per_row, list_ref, blocks_ref, out_ref):
    out_ref[...] = jnp.zeros_like(out_ref)
    add_products(per_row, list_ref, blocks_ref, out_ref, lambda a, b: (a < SLOTS) & (b < SLOTS))


def product_kernel(cols, piece, list_ref, blocks_ref, start_ref, *refs):
    lefts, group = cols - 1, len(GROUP)
    left_refs, right_refs = refs[:lefts], refs[lefts : lefts + group]
    out_ref, held_ref = refs[lefts + group :]
    mine = piece_of(lax.axis_index(("y", "col")))
    out_ref[...] = start_ref[...]
    held_ref[: SLOTS * BS, :] = blocks_ref[...]
    at = SLOTS * BS
    for ref in left_refs:
        held_ref[at : at + LCAP * BS, :] = ref[...]
        at += LCAP * BS
    for g, ref in enumerate(right_refs):
        for k in range(RCAP):
            to = pl.ds(pl.multiple_of(at + k * BS + (mine ^ g) * piece, piece), piece)
            held_ref[to, :] = ref[k * piece : (k + 1) * piece, :]
    add_products(cols * SLOTS, list_ref, held_ref, out_ref, lambda a, b: (a >= SLOTS) | (b >= SLOTS))


def swapped(x, axis, mask):
    return lax.ppermute(x, axis, [(i, i ^ mask) for i in range(lax.axis_size(axis))])


def packed_body(blocks, block_rows, block_cols):
    planes, cols = lax.axis_size("z"), lax.axis_size("col")
    rows = 2 * planes
    plane = 2 * cols
    devices = rows * cols
    n = devices * SLOTS
    group = len(GROUP)
    piece = BS // group
    in_plane = ("y", "col")
    flat = blocks.reshape(SLOTS * BS, BS)
    params = pltpu.CompilerParams(vmem_limit_bytes=VMEM_LIMIT)
    vmem = pl.BlockSpec(memory_space=pltpu.VMEM)
    smem = pl.BlockSpec(memory_space=pltpu.SMEM)

    def floats(height):
        return jax.ShapeDtypeStruct((height, BS), jnp.float32)

    def ints(*shape):
        return jax.ShapeDtypeStruct(shape, jnp.int32)

    def call(kernel, name, ins, outs, scratch=(), specs=None):
        return pl.pallas_call(
            kernel,
            out_shape=outs,
            in_specs=ins,
            out_specs=[vmem] * len(outs) if specs is None else specs,
            scratch_shapes=scratch,
            compiler_params=params,
            name=name,
        )

    spread = call(
        lambda *refs: spread_kernel(piece, *refs), "spread", [vmem], [floats(SLOTS * piece)] * (group - 1)
    )(flat)
    pieces = [swapped(x, in_plane, mask) for x, mask in zip(spread, GROUP[1:])]
    idx = jnp.concatenate([block_rows[0], block_cols[0]])
    idx = lax.all_to_all(jnp.broadcast_to(idx[None], (devices, 2, SLOTS)), ("z", "y", "col"), 0, 0)
    table, listed, over = call(
        lambda *refs: plan_kernel(rows, cols, *refs),
        "plan",
        [vmem],
        [ints(24, BS), ints(8, n), ints(1, 1)],
        specs=[vmem, vmem, smem],
    )(idx)

    def packed():
        *outgoing, held = call(
            lambda *refs: cross_kernel(planes, cols, piece, *refs),
            "cross",
            [smem] + [vmem] * group,
            [floats(LCAP * BS)] * (cols - 1) + [floats(ZCAP * piece)] * (planes - 1) + [floats(group * SLOTS * piece)],
        )(table, flat, *pieces)
        crossed = [swapped(x, "z", m + 1) for m, x in enumerate(outgoing[cols - 1 :])]
        lefts = [swapped(x, "col", m + 1) for m, x in enumerate(outgoing[: cols - 1])]
        own = call(
            lambda *refs: own_kernel(cols * SLOTS, *refs), "own", [smem, vmem], [floats(SLOTS * BS)]
        )(listed, flat)
        held, *own = lax.optimization_barrier((held, *own))
        giving = call(
            lambda *refs: give_kernel(planes, piece, *refs),
            "give",
            [smem] + [vmem] * planes,
            [floats(RCAP * piece)] * group,
            [pltpu.VMEM(((group * SLOTS + (planes - 1) * ZCAP) * piece, BS), jnp.float32)],
        )(table, held, *crossed)
        rights = [swapped(x, in_plane, mask) if mask else x for x, mask in zip(giving, GROUP)]
        out = call(
            lambda *refs: product_kernel(cols, piece, *refs),
            "products",
            [smem] + [vmem] * (2 + cols - 1 + group),
            [floats(SLOTS * BS)],
            [pltpu.VMEM(((SLOTS + (cols - 1) * LCAP + RCAP) * BS, BS), jnp.float32)],
        )(listed, flat, *own, *lefts, *rights)
        return out[0].reshape(blocks.shape)

    return lax.cond(over[0, 0] <= 0, packed, lambda: whole_tiles(blocks, block_rows, block_cols))


def solution(mesh):
    rows, cols = mesh.devices.shape
    if cols == SECTIONS and rows == 2 * SECTIONS:
        body, row = packed_body, ("z", "y")
        mesh = jax.sharding.Mesh(mesh.devices.reshape(rows // 2, 2, cols), ("z", "y", "col"))
    else:
        body, row = general_body, "row"
    return jax.shard_map(
        body,
        mesh=mesh,
        in_specs=(P(row, "col", None, None, None), P(row, "col", None), P(row, "col", None)),
        out_specs=P(row, "col", None, None, None),
        check_vma=False,
    )
```

```python
import jax
import jax.numpy as jnp
from jax import lax
from jax.experimental import pallas as pl
from jax.experimental.pallas import tpu as pltpu
from jax.sharding import PartitionSpec as P

NBLK = 512
ACT = 2
SECTIONS = 4
BS = 128
SLOTS = 8
SIZES = ((4, 5, 6), (8, 8, 12))
LMOST, RMOST, ZMOST = SIZES[-1]
VMEM_LIMIT = 32 * 1024 * 1024


def from_root(x, axis, root):
    mine = lax.axis_index(axis) == root
    return lax.psum(jnp.where(mine, x, jnp.zeros_like(x)), axis)


def from_partner(x, axis, bit):
    return lax.ppermute(x, axis, [(i, i ^ 1 << bit) for i in range(lax.axis_size(axis))])


def shifted(value, axis, steps):
    count = lax.axis_size(axis)
    pairs = [(source, (source + steps) % count) for source in range(count)]
    return lax.ppermute(value, axis, pairs)


def section_product(panel, pair, out_rows, out_cols, depth):
    panel_vals, panel_rows, panel_cols = panel
    pair_vals, pair_inner, pair_cols = pair
    panel_iota = jnp.arange(panel_rows.shape[0], dtype=jnp.int32)
    pair_iota = jnp.arange(pair_inner.shape[0], dtype=jnp.int32)
    depth_iota = jnp.arange(depth, dtype=jnp.int32)
    panel_live = panel_rows >= 0
    earlier = (
        (panel_rows[None, :] == panel_rows[:, None])
        & panel_live[None, :]
        & (panel_iota[None, :] < panel_iota[:, None])
    )
    within = jnp.sum(earlier.astype(jnp.int32), axis=1)
    picked = (panel_rows[None, None, :] == out_rows[:, None, None]) & (
        within[None, None, :] == depth_iota[None, :, None]
    )
    picked = picked & panel_live[None, None, :] & (out_rows >= 0)[:, None, None]
    picked_int = picked.astype(jnp.int32)
    panel_slot = jnp.sum(picked_int * panel_iota[None, None, :], axis=2)
    found = jnp.sum(picked_int, axis=2) > 0
    inner = jnp.sum(picked_int * panel_cols[None, None, :], axis=2)
    matched = (pair_inner[None, None, :] == inner[:, :, None]) & (
        pair_cols[None, None, :] == out_cols[:, None, None]
    )
    matched = matched & (pair_inner >= 0)[None, None, :] & found[:, :, None]
    matched_int = matched.astype(jnp.int32)
    pair_slot = jnp.sum(matched_int * pair_iota[None, None, :], axis=2)
    weight = (jnp.sum(matched_int, axis=2) > 0).astype(jnp.float32)
    left = panel_vals[panel_slot] * weight[:, :, None, None]
    right = pair_vals[pair_slot]
    return jnp.einsum(
        "tqij,tqjk->tik",
        left,
        right,
        precision=lax.Precision.HIGHEST,
        preferred_element_type=jnp.float32,
    )


def make_pair(first, second, row_span):
    inner = jnp.concatenate([first[1], jnp.where(second[1] >= 0, second[1] + row_span, -1)])
    return (jnp.concatenate([first[0], second[0]]), inner, jnp.concatenate([first[2], second[2]]))


def order_pair(mine, other, is_even, row_span):
    first = tuple((jnp.where(is_even, one, two) for one, two in zip(mine, other)))
    second = tuple((jnp.where(is_even, two, one) for one, two in zip(mine, other)))
    return make_pair(first, second, row_span)


def fetch_panel(tile, row_index, col_count, section):
    root = (row_index // 2 + section) % col_count
    return tuple(from_root(one, "col", root) for one in tile)


def general_body(blocks, block_rows, block_cols):
    tile = (blocks[0, 0], block_rows[0, 0], block_cols[0, 0])
    row_count = lax.axis_size("row")
    col_count = lax.axis_size("col")
    row_span = NBLK // row_count
    row_index = lax.axis_index("row")
    is_even = row_index % 2 == 0
    depth = 2 * ACT
    total = jnp.zeros(blocks.shape[2:], jnp.float32)
    partner = from_partner((tile[0], tile[1], tile[2]), "row", 0)
    current = order_pair(tile, partner, is_even, row_span)
    for section in range(SECTIONS):
        panel = fetch_panel(tile, row_index, col_count, section)
        if section > 0:
            current = shifted((current[0], current[1], current[2]), "row", -2)
        total = total + section_product(panel, current, tile[1], tile[2], depth)
    return total[None, None]


def everything(x, axis):
    return lax.all_to_all(jnp.broadcast_to(x[None], (lax.axis_size(axis),) + x.shape), axis, 0, 0)


def whole_tiles(blocks, block_rows, block_cols):
    tile = (blocks[0, 0], block_rows[0, 0], block_cols[0, 0])
    row_span = NBLK // lax.axis_size(("z", "y"))
    col_count = lax.axis_size("col")
    row_index = lax.axis_index(("z", "y"))
    panels = tuple(everything(one, "col") for one in tile)
    column = tuple(everything(one, ("z", "y")) for one in tile)

    def section(step, total):
        root = (row_index // 2 + step) % col_count
        take = lambda arrays, at: tuple(lax.dynamic_index_in_dim(a, at, 0, False) for a in arrays)
        pair = make_pair(take(column, 2 * root), take(column, 2 * root + 1), row_span)
        return total + section_product(take(panels, root), pair, tile[1], tile[2], 2 * ACT)

    total = lax.fori_loop(0, SECTIONS, section, jnp.zeros(blocks.shape[2:], jnp.float32))
    return total[None, None]


GROUP = (0, 1, 4, 5)


def piece_of(p):
    return 2 * (p // 4) + p % 2


def group_of(p):
    return (p // 2) % 2


def bf(x):
    return x.astype(jnp.bfloat16)


def ind(x):
    return bf(jnp.where(x, 1.0, 0.0))


def mm(a, b, transposed=False):
    dims = (((1,), (1 if transposed else 0,)), ((), ()))
    return lax.dot_general(a, b, dims, preferred_element_type=jnp.float32)


def plan_kernel(rows, cols, idx_ref, table_ref, list_ref, size_ref):
    devices = rows * cols
    plane = 2 * cols
    n = devices * SLOTS
    in_plane = plane * SLOTS
    rb = NBLK // rows
    cb = NBLK // cols
    per_row = cols * SLOTS
    lefts = (cols - 1) * LMOST
    my_plane, my_p = lax.axis_index("z"), lax.axis_index(("y", "col"))
    my_row = 2 * my_plane + lax.axis_index("y")
    my_col = lax.axis_index("col")
    me = my_row * cols + my_col

    sub = lax.broadcasted_iota(jnp.int32, (n, 1), 0)
    lane = lax.broadcasted_iota(jnp.int32, (1, n), 1)
    dev = lax.broadcasted_iota(jnp.int32, (devices, 1), 0)
    dev_r = lax.broadcasted_iota(jnp.int32, (1, devices), 1)
    slot = lax.broadcasted_iota(jnp.int32, (1, SLOTS), 1)
    diagonal = sub == lane

    def as_row(column):
        return jnp.sum(jnp.where(diagonal, column, 0.0), axis=0, keepdims=True)

    def as_column(row):
        return jnp.sum(jnp.where(diagonal, row, 0.0), axis=1, keepdims=True)

    repeat = ind((sub // SLOTS) == dev_r)

    def column(k):
        values = mm(repeat, bf(idx_ref[:, k, :].astype(jnp.float32)))
        return jnp.sum(jnp.where((sub % SLOTS) == slot, values, 0.0), axis=1, keepdims=True)

    up = ((sub // per_row) * rb).astype(jnp.float32)
    along = (((sub // SLOTS) % cols) * cb).astype(jnp.float32)
    row_c, col_c = column(0), column(1)
    row_c = jnp.where(row_c >= 0, row_c + up, -1.0)
    col_c = jnp.where(col_c >= 0, col_c + along, -2.0)
    row_r, col_r = as_row(row_c), as_row(col_c)

    slot_r = (lane % SLOTS).astype(jnp.float32)
    hit = mm(bf(jnp.where(col_c == col_r, 1.0 + 16.0 * slot_r, 0.0)), ind(row_c == row_r))
    product = (row_c == col_r) & (hit > 0)
    product_b = ind(product)

    in_row = (lane // per_row) == (dev // cols)
    in_col = ((lane // SLOTS) % cols) == (dev % cols)
    other = (lane // SLOTS) != dev
    left = in_row & other & (mm(ind(in_col), product_b) > 0)
    right = in_col & other & (mm(ind(in_row), product_b, transposed=True) > 0)
    before = sub < lane
    same_device = (sub // SLOTS) == (lane // SLOTS)
    left_at = jnp.where(left, mm(ind(left), ind(before & same_device)), -1.0)
    right_at = jnp.where(right, mm(ind(right), ind(before)), -1.0)

    zed = lax.broadcasted_iota(jnp.int32, (8, 1), 0)
    cross = (mm(ind((dev_r // plane) == zed), ind(right)) > 0) & ((lane // in_plane) != zed)
    together = ((sub // in_plane) == (lane // in_plane)) & (
        group_of((sub // SLOTS) % plane) == group_of((lane // SLOTS) % plane)
    )
    cross_at = jnp.where(cross, mm(ind(cross), ind(before & together)), -1.0)

    tops = [jnp.max(at) + 1.0 for at in (left_at, right_at, cross_at)]
    size = jnp.int32(0)
    for most in SIZES:
        fits = (tops[0] <= most[0]) & (tops[1] <= most[1]) & (tops[2] <= most[2])
        size = size + jnp.where(fits, 0, 1)
    size_ref[0, 0] = size

    lanes = lax.broadcasted_iota(jnp.int32, (1, BS), 1)

    def table(first, at, value, most):
        out = jnp.zeros((8, BS), jnp.float32)
        for k in range(most):
            one = jnp.sum(jnp.where(at == k, value + 1.0, 0.0), axis=1, keepdims=True)
            out = jnp.where(lanes == k, one, out)
        table_ref[first : first + 8, :] = out.astype(jnp.int32) - 1

    mine = (lane // SLOTS) == me
    to_col = mm(ind(my_row * cols + zed % cols == dev_r), bf(left_at))
    table(0, jnp.where(mine, to_col, -1.0), slot_r, LMOST)
    here = ((lane // in_plane) == my_plane) & (group_of((lane // SLOTS) % plane) == group_of(my_p))
    partner = piece_of((lane // SLOTS) % plane) ^ piece_of(my_p)
    local = (partner * SLOTS + lane % SLOTS).astype(jnp.float32)
    table(8, jnp.where(here, cross_at, -1.0), local, ZMOST)
    came = jnp.sum(jnp.where(zed == my_plane, cross_at, 0.0), axis=0, keepdims=True)
    away = len(GROUP) * SLOTS + ZMOST * (((lane // in_plane) ^ my_plane) - 1)
    source = jnp.where((lane // in_plane) == my_plane, local, away.astype(jnp.float32) + came)
    partners = jnp.zeros((8, devices), jnp.bool_)
    for g, mask in enumerate(GROUP):
        partners = partners | ((zed == g) & (dev_r == my_plane * plane + (my_p ^ mask)))
    table(16, mm(ind(partners), bf(right_at)), source, RMOST)

    left_me = jnp.sum(jnp.where(dev == me, left_at, 0.0), axis=0, keepdims=True)
    right_me = jnp.sum(jnp.where(dev == me, right_at, 0.0), axis=0, keepdims=True)
    from_col = ((lane // SLOTS) % cols) ^ my_col
    held_a = jnp.where(mine, slot_r, (SLOTS + LMOST * (from_col - 1)).astype(jnp.float32) + left_me)
    held_b = as_column(jnp.where(mine, slot_r, SLOTS + lefts + right_me))
    my_product = product & (((sub // SLOTS) % cols) == my_col) & ((lane // per_row) == my_row)
    rank = mm(ind(lane < sub), ind(my_product))
    code = (hit - 1.0) * 256.0 + held_a * 64.0 + held_b + 1.0
    out_sub = lax.broadcasted_iota(jnp.int32, (list_ref.shape[0], 1), 0)
    listed = jnp.zeros(list_ref.shape, jnp.float32)
    for k in range(2 * ACT):
        one = jnp.sum(jnp.where(my_product & (rank == k), code, 0.0), axis=0, keepdims=True)
        listed = jnp.where(out_sub == k, one, listed)
    list_ref[...] = listed.astype(jnp.int32) - 1


def copy_listed(table_ref, row, most, height, sources, to_ref):
    for k in range(most):
        at = table_ref[row, k]

        @pl.when(at >= 0)
        def _():
            for ref, first, count, stride, skip in sources:

                @pl.when((at >= first) & (at < first + count))
                def _():
                    here = pl.ds(pl.multiple_of((at - first) * stride + skip, height), height)
                    to_ref[k * height : (k + 1) * height, :] = ref[here, :]


def group_pieces(piece, blocks_ref, piece_refs):
    mine = piece_of(lax.axis_index(("y", "col")))
    sources = [(blocks_ref, 0, SLOTS, BS, mine * piece)]
    return sources + [(ref, (g + 1) * SLOTS, SLOTS, piece, 0) for g, ref in enumerate(piece_refs)]


def spread_kernel(piece, blocks_ref, rows_ref, cols_ref, idx_ref, *outs):
    mine = piece_of(lax.axis_index(("y", "col")))
    for half, ref in enumerate((rows_ref, cols_ref)):
        idx_ref[:, half, :] = jnp.broadcast_to(ref[...], (idx_ref.shape[0], SLOTS))
    for g, out_ref in enumerate(outs):
        for t in range(SLOTS):
            at = pl.ds(pl.multiple_of(t * BS + (mine ^ (g + 1)) * piece, piece), piece)
            out_ref[t * piece : (t + 1) * piece, :] = blocks_ref[at, :]


def cross_kernel(piece, most, table_ref, blocks_ref, *refs):
    partners = len(GROUP) - 1
    sources = group_pieces(piece, blocks_ref, refs[:partners])
    for m, out_ref in enumerate(refs[partners:]):
        copy_listed(table_ref, 8 + (lax.axis_index("z") ^ (m + 1)), most, piece, sources, out_ref)


def left_kernel(most, table_ref, blocks_ref, *outs):
    for m, out_ref in enumerate(outs):
        copy_listed(table_ref, lax.axis_index("col") ^ (m + 1), most, BS, [(blocks_ref, 0, SLOTS, BS, 0)], out_ref)


def give_kernel(planes, piece, zmost, most, table_ref, blocks_ref, *refs):
    partners = len(GROUP) - 1
    piece_refs, crossed_refs = refs[:partners], refs[partners : partners + planes - 1]
    sources = group_pieces(piece, blocks_ref, piece_refs)
    first = len(GROUP) * SLOTS
    sources += [(ref, first + m * ZMOST, zmost, piece, 0) for m, ref in enumerate(crossed_refs)]
    for g, out_ref in enumerate(refs[partners + planes - 1 :]):
        copy_listed(table_ref, 16 + g, most, piece, sources, out_ref)


def add_products(per_row, list_ref, held_ref, out_ref, wanted):
    first = (2 * lax.axis_index("z") + lax.axis_index("y")) * per_row

    def block(at):
        x = held_ref[pl.ds(pl.multiple_of(at * BS, BS), BS), :]
        high = bf(x)
        return high, bf(x - high.astype(jnp.float32))

    def one(i, k):
        code = list_ref[k, first + i]
        a, b = (code // 64) % 64, code % 64

        @pl.when((code >= 0) & wanted(a, b))
        def _():
            a_high, a_low = block(a)
            b_high, b_low = block(b)
            at = pl.ds(pl.multiple_of((code // 4096) * BS, BS), BS)
            out_ref[at, :] += mm(
                jnp.concatenate([a_high, a_high, a_low], axis=1), jnp.concatenate([b_high, b_low, b_high], axis=0)
            )

        if k + 1 < 2 * ACT:

            @pl.when(code >= 0)
            def _():
                one(i, k + 1)

    def entry(i, carry):
        one(i, 0)
        return carry

    lax.fori_loop(0, per_row, entry, 0)


def own_kernel(per_row, list_ref, blocks_ref, out_ref):
    out_ref[...] = jnp.zeros_like(out_ref)
    add_products(per_row, list_ref, blocks_ref, out_ref, lambda a, b: (a < SLOTS) & (b < SLOTS))


def product_kernel(cols, piece, lmost, rmost, list_ref, blocks_ref, start_ref, *refs):
    lefts, group = cols - 1, len(GROUP)
    left_refs, right_refs = refs[:lefts], refs[lefts : lefts + group]
    out_ref, held_ref = refs[lefts + group :]
    mine = piece_of(lax.axis_index(("y", "col")))
    out_ref[...] = start_ref[...]
    held_ref[: SLOTS * BS, :] = blocks_ref[...]
    at = SLOTS * BS
    for ref in left_refs:
        held_ref[at : at + lmost * BS, :] = ref[...]
        at += LMOST * BS
    for g, ref in enumerate(right_refs):
        for k in range(rmost):
            to = pl.ds(pl.multiple_of(at + k * BS + (mine ^ g) * piece, piece), piece)
            held_ref[to, :] = ref[k * piece : (k + 1) * piece, :]
    add_products(cols * SLOTS, list_ref, held_ref, out_ref, lambda a, b: (a >= SLOTS) | (b >= SLOTS))


def swapped(x, axis, mask):
    return lax.ppermute(x, axis, [(i, i ^ mask) for i in range(lax.axis_size(axis))])


def packed_body(blocks, block_rows, block_cols):
    planes, cols = lax.axis_size("z"), lax.axis_size("col")
    rows = 2 * planes
    plane = 2 * cols
    devices = rows * cols
    n = devices * SLOTS
    group = len(GROUP)
    piece = BS // group
    in_plane = ("y", "col")
    flat = blocks.reshape(SLOTS * BS, BS)
    params = pltpu.CompilerParams(vmem_limit_bytes=VMEM_LIMIT)
    vmem = pl.BlockSpec(memory_space=pltpu.VMEM)
    smem = pl.BlockSpec(memory_space=pltpu.SMEM)

    def floats(height):
        return jax.ShapeDtypeStruct((height, BS), jnp.float32)

    def ints(*shape):
        return jax.ShapeDtypeStruct(shape, jnp.int32)

    def call(kernel, name, ins, outs, scratch=(), specs=None):
        return pl.pallas_call(
            kernel,
            out_shape=outs,
            in_specs=ins,
            out_specs=[vmem] * len(outs) if specs is None else specs,
            scratch_shapes=scratch,
            compiler_params=params,
            name=name,
        )

    idx, *spread = call(
        lambda *refs: spread_kernel(piece, *refs),
        "spread",
        [vmem] * 3,
        [ints(devices, 2, SLOTS)] + [floats(SLOTS * piece)] * (group - 1),
    )(flat, block_rows[0], block_cols[0])
    pieces = [swapped(x, in_plane, mask) for x, mask in zip(spread, GROUP[1:])]
    idx = lax.all_to_all(idx, ("z", "y", "col"), 0, 0)
    table, listed, size = call(
        lambda *refs: plan_kernel(rows, cols, *refs),
        "plan",
        [vmem],
        [ints(24, BS), ints(8, n), ints(1, 1)],
        specs=[vmem, vmem, smem],
    )(idx)

    def packed(lmost, rmost, zmost):
        crossing = call(
            lambda *refs: cross_kernel(piece, zmost, *refs),
            "cross",
            [smem] + [vmem] * group,
            [floats(zmost * piece)] * (planes - 1),
        )(table, flat, *pieces)
        crossed = [swapped(x, "z", m + 1) for m, x in enumerate(crossing)]
        own = call(
            lambda *refs: own_kernel(cols * SLOTS, *refs), "own", [smem, vmem], [floats(SLOTS * BS)]
        )(listed, flat)
        later, *own = lax.optimization_barrier((table, *own))
        leaving = call(
            lambda *refs: left_kernel(lmost, *refs), "left", [smem, vmem], [floats(lmost * BS)] * (cols - 1)
        )(later, flat)
        lefts = [swapped(x, "col", m + 1) for m, x in enumerate(leaving)]
        giving = call(
            lambda *refs: give_kernel(planes, piece, zmost, rmost, *refs),
            "give",
            [smem] + [vmem] * (group + planes - 1),
            [floats(rmost * piece)] * group,
        )(later, flat, *pieces, *crossed)
        rights = [swapped(x, in_plane, mask) if mask else x for x, mask in zip(giving, GROUP)]
        out = call(
            lambda *refs: product_kernel(cols, piece, lmost, rmost, *refs),
            "products",
            [smem] + [vmem] * (2 + cols - 1 + group),
            [floats(SLOTS * BS)],
            [pltpu.VMEM(((SLOTS + (cols - 1) * LMOST + rmost) * BS, BS), jnp.float32)],
        )(listed, flat, *own, *lefts, *rights)
        return out[0].reshape(blocks.shape)

    branches = [lambda most=most: packed(*most) for most in SIZES]
    return lax.switch(size[0, 0], branches + [lambda: whole_tiles(blocks, block_rows, block_cols)])


def solution(mesh):
    rows, cols = mesh.devices.shape
    if cols == SECTIONS and rows == 2 * SECTIONS:
        body, row = packed_body, ("z", "y")
        mesh = jax.sharding.Mesh(mesh.devices.reshape(rows // 2, 2, cols), ("z", "y", "col"))
    else:
        body, row = general_body, "row"
    return jax.shard_map(
        body,
        mesh=mesh,
        in_specs=(P(row, "col", None, None, None), P(row, "col", None), P(row, "col", None)),
        out_specs=P(row, "col", None, None, None),
        check_vma=False,
    )
```

```python
import jax
import jax.numpy as jnp
from jax import lax
from jax.experimental import pallas as pl
from jax.experimental.pallas import tpu as pltpu
from jax.sharding import PartitionSpec as P

NBLK = 512
ACT = 2
SECTIONS = 4
BS = 128
SLOTS = 8
SIZES = ((3, 4, 4), (4, 5, 6), (8, 8, 12))
LMOST, RMOST, ZMOST = SIZES[-1]
LEFTS, CROSS, GIVE = 0, 16, 32
VMEM_LIMIT = 32 * 1024 * 1024


def from_root(x, axis, root):
    mine = lax.axis_index(axis) == root
    return lax.psum(jnp.where(mine, x, jnp.zeros_like(x)), axis)


def from_partner(x, axis, bit):
    return lax.ppermute(x, axis, [(i, i ^ 1 << bit) for i in range(lax.axis_size(axis))])


def shifted(value, axis, steps):
    count = lax.axis_size(axis)
    pairs = [(source, (source + steps) % count) for source in range(count)]
    return lax.ppermute(value, axis, pairs)


def section_product(panel, pair, out_rows, out_cols, depth):
    panel_vals, panel_rows, panel_cols = panel
    pair_vals, pair_inner, pair_cols = pair
    panel_iota = jnp.arange(panel_rows.shape[0], dtype=jnp.int32)
    pair_iota = jnp.arange(pair_inner.shape[0], dtype=jnp.int32)
    depth_iota = jnp.arange(depth, dtype=jnp.int32)
    panel_live = panel_rows >= 0
    earlier = (
        (panel_rows[None, :] == panel_rows[:, None])
        & panel_live[None, :]
        & (panel_iota[None, :] < panel_iota[:, None])
    )
    within = jnp.sum(earlier.astype(jnp.int32), axis=1)
    picked = (panel_rows[None, None, :] == out_rows[:, None, None]) & (
        within[None, None, :] == depth_iota[None, :, None]
    )
    picked = picked & panel_live[None, None, :] & (out_rows >= 0)[:, None, None]
    picked_int = picked.astype(jnp.int32)
    panel_slot = jnp.sum(picked_int * panel_iota[None, None, :], axis=2)
    found = jnp.sum(picked_int, axis=2) > 0
    inner = jnp.sum(picked_int * panel_cols[None, None, :], axis=2)
    matched = (pair_inner[None, None, :] == inner[:, :, None]) & (
        pair_cols[None, None, :] == out_cols[:, None, None]
    )
    matched = matched & (pair_inner >= 0)[None, None, :] & found[:, :, None]
    matched_int = matched.astype(jnp.int32)
    pair_slot = jnp.sum(matched_int * pair_iota[None, None, :], axis=2)
    weight = (jnp.sum(matched_int, axis=2) > 0).astype(jnp.float32)
    left = panel_vals[panel_slot] * weight[:, :, None, None]
    right = pair_vals[pair_slot]
    return jnp.einsum(
        "tqij,tqjk->tik",
        left,
        right,
        precision=lax.Precision.HIGHEST,
        preferred_element_type=jnp.float32,
    )


def make_pair(first, second, row_span):
    inner = jnp.concatenate([first[1], jnp.where(second[1] >= 0, second[1] + row_span, -1)])
    return (jnp.concatenate([first[0], second[0]]), inner, jnp.concatenate([first[2], second[2]]))


def order_pair(mine, other, is_even, row_span):
    first = tuple((jnp.where(is_even, one, two) for one, two in zip(mine, other)))
    second = tuple((jnp.where(is_even, two, one) for one, two in zip(mine, other)))
    return make_pair(first, second, row_span)


def fetch_panel(tile, row_index, col_count, section):
    root = (row_index // 2 + section) % col_count
    return tuple(from_root(one, "col", root) for one in tile)


def general_body(blocks, block_rows, block_cols):
    tile = (blocks[0, 0], block_rows[0, 0], block_cols[0, 0])
    row_count = lax.axis_size("row")
    col_count = lax.axis_size("col")
    row_span = NBLK // row_count
    row_index = lax.axis_index("row")
    is_even = row_index % 2 == 0
    depth = 2 * ACT
    total = jnp.zeros(blocks.shape[2:], jnp.float32)
    partner = from_partner((tile[0], tile[1], tile[2]), "row", 0)
    current = order_pair(tile, partner, is_even, row_span)
    for section in range(SECTIONS):
        panel = fetch_panel(tile, row_index, col_count, section)
        if section > 0:
            current = shifted((current[0], current[1], current[2]), "row", -2)
        total = total + section_product(panel, current, tile[1], tile[2], depth)
    return total[None, None]


def everything(x, axis):
    return lax.all_to_all(jnp.broadcast_to(x[None], (lax.axis_size(axis),) + x.shape), axis, 0, 0)


def whole_tiles(blocks, block_rows, block_cols):
    tile = (blocks[0, 0], block_rows[0, 0], block_cols[0, 0])
    row_span = NBLK // lax.axis_size(("z", "y"))
    col_count = lax.axis_size("col")
    row_index = lax.axis_index(("z", "y"))
    panels = tuple(everything(one, "col") for one in tile)
    column = tuple(everything(one, ("z", "y")) for one in tile)

    def section(step, total):
        root = (row_index // 2 + step) % col_count
        take = lambda arrays, at: tuple(lax.dynamic_index_in_dim(a, at, 0, False) for a in arrays)
        pair = make_pair(take(column, 2 * root), take(column, 2 * root + 1), row_span)
        return total + section_product(take(panels, root), pair, tile[1], tile[2], 2 * ACT)

    total = lax.fori_loop(0, SECTIONS, section, jnp.zeros(blocks.shape[2:], jnp.float32))
    return total[None, None]


GROUP = (0, 1, 4, 5)


def piece_of(p):
    return 2 * (p // 4) + p % 2


def group_of(p):
    return (p // 2) % 2


def bf(x):
    return x.astype(jnp.bfloat16)


def ind(x):
    return bf(jnp.where(x, 1.0, 0.0))


def mm(a, b, transposed=False):
    dims = (((1,), (1 if transposed else 0,)), ((), ()))
    return lax.dot_general(a, b, dims, preferred_element_type=jnp.float32)


def plan_kernel(rows, cols, idx_ref, table_ref, size_ref):
    devices = rows * cols
    plane = 2 * cols
    n = devices * SLOTS
    in_plane = plane * SLOTS
    rb = NBLK // rows
    cb = NBLK // cols
    per_row = cols * SLOTS
    lefts = (cols - 1) * LMOST
    my_plane, my_p = lax.axis_index("z"), lax.axis_index(("y", "col"))
    my_row = 2 * my_plane + lax.axis_index("y")
    my_col = lax.axis_index("col")
    me = my_row * cols + my_col

    sub = lax.broadcasted_iota(jnp.int32, (n, 1), 0)
    lane = lax.broadcasted_iota(jnp.int32, (1, n), 1)
    dev = lax.broadcasted_iota(jnp.int32, (devices, 1), 0)
    dev_r = lax.broadcasted_iota(jnp.int32, (1, devices), 1)
    slot = lax.broadcasted_iota(jnp.int32, (1, SLOTS), 1)
    diagonal = sub == lane

    def as_row(column):
        return jnp.sum(jnp.where(diagonal, column, 0.0), axis=0, keepdims=True)

    def as_column(row):
        return jnp.sum(jnp.where(diagonal, row, 0.0), axis=1, keepdims=True)

    repeat = ind((sub // SLOTS) == dev_r)

    def column(k):
        values = mm(repeat, bf(idx_ref[:, k, :].astype(jnp.float32)))
        return jnp.sum(jnp.where((sub % SLOTS) == slot, values, 0.0), axis=1, keepdims=True)

    up = ((sub // per_row) * rb).astype(jnp.float32)
    along = (((sub // SLOTS) % cols) * cb).astype(jnp.float32)
    row_c, col_c = column(0), column(1)
    row_c = jnp.where(row_c >= 0, row_c + up, -1.0)
    col_c = jnp.where(col_c >= 0, col_c + along, -2.0)
    row_r, col_r = as_row(row_c), as_row(col_c)

    slot_r = (lane % SLOTS).astype(jnp.float32)
    hit = mm(bf(jnp.where(col_c == col_r, 1.0 + 16.0 * slot_r, 0.0)), ind(row_c == row_r))
    product = (row_c == col_r) & (hit > 0)
    product_b = ind(product)

    in_row = (lane // per_row) == (dev // cols)
    in_col = ((lane // SLOTS) % cols) == (dev % cols)
    other = (lane // SLOTS) != dev
    left = in_row & other & (mm(ind(in_col), product_b) > 0)
    right = in_col & other & (mm(ind(in_row), product_b, transposed=True) > 0)
    before = sub < lane
    same_device = (sub // SLOTS) == (lane // SLOTS)
    left_at = jnp.where(left, mm(ind(left), ind(before & same_device)), -1.0)
    right_at = jnp.where(right, mm(ind(right), ind(before)), -1.0)

    zed = lax.broadcasted_iota(jnp.int32, (8, 1), 0) - 4
    cross = (mm(ind((dev_r // plane) == zed), ind(right)) > 0) & ((lane // in_plane) != zed)
    together = ((sub // in_plane) == (lane // in_plane)) & (
        group_of((sub // SLOTS) % plane) == group_of((lane // SLOTS) % plane)
    )
    cross_at = jnp.where(cross, mm(ind(cross), ind(before & together)), -1.0)

    tops = [jnp.max(at) + 1.0 for at in (left_at, right_at, cross_at)]
    size = jnp.int32(0)
    for most in SIZES:
        fits = (tops[0] <= most[0]) & (tops[1] <= most[1]) & (tops[2] <= most[2])
        size = size + jnp.where(fits, 0, 1)
    size_ref[0, 0] = size

    lanes = lax.broadcasted_iota(jnp.int32, (1, BS), 1)
    out_sub = lax.broadcasted_iota(jnp.int32, (8, 1), 0)

    def listed(out, first, at, value, most):
        for k in range(most):
            one = jnp.sum(jnp.where(at == k, value + 1.0, 0.0), axis=1, keepdims=True)
            out = jnp.where((out_sub >= 4) & (lanes == first + k), one, out)
        return out

    out = jnp.zeros((8, BS), jnp.float32)
    zed = out_sub - 4
    mine = (lane // SLOTS) == me
    to_col = mm(ind((my_row * cols + zed == dev_r) & (zed >= 0)), bf(left_at))
    out = listed(out, LEFTS, jnp.where(mine, to_col, -1.0), slot_r, LMOST)
    here = ((lane // in_plane) == my_plane) & (group_of((lane // SLOTS) % plane) == group_of(my_p))
    partner = piece_of((lane // SLOTS) % plane) ^ piece_of(my_p)
    local = (partner * SLOTS + lane % SLOTS).astype(jnp.float32)
    out = listed(out, CROSS, jnp.where(here, cross_at, -1.0), local, ZMOST)
    came = jnp.sum(jnp.where(zed == my_plane, cross_at, 0.0), axis=0, keepdims=True)
    away = len(GROUP) * SLOTS + ZMOST * (((lane // in_plane) ^ my_plane) - 1)
    source = jnp.where((lane // in_plane) == my_plane, local, away.astype(jnp.float32) + came)
    partners = jnp.zeros((8, devices), jnp.bool_)
    for g, mask in enumerate(GROUP):
        partners = partners | ((zed == g) & (dev_r == my_plane * plane + (my_p ^ mask)))
    out = listed(out, GIVE, mm(ind(partners), bf(right_at)), source, RMOST)

    left_me = jnp.sum(jnp.where(dev == me, left_at, 0.0), axis=0, keepdims=True)
    right_me = jnp.sum(jnp.where(dev == me, right_at, 0.0), axis=0, keepdims=True)
    from_col = ((lane // SLOTS) % cols) ^ my_col
    held_a = jnp.where(mine, slot_r, (SLOTS + LMOST * (from_col - 1)).astype(jnp.float32) + left_me)
    held_b = as_column(jnp.where(mine, slot_r, SLOTS + lefts + right_me))
    my_product = product & (((sub // SLOTS) % cols) == my_col) & ((lane // per_row) == my_row)
    rank = mm(ind(lane < sub), ind(my_product))
    code = (hit - 1.0) * 256.0 + held_a * 64.0 + held_b + 1.0
    for k in range(2 * ACT):
        one = jnp.sum(jnp.where(my_product & (rank == k), code, 0.0), axis=0, keepdims=True)
        one = sum(one[:, i : i + BS] for i in range(0, n, BS))
        out = jnp.where(out_sub == k, one, out)
    table_ref[...] = out.astype(jnp.int32) - 1


def copy_listed(table_ref, row, first_lane, most, height, sources, to_ref):
    for k in range(most):
        at = table_ref[4 + row, first_lane + k]

        @pl.when(at >= 0)
        def _():
            for ref, first, count, stride, skip in sources:

                @pl.when((at >= first) & (at < first + count))
                def _():
                    here = pl.ds(pl.multiple_of((at - first) * stride + skip, height), height)
                    to_ref[k * height : (k + 1) * height, :] = ref[here, :]


def group_pieces(piece, blocks_ref, piece_refs):
    mine = piece_of(lax.axis_index(("y", "col")))
    sources = [(blocks_ref, 0, SLOTS, BS, mine * piece)]
    return sources + [(ref, (g + 1) * SLOTS, SLOTS, piece, 0) for g, ref in enumerate(piece_refs)]


def index_kernel(rows_ref, cols_ref, idx_ref):
    for half, ref in enumerate((rows_ref, cols_ref)):
        idx_ref[:, half, :] = jnp.broadcast_to(ref[...], (idx_ref.shape[0], SLOTS))


def spread_kernel(piece, blocks_ref, *outs):
    mine = piece_of(lax.axis_index(("y", "col")))
    for g, out_ref in enumerate(outs):
        for t in range(SLOTS):
            at = pl.ds(pl.multiple_of(t * BS + (mine ^ (g + 1)) * piece, piece), piece)
            out_ref[t * piece : (t + 1) * piece, :] = blocks_ref[at, :]


def cross_kernel(piece, most, table_ref, blocks_ref, *refs):
    partners = len(GROUP) - 1
    sources = group_pieces(piece, blocks_ref, refs[:partners])
    for m, out_ref in enumerate(refs[partners:]):
        copy_listed(table_ref, lax.axis_index("z") ^ (m + 1), CROSS, most, piece, sources, out_ref)


def left_kernel(most, table_ref, blocks_ref, *outs):
    for m, out_ref in enumerate(outs):
        copy_listed(table_ref, lax.axis_index("col") ^ (m + 1), LEFTS, most, BS, [(blocks_ref, 0, SLOTS, BS, 0)], out_ref)


def give_kernel(planes, piece, zmost, most, table_ref, blocks_ref, *refs):
    partners = len(GROUP) - 1
    piece_refs, crossed_refs = refs[:partners], refs[partners : partners + planes - 1]
    sources = group_pieces(piece, blocks_ref, piece_refs)
    first = len(GROUP) * SLOTS
    sources += [(ref, first + m * ZMOST, zmost, piece, 0) for m, ref in enumerate(crossed_refs)]
    for g, out_ref in enumerate(refs[partners + planes - 1 :]):
        copy_listed(table_ref, g, GIVE, most, piece, sources, out_ref)


def add_products(entries, table_ref, held_ref, out_ref, wanted):

    def block(at):
        x = held_ref[pl.ds(pl.multiple_of(at * BS, BS), BS), :]
        high = bf(x)
        return high, bf(x - high.astype(jnp.float32))

    def one(i, k):
        code = table_ref[k, i]
        a, b = (code // 64) % 64, code % 64

        @pl.when((code >= 0) & wanted(a, b))
        def _():
            a_high, a_low = block(a)
            b_high, b_low = block(b)
            at = pl.ds(pl.multiple_of((code // 4096) * BS, BS), BS)
            out_ref[at, :] += mm(
                jnp.concatenate([a_high, a_high, a_low], axis=1), jnp.concatenate([b_high, b_low, b_high], axis=0)
            )

        if k + 1 < 2 * ACT:

            @pl.when(code >= 0)
            def _():
                one(i, k + 1)

    def entry(i, carry):
        one(i, 0)
        return carry

    lax.fori_loop(*entries, entry, 0)


def first_entry(cols):
    return (2 * lax.axis_index("z") + lax.axis_index("y")) * cols * SLOTS % BS


def own_kernel(cols, slots, table_ref, blocks_ref, *refs):
    out_ref = refs[-1]
    out_ref[...] = refs[0][...] if len(refs) > 1 else jnp.zeros_like(out_ref)
    first = first_entry(cols) + lax.axis_index("col") * SLOTS
    entries = (first + slots[0], first + slots[1])
    add_products(entries, table_ref, blocks_ref, out_ref, lambda a, b: (a < SLOTS) & (b < SLOTS))


def product_kernel(cols, piece, lmost, rmost, table_ref, blocks_ref, start_ref, *refs):
    lefts, group = cols - 1, len(GROUP)
    left_refs, right_refs = refs[:lefts], refs[lefts : lefts + group]
    out_ref, held_ref = refs[lefts + group :]
    mine = piece_of(lax.axis_index(("y", "col")))
    out_ref[...] = start_ref[...]
    held_ref[: SLOTS * BS, :] = blocks_ref[...]
    at = SLOTS * BS
    for ref in left_refs:
        held_ref[at : at + lmost * BS, :] = ref[...]
        at += LMOST * BS
    for g, ref in enumerate(right_refs):
        for k in range(rmost):
            to = pl.ds(pl.multiple_of(at + k * BS + (mine ^ g) * piece, piece), piece)
            held_ref[to, :] = ref[k * piece : (k + 1) * piece, :]
    entries = (first_entry(cols), first_entry(cols) + cols * SLOTS)
    add_products(entries, table_ref, held_ref, out_ref, lambda a, b: (a >= SLOTS) | (b >= SLOTS))


def swapped(x, axis, mask):
    return lax.ppermute(x, axis, [(i, i ^ mask) for i in range(lax.axis_size(axis))])


def packed_body(blocks, block_rows, block_cols):
    planes, cols = lax.axis_size("z"), lax.axis_size("col")
    rows = 2 * planes
    plane = 2 * cols
    devices = rows * cols
    n = devices * SLOTS
    group = len(GROUP)
    piece = BS // group
    in_plane = ("y", "col")
    flat = blocks.reshape(SLOTS * BS, BS)
    params = pltpu.CompilerParams(vmem_limit_bytes=VMEM_LIMIT)
    vmem = pl.BlockSpec(memory_space=pltpu.VMEM)
    smem = pl.BlockSpec(memory_space=pltpu.SMEM)

    def floats(height):
        return jax.ShapeDtypeStruct((height, BS), jnp.float32)

    def ints(*shape):
        return jax.ShapeDtypeStruct(shape, jnp.int32)

    def call(kernel, name, ins, outs, scratch=(), specs=None, cost=None):
        return pl.pallas_call(
            kernel,
            out_shape=outs,
            in_specs=ins,
            out_specs=[vmem] * len(outs) if specs is None else specs,
            scratch_shapes=scratch,
            compiler_params=params,
            cost_estimate=cost,
            name=name,
        )

    idx = call(index_kernel, "index", [vmem] * 2, [ints(devices, 2, SLOTS)])(block_rows[0], block_cols[0])[0]
    idx, source = lax.optimization_barrier((idx, flat))
    spread = call(
        lambda *refs: spread_kernel(piece, *refs), "spread", [vmem], [floats(SLOTS * piece)] * (group - 1)
    )(source)
    pieces = [swapped(x, in_plane, mask) for x, mask in zip(spread, GROUP[1:])]
    idx = lax.all_to_all(idx, ("z", "y", "col"), 0, 0)
    table, size = call(
        lambda *refs: plan_kernel(rows, cols, *refs),
        "plan",
        [vmem],
        [ints(8, BS), ints(1, 1)],
        specs=[vmem, smem],
        cost=pl.CostEstimate(flops=20_000_000_000, bytes_accessed=100_000, transcendentals=0),
    )(idx)

    def packed(lmost, rmost, zmost):
        crossing = call(
            lambda *refs: cross_kernel(piece, zmost, *refs),
            "cross",
            [smem] + [vmem] * group,
            [floats(zmost * piece)] * (planes - 1),
        )(table, flat, *pieces)
        crossed = [swapped(x, "z", m + 1) for m, x in enumerate(crossing)]
        own = call(
            lambda *refs: own_kernel(cols, (0, 2), *refs), "own", [smem, vmem], [floats(SLOTS * BS)]
        )(table, flat)
        later, *own = lax.optimization_barrier((table, *own))
        leaving = call(
            lambda *refs: left_kernel(lmost, *refs), "left", [smem, vmem], [floats(lmost * BS)] * (cols - 1)
        )(later, flat)
        later, own, *leaving = lax.optimization_barrier((later, own[0], *leaving))
        own = call(
            lambda *refs: own_kernel(cols, (2, SLOTS), *refs), "own", [smem, vmem, vmem], [floats(SLOTS * BS)]
        )(later, flat, own)
        later, *own = lax.optimization_barrier((later, *own))
        lefts = [swapped(x, "col", m + 1) for m, x in enumerate(leaving)]
        giving = call(
            lambda *refs: give_kernel(planes, piece, zmost, rmost, *refs),
            "give",
            [smem] + [vmem] * (group + planes - 1),
            [floats(rmost * piece)] * group,
        )(later, flat, *pieces, *crossed)
        rights = [swapped(x, in_plane, mask) if mask else x for x, mask in zip(giving, GROUP)]
        out = call(
            lambda *refs: product_kernel(cols, piece, lmost, rmost, *refs),
            "products",
            [smem] + [vmem] * (2 + cols - 1 + group),
            [floats(SLOTS * BS)],
            [pltpu.VMEM(((SLOTS + (cols - 1) * LMOST + rmost) * BS, BS), jnp.float32)],
        )(later, flat, *own, *lefts, *rights)
        return out[0].reshape(blocks.shape)

    branches = [lambda most=most: packed(*most) for most in SIZES]
    return lax.switch(size[0, 0], branches + [lambda: whole_tiles(blocks, block_rows, block_cols)])


def solution(mesh):
    rows, cols = mesh.devices.shape
    if cols == SECTIONS and rows == 2 * SECTIONS:
        body, row = packed_body, ("z", "y")
        mesh = jax.sharding.Mesh(mesh.devices.reshape(rows // 2, 2, cols), ("z", "y", "col"))
    else:
        body, row = general_body, "row"
    return jax.shard_map(
        body,
        mesh=mesh,
        in_specs=(P(row, "col", None, None, None), P(row, "col", None), P(row, "col", None)),
        out_specs=P(row, "col", None, None, None),
        check_vma=False,
    )
```

```python
import jax
import jax.numpy as jnp
from jax import lax
from jax.experimental import pallas as pl
from jax.experimental.pallas import tpu as pltpu
from jax.sharding import PartitionSpec as P

NBLK = 512
ACT = 2
SECTIONS = 4
BS = 128
SLOTS = 8
SIZES = ((4, 3, 3), (5, 4, 4), (8, 8, 8))
LMOST, RMOST, ZMOST = SIZES[-1]
LEFTS, CROSS, GIVE = 0, 16, 32
VMEM_LIMIT = 32 * 1024 * 1024


def from_root(x, axis, root):
    mine = lax.axis_index(axis) == root
    return lax.psum(jnp.where(mine, x, jnp.zeros_like(x)), axis)


def from_partner(x, axis, bit):
    return lax.ppermute(x, axis, [(i, i ^ 1 << bit) for i in range(lax.axis_size(axis))])


def shifted(value, axis, steps):
    count = lax.axis_size(axis)
    pairs = [(source, (source + steps) % count) for source in range(count)]
    return lax.ppermute(value, axis, pairs)


def section_product(panel, pair, out_rows, out_cols, depth):
    panel_vals, panel_rows, panel_cols = panel
    pair_vals, pair_inner, pair_cols = pair
    panel_iota = jnp.arange(panel_rows.shape[0], dtype=jnp.int32)
    pair_iota = jnp.arange(pair_inner.shape[0], dtype=jnp.int32)
    depth_iota = jnp.arange(depth, dtype=jnp.int32)
    panel_live = panel_rows >= 0
    earlier = (
        (panel_rows[None, :] == panel_rows[:, None])
        & panel_live[None, :]
        & (panel_iota[None, :] < panel_iota[:, None])
    )
    within = jnp.sum(earlier.astype(jnp.int32), axis=1)
    picked = (panel_rows[None, None, :] == out_rows[:, None, None]) & (
        within[None, None, :] == depth_iota[None, :, None]
    )
    picked = picked & panel_live[None, None, :] & (out_rows >= 0)[:, None, None]
    picked_int = picked.astype(jnp.int32)
    panel_slot = jnp.sum(picked_int * panel_iota[None, None, :], axis=2)
    found = jnp.sum(picked_int, axis=2) > 0
    inner = jnp.sum(picked_int * panel_cols[None, None, :], axis=2)
    matched = (pair_inner[None, None, :] == inner[:, :, None]) & (
        pair_cols[None, None, :] == out_cols[:, None, None]
    )
    matched = matched & (pair_inner >= 0)[None, None, :] & found[:, :, None]
    matched_int = matched.astype(jnp.int32)
    pair_slot = jnp.sum(matched_int * pair_iota[None, None, :], axis=2)
    weight = (jnp.sum(matched_int, axis=2) > 0).astype(jnp.float32)
    left = panel_vals[panel_slot] * weight[:, :, None, None]
    right = pair_vals[pair_slot]
    return jnp.einsum(
        "tqij,tqjk->tik",
        left,
        right,
        precision=lax.Precision.HIGHEST,
        preferred_element_type=jnp.float32,
    )


def make_pair(first, second, row_span):
    inner = jnp.concatenate([first[1], jnp.where(second[1] >= 0, second[1] + row_span, -1)])
    return (jnp.concatenate([first[0], second[0]]), inner, jnp.concatenate([first[2], second[2]]))


def order_pair(mine, other, is_even, row_span):
    first = tuple((jnp.where(is_even, one, two) for one, two in zip(mine, other)))
    second = tuple((jnp.where(is_even, two, one) for one, two in zip(mine, other)))
    return make_pair(first, second, row_span)


def fetch_panel(tile, row_index, col_count, section):
    root = (row_index // 2 + section) % col_count
    return tuple(from_root(one, "col", root) for one in tile)


def general_body(blocks, block_rows, block_cols):
    tile = (blocks[0, 0], block_rows[0, 0], block_cols[0, 0])
    row_count = lax.axis_size("row")
    col_count = lax.axis_size("col")
    row_span = NBLK // row_count
    row_index = lax.axis_index("row")
    is_even = row_index % 2 == 0
    depth = 2 * ACT
    total = jnp.zeros(blocks.shape[2:], jnp.float32)
    partner = from_partner((tile[0], tile[1], tile[2]), "row", 0)
    current = order_pair(tile, partner, is_even, row_span)
    for section in range(SECTIONS):
        panel = fetch_panel(tile, row_index, col_count, section)
        if section > 0:
            current = shifted((current[0], current[1], current[2]), "row", -2)
        total = total + section_product(panel, current, tile[1], tile[2], depth)
    return total[None, None]


def everything(x, axis):
    return lax.all_to_all(jnp.broadcast_to(x[None], (lax.axis_size(axis),) + x.shape), axis, 0, 0)


def whole_tiles(blocks, block_rows, block_cols):
    tile = (blocks[0, 0], block_rows[0, 0], block_cols[0, 0])
    row_span = NBLK // lax.axis_size(("z", "y"))
    col_count = lax.axis_size("col")
    row_index = lax.axis_index(("z", "y"))
    panels = tuple(everything(one, "col") for one in tile)
    column = tuple(everything(one, ("z", "y")) for one in tile)

    def section(step, total):
        root = (row_index // 2 + step) % col_count
        take = lambda arrays, at: tuple(lax.dynamic_index_in_dim(a, at, 0, False) for a in arrays)
        pair = make_pair(take(column, 2 * root), take(column, 2 * root + 1), row_span)
        return total + section_product(take(panels, root), pair, tile[1], tile[2], 2 * ACT)

    total = lax.fori_loop(0, SECTIONS, section, jnp.zeros(blocks.shape[2:], jnp.float32))
    return total[None, None]


CHIP = 2 * SLOTS
GIVES = (0, 1, 4, 5)


def piece_of(p):
    return p % 2


def group_of(p):
    return p // 2


def bf(x):
    return x.astype(jnp.bfloat16)


def ind(x):
    return bf(jnp.where(x, 1.0, 0.0))


def mm(a, b, transposed=False):
    dims = (((1,), (1 if transposed else 0,)), ((), ()))
    return lax.dot_general(a, b, dims, preferred_element_type=jnp.float32)


def plan_kernel(rows, cols, idx_ref, table_ref, size_ref):
    devices = rows * cols
    plane = 2 * cols
    n = devices * SLOTS
    in_plane = plane * SLOTS
    rb = NBLK // rows
    cb = NBLK // cols
    per_row = cols * SLOTS
    my_plane, my_p = lax.axis_index("z"), lax.axis_index(("y", "col"))
    my_row = 2 * my_plane + lax.axis_index("y")
    my_col = lax.axis_index("col")
    me = my_row * cols + my_col

    sub = lax.broadcasted_iota(jnp.int32, (n, 1), 0)
    lane = lax.broadcasted_iota(jnp.int32, (1, n), 1)
    dev = lax.broadcasted_iota(jnp.int32, (devices, 1), 0)
    dev_r = lax.broadcasted_iota(jnp.int32, (1, devices), 1)
    slot = lax.broadcasted_iota(jnp.int32, (1, SLOTS), 1)
    diagonal = sub == lane

    def as_row(column):
        return jnp.sum(jnp.where(diagonal, column, 0.0), axis=0, keepdims=True)

    def as_column(row):
        return jnp.sum(jnp.where(diagonal, row, 0.0), axis=1, keepdims=True)

    repeat = ind((sub // SLOTS) == dev_r)

    def column(k):
        values = mm(repeat, bf(idx_ref[:, k, :].astype(jnp.float32)))
        return jnp.sum(jnp.where((sub % SLOTS) == slot, values, 0.0), axis=1, keepdims=True)

    up = ((sub // per_row) * rb).astype(jnp.float32)
    along = (((sub // SLOTS) % cols) * cb).astype(jnp.float32)
    row_c, col_c = column(0), column(1)
    row_c = jnp.where(row_c >= 0, row_c + up, -1.0)
    col_c = jnp.where(col_c >= 0, col_c + along, -2.0)
    row_r, col_r = as_row(row_c), as_row(col_c)

    slot_r = (lane % SLOTS).astype(jnp.float32)
    hit = mm(bf(jnp.where(col_c == col_r, 1.0 + 16.0 * slot_r, 0.0)), ind(row_c == row_r))
    product = (row_c == col_r) & (hit > 0)
    product_b = ind(product)

    in_row = (lane // per_row) == (dev // cols)
    in_col = ((lane // SLOTS) % cols) == (dev % cols)
    other = (lane // SLOTS) != dev
    left = in_row & other & (mm(ind(in_col), product_b) > 0)
    right = in_col & other & (mm(ind(in_row), product_b, transposed=True) > 0)
    before = sub < lane
    group_r = group_of((lane // SLOTS) % plane)
    same_group = group_of((sub // SLOTS) % plane) == group_r
    across = left & ((lane // CHIP) != (dev // 2))
    left_at = jnp.where(across, mm(ind(across), ind(before)), -1.0)
    right_at = jnp.where(right, mm(ind(right), ind(before & same_group)), -1.0)

    zed = lax.broadcasted_iota(jnp.int32, (8, 1), 0) - 4
    cross = (mm(ind((dev_r // plane) == zed), ind(right)) > 0) & ((lane // in_plane) != zed)
    together = same_group & ((sub // in_plane) == (lane // in_plane))
    cross_at = jnp.where(cross, mm(ind(cross), ind(before & together)), -1.0)

    tops = [jnp.max(at) + 1.0 for at in (left_at, right_at, cross_at)]
    size = jnp.int32(0)
    for most in SIZES:
        fits = (tops[0] <= most[0]) & (tops[1] <= most[1]) & (tops[2] <= most[2])
        size = size + jnp.where(fits, 0, 1)
    size_ref[0, 0] = size

    lanes = lax.broadcasted_iota(jnp.int32, (1, BS), 1)
    out_sub = lax.broadcasted_iota(jnp.int32, (8, 1), 0)

    def listed(out, first, at, value, most):
        for k in range(most):
            one = jnp.sum(jnp.where(at == k, value + 1.0, 0.0), axis=1, keepdims=True)
            out = jnp.where((out_sub >= 4) & (lanes == first + k), one, out)
        return out

    out = jnp.zeros((8, BS), jnp.float32)
    zed = out_sub - 4
    mine = (lane // SLOTS) == me
    place = (lane % SLOTS + jnp.where(mine, 0, SLOTS)).astype(jnp.float32)
    to_across = jnp.sum(jnp.where(dev == (me ^ 2), left_at, 0.0), axis=0, keepdims=True)
    out = listed(out, LEFTS, jnp.where((lane // CHIP) == me // 2, to_across, -1.0), place, LMOST)
    here = (lane // CHIP) == me // 2
    out = listed(out, CROSS, jnp.where(here, cross_at, -1.0), place, ZMOST)
    came = jnp.sum(jnp.where(zed == my_plane, cross_at, 0.0), axis=0, keepdims=True)
    away = CHIP + ZMOST * (((lane // in_plane) ^ my_plane) - 1)
    source = jnp.where((lane // in_plane) == my_plane, place, away.astype(jnp.float32) + came)
    partners = jnp.zeros((8, devices), jnp.bool_)
    for g, mask in enumerate(GIVES):
        partners = partners | ((zed == g) & (dev_r == my_plane * plane + (my_p ^ mask)))
    out = listed(out, GIVE, jnp.where(group_r == group_of(my_p), mm(ind(partners), bf(right_at)), -1.0), source, RMOST)

    left_me = jnp.sum(jnp.where(dev == me, left_at, 0.0), axis=0, keepdims=True)
    right_me = jnp.sum(jnp.where(dev == me, right_at, 0.0), axis=0, keepdims=True)
    held_a = jnp.where(here, place, CHIP + left_me)
    other_y = jnp.where((lane // per_row) % 2 == my_row % 2, 0.0, float(RMOST))
    held_b = as_column(jnp.where(mine, slot_r, CHIP + LMOST + other_y + right_me))
    my_product = product & (((sub // SLOTS) % cols) == my_col) & ((lane // per_row) == my_row)
    rank = mm(ind(lane < sub), ind(my_product))
    code = (hit - 1.0) * 256.0 + held_a * 64.0 + held_b + 1.0
    for k in range(2 * ACT):
        one = jnp.sum(jnp.where(my_product & (rank == k), code, 0.0), axis=0, keepdims=True)
        one = sum(one[:, i : i + BS] for i in range(0, n, BS))
        out = jnp.where(out_sub == k, one, out)
    table_ref[...] = out.astype(jnp.int32) - 1


def copy_listed(table_ref, row, first_lane, most, height, sources, to_ref):
    for k in range(most):
        at = table_ref[4 + row, first_lane + k]

        @pl.when(at >= 0)
        def _():
            for ref, first, count, stride, skip in sources:

                @pl.when((at >= first) & (at < first + count))
                def _():
                    here = pl.ds(pl.multiple_of((at - first) * stride + skip, height), height)
                    to_ref[k * height : (k + 1) * height, :] = ref[here, :]


def chip_halves(blocks_ref, other_ref):
    skip = piece_of(lax.axis_index(("y", "col"))) * (BS // 2)
    return [(blocks_ref, 0, SLOTS, BS, skip), (other_ref, SLOTS, SLOTS, BS, skip)]


def index_kernel(rows_ref, cols_ref, idx_ref):
    idx_ref[...] = jnp.broadcast_to(jnp.concatenate([rows_ref[...], cols_ref[...]])[None], idx_ref.shape)


def cross_kernel(most, table_ref, blocks_ref, other_ref, *outs):
    for m, out_ref in enumerate(outs):
        row = lax.axis_index("z") ^ (m + 1)
        copy_listed(table_ref, row, CROSS, most, BS // 2, chip_halves(blocks_ref, other_ref), out_ref)


def left_kernel(most, table_ref, blocks_ref, other_ref, out_ref):
    sources = [(blocks_ref, 0, SLOTS, BS, 0), (other_ref, SLOTS, SLOTS, BS, 0)]
    copy_listed(table_ref, 0, LEFTS, most, BS, sources, out_ref)


def give_kernel(planes, zmost, most, table_ref, blocks_ref, other_ref, *refs):
    sources = chip_halves(blocks_ref, other_ref)
    sources += [(ref, CHIP + m * ZMOST, zmost, BS // 2, 0) for m, ref in enumerate(refs[: planes - 1])]
    for g, out_ref in enumerate(refs[planes - 1 :]):
        copy_listed(table_ref, g, GIVE, most, BS // 2, sources, out_ref)


def add_products(entries, table_ref, left_ref, first_left, right_ref, out_ref, wanted):

    def block(held_ref, at):
        x = held_ref[pl.ds(pl.multiple_of(at * BS, BS), BS), :]
        high = bf(x)
        return high, bf(x - high.astype(jnp.float32))

    def one(i, k):
        code = table_ref[k, i]
        a, b = (code // 64) % 64, code % 64

        @pl.when((code >= 0) & wanted(a, b))
        def _():
            a_high, a_low = block(left_ref, a - first_left)
            b_high, b_low = block(right_ref, b)
            at = pl.ds(pl.multiple_of((code // 4096) * BS, BS), BS)
            out_ref[at, :] += mm(
                jnp.concatenate([a_high, a_high, a_low], axis=1), jnp.concatenate([b_high, b_low, b_high], axis=0)
            )

        if k + 1 < 2 * ACT:

            @pl.when(code >= 0)
            def _():
                one(i, k + 1)

    def entry(i, carry):
        one(i, 0)
        return carry

    lax.fori_loop(*entries, entry, 0)


def first_entry(cols):
    return (2 * lax.axis_index("z") + lax.axis_index("y")) * cols * SLOTS % BS


def own_kernel(cols, core, table_ref, left_ref, blocks_ref, *refs):
    out_ref = refs[-1]
    out_ref[...] = refs[0][...] if len(refs) > 1 else jnp.zeros_like(out_ref)
    first = first_entry(cols) + (lax.axis_index("col") ^ core) * SLOTS
    wanted = lambda a, b: b < SLOTS
    add_products((first, first + SLOTS), table_ref, left_ref, core * SLOTS, blocks_ref, out_ref, wanted)


def product_kernel(cols, lmost, rmost, table_ref, blocks_ref, other_ref, start_ref, left_ref, *refs):
    right_refs, (out_ref, held_ref) = refs[: len(GIVES)], refs[len(GIVES) :]
    half = BS // 2
    mine = piece_of(lax.axis_index(("y", "col")))
    out_ref[...] = start_ref[...]
    held_ref[: SLOTS * BS, :] = blocks_ref[...]
    held_ref[SLOTS * BS : CHIP * BS, :] = other_ref[...]
    held_ref[CHIP * BS : (CHIP + lmost) * BS, :] = left_ref[...]
    for g, ref in enumerate(right_refs):
        for k in range(rmost):
            to = (CHIP + LMOST + g // 2 * RMOST + k) * BS + (mine ^ (g % 2)) * half
            held_ref[pl.ds(pl.multiple_of(to, half), half), :] = ref[k * half : (k + 1) * half, :]
    entries = (first_entry(cols), first_entry(cols) + cols * SLOTS)
    wanted = lambda a, b: (a >= CHIP) | (b >= SLOTS)
    add_products(entries, table_ref, held_ref, 0, held_ref, out_ref, wanted)


def swapped(x, axis, mask):
    return lax.ppermute(x, axis, [(i, i ^ mask) for i in range(lax.axis_size(axis))])


def packed_body(blocks, block_rows, block_cols):
    planes, cols = lax.axis_size("z"), lax.axis_size("col")
    rows = 2 * planes
    plane = 2 * cols
    devices = rows * cols
    n = devices * SLOTS
    half = BS // 2
    in_plane = ("y", "col")
    flat = blocks.reshape(SLOTS * BS, BS)
    params = pltpu.CompilerParams(vmem_limit_bytes=VMEM_LIMIT)
    vmem = pl.BlockSpec(memory_space=pltpu.VMEM)
    smem = pl.BlockSpec(memory_space=pltpu.SMEM)

    def floats(height):
        return jax.ShapeDtypeStruct((height, BS), jnp.float32)

    def ints(*shape):
        return jax.ShapeDtypeStruct(shape, jnp.int32)

    def call(kernel, name, ins, outs, scratch=(), specs=None, cost=None):
        return pl.pallas_call(
            kernel,
            out_shape=outs,
            in_specs=ins,
            out_specs=[vmem] * len(outs) if specs is None else specs,
            scratch_shapes=scratch,
            compiler_params=params,
            cost_estimate=cost,
            name=name,
        )

    idx = call(index_kernel, "index", [vmem] * 2, [ints(devices, 2, SLOTS)])(block_rows[0], block_cols[0])[0]
    idx, source = lax.optimization_barrier((idx, flat))
    other = swapped(source, in_plane, 1)
    idx = lax.all_to_all(idx, ("z", "y", "col"), 0, 0)
    table, size = call(
        lambda *refs: plan_kernel(rows, cols, *refs),
        "plan",
        [vmem],
        [ints(8, BS), ints(1, 1)],
        specs=[vmem, smem],
        cost=pl.CostEstimate(flops=20_000_000_000, bytes_accessed=100_000, transcendentals=0),
    )(idx)

    def packed(lmost, rmost, zmost):
        crossing = call(
            lambda *refs: cross_kernel(zmost, *refs),
            "cross",
            [smem] + [vmem] * 2,
            [floats(zmost * half)] * (planes - 1),
        )(table, flat, other)
        crossed = [swapped(x, "z", m + 1) for m, x in enumerate(crossing)]
        own = call(
            lambda *refs: own_kernel(cols, 1, *refs), "other", [smem] + [vmem] * 2, [floats(SLOTS * BS)]
        )(table, other, flat)
        later, *own = lax.optimization_barrier((table, *own))
        leaving = call(
            lambda *refs: left_kernel(lmost, *refs), "left", [smem] + [vmem] * 2, [floats(lmost * BS)]
        )(later, flat, other)
        later, own, *leaving = lax.optimization_barrier((later, own[0], *leaving))
        own = call(
            lambda *refs: own_kernel(cols, 0, *refs), "own", [smem] + [vmem] * 3, [floats(SLOTS * BS)]
        )(later, flat, flat, own)
        later, *own = lax.optimization_barrier((later, *own))
        lefts = swapped(leaving[0], in_plane, 2)
        giving = call(
            lambda *refs: give_kernel(planes, zmost, rmost, *refs),
            "give",
            [smem] + [vmem] * (2 + planes - 1),
            [floats(rmost * half)] * len(GIVES),
        )(later, flat, other, *crossed)
        rights = [swapped(x, in_plane, mask) if mask else x for x, mask in zip(giving, GIVES)]
        out = call(
            lambda *refs: product_kernel(cols, lmost, rmost, *refs),
            "products",
            [smem] + [vmem] * (4 + len(GIVES)),
            [floats(SLOTS * BS)],
            [pltpu.VMEM(((CHIP + LMOST + RMOST + rmost) * BS, BS), jnp.float32)],
        )(later, flat, other, *own, lefts, *rights)
        return out[0].reshape(blocks.shape)

    branches = [lambda most=most: packed(*most) for most in SIZES]
    return lax.switch(size[0, 0], branches + [lambda: whole_tiles(blocks, block_rows, block_cols)])


def solution(mesh):
    rows, cols = mesh.devices.shape
    if cols == SECTIONS and rows == 2 * SECTIONS:
        body, row = packed_body, ("z", "y")
        mesh = jax.sharding.Mesh(mesh.devices.reshape(rows // 2, 2, cols), ("z", "y", "col"))
    else:
        body, row = general_body, "row"
    return jax.shard_map(
        body,
        mesh=mesh,
        in_specs=(P(row, "col", None, None, None), P(row, "col", None), P(row, "col", None)),
        out_specs=P(row, "col", None, None, None),
        check_vma=False,
    )
```

```python
import jax
import jax.numpy as jnp
from jax import lax
from jax.experimental import pallas as pl
from jax.experimental.pallas import tpu as pltpu
from jax.sharding import PartitionSpec as P

NBLK = 512
ACT = 2
SECTIONS = 4
BS = 128
SLOTS = 8
SIZES = ((4, 3, (4, 2, 2)), (4, 3, (4, 3, 3)), (5, 4, (5, 4, 4)), (8, 8, (8, 8, 8)))
LMOST, RMOST, ZMOST = 8, 8, 8
LEFTS, CROSS, GIVE = 0, 16, 32
VMEM_LIMIT = 32 * 1024 * 1024


def from_root(x, axis, root):
    mine = lax.axis_index(axis) == root
    return lax.psum(jnp.where(mine, x, jnp.zeros_like(x)), axis)


def from_partner(x, axis, bit):
    return lax.ppermute(x, axis, [(i, i ^ 1 << bit) for i in range(lax.axis_size(axis))])


def shifted(value, axis, steps):
    count = lax.axis_size(axis)
    pairs = [(source, (source + steps) % count) for source in range(count)]
    return lax.ppermute(value, axis, pairs)


def section_product(panel, pair, out_rows, out_cols, depth):
    panel_vals, panel_rows, panel_cols = panel
    pair_vals, pair_inner, pair_cols = pair
    panel_iota = jnp.arange(panel_rows.shape[0], dtype=jnp.int32)
    pair_iota = jnp.arange(pair_inner.shape[0], dtype=jnp.int32)
    depth_iota = jnp.arange(depth, dtype=jnp.int32)
    panel_live = panel_rows >= 0
    earlier = (
        (panel_rows[None, :] == panel_rows[:, None])
        & panel_live[None, :]
        & (panel_iota[None, :] < panel_iota[:, None])
    )
    within = jnp.sum(earlier.astype(jnp.int32), axis=1)
    picked = (panel_rows[None, None, :] == out_rows[:, None, None]) & (
        within[None, None, :] == depth_iota[None, :, None]
    )
    picked = picked & panel_live[None, None, :] & (out_rows >= 0)[:, None, None]
    picked_int = picked.astype(jnp.int32)
    panel_slot = jnp.sum(picked_int * panel_iota[None, None, :], axis=2)
    found = jnp.sum(picked_int, axis=2) > 0
    inner = jnp.sum(picked_int * panel_cols[None, None, :], axis=2)
    matched = (pair_inner[None, None, :] == inner[:, :, None]) & (
        pair_cols[None, None, :] == out_cols[:, None, None]
    )
    matched = matched & (pair_inner >= 0)[None, None, :] & found[:, :, None]
    matched_int = matched.astype(jnp.int32)
    pair_slot = jnp.sum(matched_int * pair_iota[None, None, :], axis=2)
    weight = (jnp.sum(matched_int, axis=2) > 0).astype(jnp.float32)
    left = panel_vals[panel_slot] * weight[:, :, None, None]
    right = pair_vals[pair_slot]
    return jnp.einsum(
        "tqij,tqjk->tik",
        left,
        right,
        precision=lax.Precision.HIGHEST,
        preferred_element_type=jnp.float32,
    )


def make_pair(first, second, row_span):
    inner = jnp.concatenate([first[1], jnp.where(second[1] >= 0, second[1] + row_span, -1)])
    return (jnp.concatenate([first[0], second[0]]), inner, jnp.concatenate([first[2], second[2]]))


def order_pair(mine, other, is_even, row_span):
    first = tuple((jnp.where(is_even, one, two) for one, two in zip(mine, other)))
    second = tuple((jnp.where(is_even, two, one) for one, two in zip(mine, other)))
    return make_pair(first, second, row_span)


def fetch_panel(tile, row_index, col_count, section):
    root = (row_index // 2 + section) % col_count
    return tuple(from_root(one, "col", root) for one in tile)


def general_body(blocks, block_rows, block_cols):
    tile = (blocks[0, 0], block_rows[0, 0], block_cols[0, 0])
    row_count = lax.axis_size("row")
    col_count = lax.axis_size("col")
    row_span = NBLK // row_count
    row_index = lax.axis_index("row")
    is_even = row_index % 2 == 0
    depth = 2 * ACT
    total = jnp.zeros(blocks.shape[2:], jnp.float32)
    partner = from_partner((tile[0], tile[1], tile[2]), "row", 0)
    current = order_pair(tile, partner, is_even, row_span)
    for section in range(SECTIONS):
        panel = fetch_panel(tile, row_index, col_count, section)
        if section > 0:
            current = shifted((current[0], current[1], current[2]), "row", -2)
        total = total + section_product(panel, current, tile[1], tile[2], depth)
    return total[None, None]


def everything(x, axis):
    return lax.all_to_all(jnp.broadcast_to(x[None], (lax.axis_size(axis),) + x.shape), axis, 0, 0)


def whole_tiles(blocks, block_rows, block_cols):
    tile = (blocks[0, 0], block_rows[0, 0], block_cols[0, 0])
    row_span = NBLK // lax.axis_size(("z", "y"))
    col_count = lax.axis_size("col")
    row_index = lax.axis_index(("z", "y"))
    panels = tuple(everything(one, "col") for one in tile)
    column = tuple(everything(one, ("z", "y")) for one in tile)

    def section(step, total):
        root = (row_index // 2 + step) % col_count
        take = lambda arrays, at: tuple(lax.dynamic_index_in_dim(a, at, 0, False) for a in arrays)
        pair = make_pair(take(column, 2 * root), take(column, 2 * root + 1), row_span)
        return total + section_product(take(panels, root), pair, tile[1], tile[2], 2 * ACT)

    total = lax.fori_loop(0, SECTIONS, section, jnp.zeros(blocks.shape[2:], jnp.float32))
    return total[None, None]


CHIP = 2 * SLOTS
GIVES = (0, 1, 4, 5)


def piece_of(p):
    return p % 2


def group_of(p):
    return p // 2


def bf(x):
    return x.astype(jnp.bfloat16)


def ind(x):
    return bf(jnp.where(x, 1.0, 0.0))


def mm(a, b, transposed=False):
    dims = (((1,), (1 if transposed else 0,)), ((), ()))
    return lax.dot_general(a, b, dims, preferred_element_type=jnp.float32)


def plan_kernel(rows, cols, idx_ref, table_ref, size_ref):
    devices = rows * cols
    plane = 2 * cols
    n = devices * SLOTS
    in_plane = plane * SLOTS
    rb = NBLK // rows
    cb = NBLK // cols
    per_row = cols * SLOTS
    my_plane, my_p = lax.axis_index("z"), lax.axis_index(("y", "col"))
    my_row = 2 * my_plane + lax.axis_index("y")
    my_col = lax.axis_index("col")
    me = my_row * cols + my_col

    sub = lax.broadcasted_iota(jnp.int32, (n, 1), 0)
    lane = lax.broadcasted_iota(jnp.int32, (1, n), 1)
    dev = lax.broadcasted_iota(jnp.int32, (devices, 1), 0)
    dev_r = lax.broadcasted_iota(jnp.int32, (1, devices), 1)
    slot = lax.broadcasted_iota(jnp.int32, (1, SLOTS), 1)
    diagonal = sub == lane

    def as_row(column):
        return jnp.sum(jnp.where(diagonal, column, 0.0), axis=0, keepdims=True)

    def as_column(row):
        return jnp.sum(jnp.where(diagonal, row, 0.0), axis=1, keepdims=True)

    repeat = ind((sub // SLOTS) == dev_r)

    def column(k):
        values = mm(repeat, bf(idx_ref[:, k, :].astype(jnp.float32)))
        return jnp.sum(jnp.where((sub % SLOTS) == slot, values, 0.0), axis=1, keepdims=True)

    up = ((sub // per_row) * rb).astype(jnp.float32)
    along = (((sub // SLOTS) % cols) * cb).astype(jnp.float32)
    row_c, col_c = column(0), column(1)
    row_c = jnp.where(row_c >= 0, row_c + up, -1.0)
    col_c = jnp.where(col_c >= 0, col_c + along, -2.0)
    row_r, col_r = as_row(row_c), as_row(col_c)

    slot_r = (lane % SLOTS).astype(jnp.float32)
    hit = mm(bf(jnp.where(col_c == col_r, 1.0 + 16.0 * slot_r, 0.0)), ind(row_c == row_r))
    product = (row_c == col_r) & (hit > 0)
    product_b = ind(product)

    in_row = (lane // per_row) == (dev // cols)
    in_col = ((lane // SLOTS) % cols) == (dev % cols)
    other = (lane // SLOTS) != dev
    left = in_row & other & (mm(ind(in_col), product_b) > 0)
    right = in_col & other & (mm(ind(in_row), product_b, transposed=True) > 0)
    before = sub < lane
    group_r = group_of((lane // SLOTS) % plane)
    same_group = group_of((sub // SLOTS) % plane) == group_r
    across = left & ((lane // CHIP) != (dev // 2))
    left_at = jnp.where(across, mm(ind(across), ind(before)), -1.0)
    right_at = jnp.where(right, mm(ind(right), ind(before & same_group)), -1.0)

    zed = lax.broadcasted_iota(jnp.int32, (8, 1), 0) - 4
    cross = (mm(ind((dev_r // plane) == zed), ind(right)) > 0) & ((lane // in_plane) != zed)
    together = same_group & ((sub // in_plane) == (lane // in_plane))
    cross_at = jnp.where(cross, mm(ind(cross), ind(before & together)), -1.0)

    left_top, right_top = jnp.max(left_at) + 1.0, jnp.max(right_at) + 1.0
    step = (lane // in_plane) ^ zed
    cross_tops = [jnp.max(jnp.where(step == m + 1, cross_at, -1.0)) + 1.0 for m in range(rows // 2 - 1)]
    size = jnp.int32(0)
    for lmost, rmost, zmost in SIZES:
        fits = (left_top <= lmost) & (right_top <= rmost)
        for top, most in zip(cross_tops, zmost):
            fits = fits & (top <= most)
        size = size + jnp.where(fits, 0, 1)
    size_ref[0, 0] = size

    lanes = lax.broadcasted_iota(jnp.int32, (1, BS), 1)
    out_sub = lax.broadcasted_iota(jnp.int32, (8, 1), 0)

    def listed(out, first, at, value, most):
        for k in range(most):
            one = jnp.sum(jnp.where(at == k, value + 1.0, 0.0), axis=1, keepdims=True)
            out = jnp.where((out_sub >= 4) & (lanes == first + k), one, out)
        return out

    out = jnp.zeros((8, BS), jnp.float32)
    zed = out_sub - 4
    mine = (lane // SLOTS) == me
    place = (lane % SLOTS + jnp.where(mine, 0, SLOTS)).astype(jnp.float32)
    to_across = jnp.sum(jnp.where(dev == (me ^ 2), left_at, 0.0), axis=0, keepdims=True)
    out = listed(out, LEFTS, jnp.where((lane // CHIP) == me // 2, to_across, -1.0), place, LMOST)
    here = (lane // CHIP) == me // 2
    out = listed(out, CROSS, jnp.where(here, cross_at, -1.0), place, ZMOST)
    came = jnp.sum(jnp.where(zed == my_plane, cross_at, 0.0), axis=0, keepdims=True)
    away = CHIP + ZMOST * (((lane // in_plane) ^ my_plane) - 1)
    source = jnp.where((lane // in_plane) == my_plane, place, away.astype(jnp.float32) + came)
    partners = jnp.zeros((8, devices), jnp.bool_)
    for g, mask in enumerate(GIVES):
        partners = partners | ((zed == g) & (dev_r == my_plane * plane + (my_p ^ mask)))
    out = listed(out, GIVE, jnp.where(group_r == group_of(my_p), mm(ind(partners), bf(right_at)), -1.0), source, RMOST)

    left_me = jnp.sum(jnp.where(dev == me, left_at, 0.0), axis=0, keepdims=True)
    right_me = jnp.sum(jnp.where(dev == me, right_at, 0.0), axis=0, keepdims=True)
    held_a = jnp.where(here, place, CHIP + left_me)
    other_y = jnp.where((lane // per_row) % 2 == my_row % 2, 0.0, float(RMOST))
    held_b = as_column(jnp.where(mine, slot_r, CHIP + LMOST + other_y + right_me))
    my_product = product & (((sub // SLOTS) % cols) == my_col) & ((lane // per_row) == my_row)
    rank = mm(ind(lane < sub), ind(my_product))
    code = (hit - 1.0) * 256.0 + held_a * 64.0 + held_b + 1.0
    for k in range(2 * ACT):
        one = jnp.sum(jnp.where(my_product & (rank == k), code, 0.0), axis=0, keepdims=True)
        one = sum(one[:, i : i + BS] for i in range(0, n, BS))
        out = jnp.where(out_sub == k, one, out)
    table_ref[...] = out.astype(jnp.int32) - 1


def copy_listed(table_ref, row, first_lane, most, height, sources, to_ref):
    for k in range(most):
        at = table_ref[4 + row, first_lane + k]

        @pl.when(at >= 0)
        def _():
            for ref, first, count, stride, skip in sources:

                @pl.when((at >= first) & (at < first + count))
                def _():
                    here = pl.ds(pl.multiple_of((at - first) * stride + skip, height), height)
                    to_ref[k * height : (k + 1) * height, :] = ref[here, :]


def chip_halves(blocks_ref, other_ref):
    skip = piece_of(lax.axis_index(("y", "col"))) * (BS // 2)
    return [(blocks_ref, 0, SLOTS, BS, skip), (other_ref, SLOTS, SLOTS, BS, skip)]


def cross_kernel(most, table_ref, blocks_ref, other_ref, *outs):
    for m, out_ref in enumerate(outs):
        row = lax.axis_index("z") ^ (m + 1)
        copy_listed(table_ref, row, CROSS, most[m], BS // 2, chip_halves(blocks_ref, other_ref), out_ref)


def left_kernel(most, table_ref, blocks_ref, other_ref, out_ref):
    sources = [(blocks_ref, 0, SLOTS, BS, 0), (other_ref, SLOTS, SLOTS, BS, 0)]
    copy_listed(table_ref, 0, LEFTS, most, BS, sources, out_ref)


def give_kernel(planes, zmost, most, table_ref, blocks_ref, other_ref, *refs):
    sources = chip_halves(blocks_ref, other_ref)
    sources += [(ref, CHIP + m * ZMOST, zmost[m], BS // 2, 0) for m, ref in enumerate(refs[: planes - 1])]
    for g, out_ref in enumerate(refs[planes - 1 :]):
        copy_listed(table_ref, g, GIVE, most, BS // 2, sources, out_ref)


def add_products(entries, table_ref, left_ref, first_left, right_ref, out_ref, wanted):

    def block(held_ref, at):
        x = held_ref[pl.ds(pl.multiple_of(at * BS, BS), BS), :]
        high = bf(x)
        return high, bf(x - high.astype(jnp.float32))

    def one(i, k):
        code = table_ref[k, i]
        a, b = (code // 64) % 64, code % 64

        @pl.when((code >= 0) & wanted(a, b))
        def _():
            a_high, a_low = block(left_ref, a - first_left)
            b_high, b_low = block(right_ref, b)
            at = pl.ds(pl.multiple_of((code // 4096) * BS, BS), BS)
            out_ref[at, :] += mm(
                jnp.concatenate([a_high, a_high, a_low], axis=1), jnp.concatenate([b_high, b_low, b_high], axis=0)
            )

        if k + 1 < 2 * ACT:

            @pl.when(code >= 0)
            def _():
                one(i, k + 1)

    def entry(i, carry):
        one(i, 0)
        return carry

    lax.fori_loop(*entries, entry, 0)


def first_entry(cols):
    return (2 * lax.axis_index("z") + lax.axis_index("y")) * cols * SLOTS % BS


def own_kernel(cols, table_ref, blocks_ref, other_ref, out_ref):
    out_ref[...] = jnp.zeros_like(out_ref)
    for core, left_ref in enumerate((blocks_ref, other_ref)):
        first = first_entry(cols) + (lax.axis_index("col") ^ core) * SLOTS
        wanted = lambda a, b: b < SLOTS
        add_products((first, first + SLOTS), table_ref, left_ref, core * SLOTS, blocks_ref, out_ref, wanted)


def across_kernel(cols, table_ref, left_ref, blocks_ref, start_ref, out_ref):
    out_ref[...] = start_ref[...]
    first = first_entry(cols) + ((lax.axis_index("col") // 2) ^ 1) * CHIP
    wanted = lambda a, b: b < SLOTS
    add_products((first, first + CHIP), table_ref, left_ref, CHIP, blocks_ref, out_ref, wanted)


def product_kernel(cols, lmost, rmost, table_ref, blocks_ref, other_ref, start_ref, left_ref, *refs):
    right_refs, (out_ref, held_ref) = refs[: len(GIVES)], refs[len(GIVES) :]
    half = BS // 2
    mine = piece_of(lax.axis_index(("y", "col")))
    out_ref[...] = start_ref[...]
    held_ref[: SLOTS * BS, :] = blocks_ref[...]
    held_ref[SLOTS * BS : CHIP * BS, :] = other_ref[...]
    held_ref[CHIP * BS : (CHIP + lmost) * BS, :] = left_ref[...]
    for g, ref in enumerate(right_refs):
        for k in range(rmost):
            to = (CHIP + LMOST + g // 2 * RMOST + k) * BS + (mine ^ (g % 2)) * half
            held_ref[pl.ds(pl.multiple_of(to, half), half), :] = ref[k * half : (k + 1) * half, :]
    entries = (first_entry(cols), first_entry(cols) + cols * SLOTS)
    wanted = lambda a, b: b >= SLOTS
    add_products(entries, table_ref, held_ref, 0, held_ref, out_ref, wanted)


def swapped(x, axis, mask):
    return lax.ppermute(x, axis, [(i, i ^ mask) for i in range(lax.axis_size(axis))])


def packed_body(blocks, block_rows, block_cols):
    planes, cols = lax.axis_size("z"), lax.axis_size("col")
    rows = 2 * planes
    plane = 2 * cols
    devices = rows * cols
    n = devices * SLOTS
    half = BS // 2
    in_plane = ("y", "col")
    flat = blocks.reshape(SLOTS * BS, BS)
    params = pltpu.CompilerParams(vmem_limit_bytes=VMEM_LIMIT)
    vmem = pl.BlockSpec(memory_space=pltpu.VMEM)
    smem = pl.BlockSpec(memory_space=pltpu.SMEM)

    long = pl.CostEstimate(flops=20_000_000_000, bytes_accessed=100_000, transcendentals=0)

    def floats(height):
        return jax.ShapeDtypeStruct((height, BS), jnp.float32)

    def ints(*shape):
        return jax.ShapeDtypeStruct(shape, jnp.int32)

    def call(kernel, name, ins, outs, scratch=(), specs=None, cost=None):
        return pl.pallas_call(
            kernel,
            out_shape=outs,
            in_specs=ins,
            out_specs=[vmem] * len(outs) if specs is None else specs,
            scratch_shapes=scratch,
            compiler_params=params,
            cost_estimate=cost,
            name=name,
        )

    both = jnp.arange(2)[None, :, None]
    idx = jnp.where(both == 0, block_rows[0][None], block_cols[0][None])
    idx = jnp.broadcast_to(idx, (devices, 2, SLOTS))
    idx, source = lax.optimization_barrier((idx, flat))
    other = swapped(source, in_plane, 1)
    idx = lax.all_to_all(idx, ("z", "y", "col"), 0, 0)
    table, size = call(
        lambda *refs: plan_kernel(rows, cols, *refs),
        "plan",
        [vmem],
        [ints(8, BS), ints(1, 1)],
        specs=[vmem, smem],
        cost=long,
    )(idx)

    def packed(lmost, rmost, zmost):
        crossing = call(
            lambda *refs: cross_kernel(zmost, *refs),
            "cross",
            [smem] + [vmem] * 2,
            [floats(most * half) for most in zmost],
        )(table, flat, other)
        later, *crossing = lax.optimization_barrier((table, *crossing))
        crossed = [swapped(x, "z", m + 1) for m, x in enumerate(crossing)]
        own = call(lambda *refs: own_kernel(cols, *refs), "own", [smem] + [vmem] * 2, [floats(SLOTS * BS)])(
            later, flat, other
        )
        leaving = call(
            lambda *refs: left_kernel(lmost, *refs), "left", [smem] + [vmem] * 2, [floats(lmost * BS)]
        )(later, flat, other)
        later, own, *leaving = lax.optimization_barrier((later, own[0], *leaving))
        lefts = swapped(leaving[0], in_plane, 2)
        giving = call(
            lambda *refs: give_kernel(planes, zmost, rmost, *refs),
            "give",
            [smem] + [vmem] * (2 + planes - 1),
            [floats(rmost * half)] * len(GIVES),
            cost=long,
        )(later, flat, other, *crossed)
        rights = [swapped(x, in_plane, mask) if mask else x for x, mask in zip(giving, GIVES)]
        own = call(
            lambda *refs: across_kernel(cols, *refs), "across", [smem] + [vmem] * 3, [floats(SLOTS * BS)]
        )(later, lefts, flat, own)
        out = call(
            lambda *refs: product_kernel(cols, lmost, rmost, *refs),
            "products",
            [smem] + [vmem] * (4 + len(GIVES)),
            [floats(SLOTS * BS)],
            [pltpu.VMEM(((CHIP + LMOST + RMOST + rmost) * BS, BS), jnp.float32)],
        )(later, flat, other, *own, lefts, *rights)
        return out[0].reshape(blocks.shape)

    branches = [lambda most=most: packed(*most) for most in SIZES]
    return lax.switch(size[0, 0], branches + [lambda: whole_tiles(blocks, block_rows, block_cols)])


def solution(mesh):
    rows, cols = mesh.devices.shape
    if cols == SECTIONS and rows == 2 * SECTIONS:
        body, row = packed_body, ("z", "y")
        mesh = jax.sharding.Mesh(mesh.devices.reshape(rows // 2, 2, cols), ("z", "y", "col"))
    else:
        body, row = general_body, "row"
    return jax.shard_map(
        body,
        mesh=mesh,
        in_specs=(P(row, "col", None, None, None), P(row, "col", None), P(row, "col", None)),
        out_specs=P(row, "col", None, None, None),
        check_vma=False,
    )
```

```python
import jax
import jax.numpy as jnp
from jax import lax
from jax.experimental import pallas as pl
from jax.experimental.pallas import tpu as pltpu
from jax.sharding import PartitionSpec as P

NBLK = 512
ACT = 2
SECTIONS = 4
BS = 128
SLOTS = 8
SIZES = (
    (4, (3, 2), (4, 2, 2)),
    (4, (3, 3), (4, 2, 3)),
    (4, (3, 3), (4, 3, 2)),
    (4, (3, 3), (4, 3, 3)),
    (5, (4, 4), (5, 4, 4)),
    (8, (8, 8), (8, 8, 8)),
)
LMOST, RMOST, ZMOST = 8, 8, 8
LEFTS, CROSS, GIVE = 0, 16, 32
VMEM_LIMIT = 32 * 1024 * 1024


def from_root(x, axis, root):
    mine = lax.axis_index(axis) == root
    return lax.psum(jnp.where(mine, x, jnp.zeros_like(x)), axis)


def from_partner(x, axis, bit):
    return lax.ppermute(x, axis, [(i, i ^ 1 << bit) for i in range(lax.axis_size(axis))])


def shifted(value, axis, steps):
    count = lax.axis_size(axis)
    pairs = [(source, (source + steps) % count) for source in range(count)]
    return lax.ppermute(value, axis, pairs)


def section_product(panel, pair, out_rows, out_cols, depth):
    panel_vals, panel_rows, panel_cols = panel
    pair_vals, pair_inner, pair_cols = pair
    panel_iota = jnp.arange(panel_rows.shape[0], dtype=jnp.int32)
    pair_iota = jnp.arange(pair_inner.shape[0], dtype=jnp.int32)
    depth_iota = jnp.arange(depth, dtype=jnp.int32)
    panel_live = panel_rows >= 0
    earlier = (
        (panel_rows[None, :] == panel_rows[:, None])
        & panel_live[None, :]
        & (panel_iota[None, :] < panel_iota[:, None])
    )
    within = jnp.sum(earlier.astype(jnp.int32), axis=1)
    picked = (panel_rows[None, None, :] == out_rows[:, None, None]) & (
        within[None, None, :] == depth_iota[None, :, None]
    )
    picked = picked & panel_live[None, None, :] & (out_rows >= 0)[:, None, None]
    picked_int = picked.astype(jnp.int32)
    panel_slot = jnp.sum(picked_int * panel_iota[None, None, :], axis=2)
    found = jnp.sum(picked_int, axis=2) > 0
    inner = jnp.sum(picked_int * panel_cols[None, None, :], axis=2)
    matched = (pair_inner[None, None, :] == inner[:, :, None]) & (
        pair_cols[None, None, :] == out_cols[:, None, None]
    )
    matched = matched & (pair_inner >= 0)[None, None, :] & found[:, :, None]
    matched_int = matched.astype(jnp.int32)
    pair_slot = jnp.sum(matched_int * pair_iota[None, None, :], axis=2)
    weight = (jnp.sum(matched_int, axis=2) > 0).astype(jnp.float32)
    left = panel_vals[panel_slot] * weight[:, :, None, None]
    right = pair_vals[pair_slot]
    return jnp.einsum(
        "tqij,tqjk->tik",
        left,
        right,
        precision=lax.Precision.HIGHEST,
        preferred_element_type=jnp.float32,
    )


def make_pair(first, second, row_span):
    inner = jnp.concatenate([first[1], jnp.where(second[1] >= 0, second[1] + row_span, -1)])
    return (jnp.concatenate([first[0], second[0]]), inner, jnp.concatenate([first[2], second[2]]))


def order_pair(mine, other, is_even, row_span):
    first = tuple((jnp.where(is_even, one, two) for one, two in zip(mine, other)))
    second = tuple((jnp.where(is_even, two, one) for one, two in zip(mine, other)))
    return make_pair(first, second, row_span)


def fetch_panel(tile, row_index, col_count, section):
    root = (row_index // 2 + section) % col_count
    return tuple(from_root(one, "col", root) for one in tile)


def general_body(blocks, block_rows, block_cols):
    tile = (blocks[0, 0], block_rows[0, 0], block_cols[0, 0])
    row_count = lax.axis_size("row")
    col_count = lax.axis_size("col")
    row_span = NBLK // row_count
    row_index = lax.axis_index("row")
    is_even = row_index % 2 == 0
    depth = 2 * ACT
    total = jnp.zeros(blocks.shape[2:], jnp.float32)
    partner = from_partner((tile[0], tile[1], tile[2]), "row", 0)
    current = order_pair(tile, partner, is_even, row_span)
    for section in range(SECTIONS):
        panel = fetch_panel(tile, row_index, col_count, section)
        if section > 0:
            current = shifted((current[0], current[1], current[2]), "row", -2)
        total = total + section_product(panel, current, tile[1], tile[2], depth)
    return total[None, None]


def everything(x, axis):
    return lax.all_to_all(jnp.broadcast_to(x[None], (lax.axis_size(axis),) + x.shape), axis, 0, 0)


def whole_tiles(blocks, block_rows, block_cols):
    tile = (blocks[0, 0], block_rows[0, 0], block_cols[0, 0])
    row_span = NBLK // lax.axis_size(("z", "y"))
    col_count = lax.axis_size("col")
    row_index = lax.axis_index(("z", "y"))
    panels = tuple(everything(one, "col") for one in tile)
    column = tuple(everything(one, ("z", "y")) for one in tile)

    def section(step, total):
        root = (row_index // 2 + step) % col_count
        take = lambda arrays, at: tuple(lax.dynamic_index_in_dim(a, at, 0, False) for a in arrays)
        pair = make_pair(take(column, 2 * root), take(column, 2 * root + 1), row_span)
        return total + section_product(take(panels, root), pair, tile[1], tile[2], 2 * ACT)

    total = lax.fori_loop(0, SECTIONS, section, jnp.zeros(blocks.shape[2:], jnp.float32))
    return total[None, None]


CHIP = 2 * SLOTS
GIVES = (0, 1, 4, 5)


def piece_of(p):
    return p % 2


def group_of(p):
    return p // 2


def bf(x):
    return x.astype(jnp.bfloat16)


def ind(x):
    return bf(jnp.where(x, 1.0, 0.0))


def mm(a, b, transposed=False):
    dims = (((1,), (1 if transposed else 0,)), ((), ()))
    return lax.dot_general(a, b, dims, preferred_element_type=jnp.float32)


def plan_kernel(rows, cols, idx_ref, table_ref, size_ref):
    devices = rows * cols
    plane = 2 * cols
    n = devices * SLOTS
    in_plane = plane * SLOTS
    rb = NBLK // rows
    cb = NBLK // cols
    per_row = cols * SLOTS
    my_plane, my_p = lax.axis_index("z"), lax.axis_index(("y", "col"))
    my_row = 2 * my_plane + lax.axis_index("y")
    my_col = lax.axis_index("col")
    me = my_row * cols + my_col

    sub = lax.broadcasted_iota(jnp.int32, (n, 1), 0)
    lane = lax.broadcasted_iota(jnp.int32, (1, n), 1)
    dev = lax.broadcasted_iota(jnp.int32, (devices, 1), 0)
    dev_r = lax.broadcasted_iota(jnp.int32, (1, devices), 1)
    slot = lax.broadcasted_iota(jnp.int32, (1, SLOTS), 1)
    diagonal = sub == lane

    def as_row(column):
        return jnp.sum(jnp.where(diagonal, column, 0.0), axis=0, keepdims=True)

    def as_column(row):
        return jnp.sum(jnp.where(diagonal, row, 0.0), axis=1, keepdims=True)

    repeat = ind((sub // SLOTS) == dev_r)

    def column(k):
        values = mm(repeat, bf(idx_ref[:, k, :].astype(jnp.float32)))
        return jnp.sum(jnp.where((sub % SLOTS) == slot, values, 0.0), axis=1, keepdims=True)

    up = ((sub // per_row) * rb).astype(jnp.float32)
    along = (((sub // SLOTS) % cols) * cb).astype(jnp.float32)
    row_c, col_c = column(0), column(1)
    row_c = jnp.where(row_c >= 0, row_c + up, -1.0)
    col_c = jnp.where(col_c >= 0, col_c + along, -2.0)
    row_r, col_r = as_row(row_c), as_row(col_c)

    slot_r = (lane % SLOTS).astype(jnp.float32)
    hit = mm(bf(jnp.where(col_c == col_r, 1.0 + 16.0 * slot_r, 0.0)), ind(row_c == row_r))
    product = (row_c == col_r) & (hit > 0)
    product_b = ind(product)

    in_row = (lane // per_row) == (dev // cols)
    in_col = ((lane // SLOTS) % cols) == (dev % cols)
    other = (lane // SLOTS) != dev
    left = in_row & other & (mm(ind(in_col), product_b) > 0)
    right = in_col & other & (mm(ind(in_row), product_b, transposed=True) > 0)
    before = sub < lane
    group_r = group_of((lane // SLOTS) % plane)
    same_group = group_of((sub // SLOTS) % plane) == group_r
    across = left & ((lane // CHIP) != (dev // 2))
    left_at = jnp.where(across, mm(ind(across), ind(before)), -1.0)
    right_at = jnp.where(right, mm(ind(right), ind(before & same_group)), -1.0)

    zed = lax.broadcasted_iota(jnp.int32, (8, 1), 0) - 4
    cross = (mm(ind((dev_r // plane) == zed), ind(right)) > 0) & ((lane // in_plane) != zed)
    together = same_group & ((sub // in_plane) == (lane // in_plane))
    cross_at = jnp.where(cross, mm(ind(cross), ind(before & together)), -1.0)

    left_top = jnp.max(left_at) + 1.0
    same_y = ((lane // per_row) % 2) == (dev // cols) % 2
    right_tops = [jnp.max(jnp.where(same_y == one, right_at, -1.0)) + 1.0 for one in (True, False)]
    step = (lane // in_plane) ^ zed
    cross_tops = [jnp.max(jnp.where(step == m + 1, cross_at, -1.0)) + 1.0 for m in range(rows // 2 - 1)]
    size = jnp.int32(len(SIZES))
    for i, (lmost, rmost, zmost) in reversed(list(enumerate(SIZES))):
        fits = left_top <= lmost
        for top, most in zip(right_tops + cross_tops, rmost + zmost):
            fits = fits & (top <= most)
        size = jnp.where(fits, i, size)
    size_ref[0, 0] = size

    lanes = lax.broadcasted_iota(jnp.int32, (1, BS), 1)
    out_sub = lax.broadcasted_iota(jnp.int32, (8, 1), 0)

    def listed(out, first, at, value, most):
        for k in range(most):
            one = jnp.sum(jnp.where(at == k, value + 1.0, 0.0), axis=1, keepdims=True)
            out = jnp.where((out_sub >= 4) & (lanes == first + k), one, out)
        return out

    out = jnp.zeros((8, BS), jnp.float32)
    zed = out_sub - 4
    mine = (lane // SLOTS) == me
    place = (lane % SLOTS + jnp.where(mine, 0, SLOTS)).astype(jnp.float32)
    to_across = jnp.sum(jnp.where(dev == (me ^ 2), left_at, 0.0), axis=0, keepdims=True)
    out = listed(out, LEFTS, jnp.where((lane // CHIP) == me // 2, to_across, -1.0), place, LMOST)
    here = (lane // CHIP) == me // 2
    out = listed(out, CROSS, jnp.where(here, cross_at, -1.0), place, ZMOST)
    came = jnp.sum(jnp.where(zed == my_plane, cross_at, 0.0), axis=0, keepdims=True)
    away = CHIP + ZMOST * (((lane // in_plane) ^ my_plane) - 1)
    source = jnp.where((lane // in_plane) == my_plane, place, away.astype(jnp.float32) + came)
    partners = jnp.zeros((8, devices), jnp.bool_)
    for g, mask in enumerate(GIVES):
        partners = partners | ((zed == g) & (dev_r == my_plane * plane + (my_p ^ mask)))
    out = listed(out, GIVE, jnp.where(group_r == group_of(my_p), mm(ind(partners), bf(right_at)), -1.0), source, RMOST)

    left_me = jnp.sum(jnp.where(dev == me, left_at, 0.0), axis=0, keepdims=True)
    right_me = jnp.sum(jnp.where(dev == me, right_at, 0.0), axis=0, keepdims=True)
    held_a = jnp.where(here, place, CHIP + left_me)
    other_y = jnp.where((lane // per_row) % 2 == my_row % 2, 0.0, float(RMOST))
    held_b = as_column(jnp.where(mine, slot_r, CHIP + LMOST + other_y + right_me))
    my_product = product & (((sub // SLOTS) % cols) == my_col) & ((lane // per_row) == my_row)
    rank = mm(ind(lane < sub), ind(my_product))
    code = (hit - 1.0) * 256.0 + held_a * 64.0 + held_b + 1.0
    for k in range(2 * ACT):
        one = jnp.sum(jnp.where(my_product & (rank == k), code, 0.0), axis=0, keepdims=True)
        one = sum(one[:, i : i + BS] for i in range(0, n, BS))
        out = jnp.where(out_sub == k, one, out)
    table_ref[...] = out.astype(jnp.int32) - 1


def copy_listed(table_ref, row, first_lane, most, height, sources, to_ref):
    for k in range(most):
        at = table_ref[4 + row, first_lane + k]

        @pl.when(at >= 0)
        def _():
            for ref, first, count, stride, skip in sources:

                @pl.when((at >= first) & (at < first + count))
                def _():
                    here = pl.ds(pl.multiple_of((at - first) * stride + skip, height), height)
                    to_ref[k * height : (k + 1) * height, :] = ref[here, :]


def chip_halves(blocks_ref, other_ref):
    skip = piece_of(lax.axis_index(("y", "col"))) * (BS // 2)
    return [(blocks_ref, 0, SLOTS, BS, skip), (other_ref, SLOTS, SLOTS, BS, skip)]


def cross_kernel(most, table_ref, blocks_ref, other_ref, *outs):
    for m, out_ref in enumerate(outs):
        row = lax.axis_index("z") ^ (m + 1)
        copy_listed(table_ref, row, CROSS, most[m], BS // 2, chip_halves(blocks_ref, other_ref), out_ref)


def left_kernel(most, table_ref, blocks_ref, other_ref, out_ref):
    sources = [(blocks_ref, 0, SLOTS, BS, 0), (other_ref, SLOTS, SLOTS, BS, 0)]
    copy_listed(table_ref, 0, LEFTS, most, BS, sources, out_ref)


def give_kernel(planes, zmost, most, table_ref, blocks_ref, other_ref, *refs):
    sources = chip_halves(blocks_ref, other_ref)
    sources += [(ref, CHIP + m * ZMOST, zmost[m], BS // 2, 0) for m, ref in enumerate(refs[: planes - 1])]
    for g, out_ref in enumerate(refs[planes - 1 :]):
        copy_listed(table_ref, g, GIVE, most[g // 2], BS // 2, sources, out_ref)


def add_products(entries, table_ref, left_ref, first_left, right_ref, first_right, out_ref, wanted):

    def block(held_ref, at):
        x = held_ref[pl.ds(pl.multiple_of(at * BS, BS), BS), :]
        high = bf(x)
        return high, bf(x - high.astype(jnp.float32))

    def one(i, k):
        code = table_ref[k, i]
        a, b = (code // 64) % 64, code % 64

        @pl.when((code >= 0) & wanted(a, b))
        def _():
            a_high, a_low = block(left_ref, a - first_left)
            b_high, b_low = block(right_ref, b - first_right)
            at = pl.ds(pl.multiple_of((code // 4096) * BS, BS), BS)
            out_ref[at, :] += mm(
                jnp.concatenate([a_high, a_high, a_low], axis=1), jnp.concatenate([b_high, b_low, b_high], axis=0)
            )

        if k + 1 < 2 * ACT:

            @pl.when(code >= 0)
            def _():
                one(i, k + 1)

    def entry(i, carry):
        one(i, 0)
        return carry

    lax.fori_loop(*entries, entry, 0)


def first_entry(cols):
    return (2 * lax.axis_index("z") + lax.axis_index("y")) * cols * SLOTS % BS


def chip_entries(cols, cores):
    for core in cores:
        first = first_entry(cols) + (lax.axis_index("col") ^ core) * SLOTS
        yield core, (first, first + SLOTS)


def own_kernel(cols, table_ref, blocks_ref, other_ref, out_ref):
    out_ref[...] = jnp.zeros_like(out_ref)
    wanted = lambda a, b: b < SLOTS
    for core, entries in chip_entries(cols, (0, 1)):
        left_ref = (blocks_ref, other_ref)[core]
        add_products(entries, table_ref, left_ref, core * SLOTS, blocks_ref, 0, out_ref, wanted)


def across_kernel(cols, table_ref, left_ref, blocks_ref, start_ref, out_ref):
    out_ref[...] = start_ref[...]
    wanted = lambda a, b: b < SLOTS
    for _, entries in chip_entries(cols, (2, 3)):
        add_products(entries, table_ref, left_ref, CHIP, blocks_ref, 0, out_ref, wanted)


def product_kernel(cols, rmost, table_ref, blocks_ref, other_ref, start_ref, left_ref, *refs):
    right_refs, (out_ref, held_ref) = refs[: len(GIVES)], refs[len(GIVES) :]
    half = BS // 2
    mine = piece_of(lax.axis_index(("y", "col")))
    for g, ref in enumerate(right_refs):
        for k in range(rmost[g // 2]):
            to = (g // 2 * RMOST + k) * BS + (mine ^ (g % 2)) * half
            held_ref[pl.ds(pl.multiple_of(to, half), half), :] = ref[k * half : (k + 1) * half, :]
    out_ref[...] = start_ref[...]
    wanted = lambda a, b: b >= SLOTS
    for core, entries in chip_entries(cols, range(4)):
        left, first = ((blocks_ref, 0), (other_ref, SLOTS), (left_ref, CHIP), (left_ref, CHIP))[core]
        add_products(entries, table_ref, left, first, held_ref, CHIP + LMOST, out_ref, wanted)


def swapped(x, axis, mask):
    return lax.ppermute(x, axis, [(i, i ^ mask) for i in range(lax.axis_size(axis))])


def packed_body(blocks, block_rows, block_cols):
    planes, cols = lax.axis_size("z"), lax.axis_size("col")
    rows = 2 * planes
    plane = 2 * cols
    devices = rows * cols
    n = devices * SLOTS
    half = BS // 2
    in_plane = ("y", "col")
    flat = blocks.reshape(SLOTS * BS, BS)
    params = pltpu.CompilerParams(vmem_limit_bytes=VMEM_LIMIT)
    vmem = pl.BlockSpec(memory_space=pltpu.VMEM)
    smem = pl.BlockSpec(memory_space=pltpu.SMEM)

    long = pl.CostEstimate(flops=20_000_000_000, bytes_accessed=100_000, transcendentals=0)

    def floats(height):
        return jax.ShapeDtypeStruct((height, BS), jnp.float32)

    def ints(*shape):
        return jax.ShapeDtypeStruct(shape, jnp.int32)

    def call(kernel, name, ins, outs, scratch=(), specs=None, cost=None):
        return pl.pallas_call(
            kernel,
            out_shape=outs,
            in_specs=ins,
            out_specs=[vmem] * len(outs) if specs is None else specs,
            scratch_shapes=scratch,
            compiler_params=params,
            cost_estimate=cost,
            name=name,
        )

    to = jnp.arange(devices)[:, None, None]
    idx = jnp.where(jnp.arange(2)[None, :, None] == 0, block_rows[0][None], block_cols[0][None])
    idx = jnp.where(to <= lax.axis_index(("z", "y", "col")) + devices, idx, -1)
    idx, source = lax.optimization_barrier((idx, flat))
    other = swapped(source, in_plane, 1)
    idx = lax.all_to_all(idx, ("z", "y", "col"), 0, 0)
    table, size = call(
        lambda *refs: plan_kernel(rows, cols, *refs),
        "plan",
        [vmem],
        [ints(8, BS), ints(1, 1)],
        specs=[vmem, smem],
        cost=long,
    )(idx)

    def packed(lmost, rmost, zmost):
        crossing = call(
            lambda *refs: cross_kernel(zmost, *refs),
            "cross",
            [smem] + [vmem] * 2,
            [floats(most * half) for most in zmost],
        )(table, flat, other)
        later, *crossing = lax.optimization_barrier((table, *crossing))
        crossed = [swapped(crossing[m], "z", m + 1) for m in reversed(range(planes - 1))][::-1]
        own = call(lambda *refs: own_kernel(cols, *refs), "own", [smem] + [vmem] * 2, [floats(SLOTS * BS)])(
            later, flat, other
        )
        leaving = call(
            lambda *refs: left_kernel(lmost, *refs), "left", [smem] + [vmem] * 2, [floats(lmost * BS)]
        )(later, flat, other)
        later, own, *leaving = lax.optimization_barrier((later, own[0], *leaving))
        lefts = swapped(leaving[0], in_plane, 2)
        giving = call(
            lambda *refs: give_kernel(planes, zmost, rmost, *refs),
            "give",
            [smem] + [vmem] * (2 + planes - 1),
            [floats(rmost[g // 2] * half) for g in range(len(GIVES))],
            cost=long,
        )(later, flat, other, *crossed)
        rights = [swapped(x, in_plane, mask) if mask else x for x, mask in reversed(list(zip(giving, GIVES)))][::-1]
        own = call(
            lambda *refs: across_kernel(cols, *refs), "across", [smem] + [vmem] * 3, [floats(SLOTS * BS)]
        )(later, lefts, flat, own)
        out = call(
            lambda *refs: product_kernel(cols, rmost, *refs),
            "products",
            [smem] + [vmem] * (4 + len(GIVES)),
            [floats(SLOTS * BS)],
            [pltpu.VMEM(((RMOST + rmost[1]) * BS, BS), jnp.float32)],
        )(later, flat, other, *own, lefts, *rights)
        return out[0].reshape(blocks.shape)

    branches = [lambda most=most: packed(*most) for most in SIZES]
    return lax.switch(size[0, 0], branches + [lambda: whole_tiles(blocks, block_rows, block_cols)])


def solution(mesh):
    rows, cols = mesh.devices.shape
    if cols == SECTIONS and rows == 2 * SECTIONS:
        body, row = packed_body, ("z", "y")
        mesh = jax.sharding.Mesh(mesh.devices.reshape(rows // 2, 2, cols), ("z", "y", "col"))
    else:
        body, row = general_body, "row"
    return jax.shard_map(
        body,
        mesh=mesh,
        in_specs=(P(row, "col", None, None, None), P(row, "col", None), P(row, "col", None)),
        out_specs=P(row, "col", None, None, None),
        check_vma=False,
    )
```

```python
import jax
import jax.numpy as jnp
from jax import lax
from jax.experimental import pallas as pl
from jax.experimental.pallas import tpu as pltpu
from jax.sharding import PartitionSpec as P

NBLK = 512
ACT = 2
SECTIONS = 4
BS = 128
SLOTS = 8
SIZES = (
    (4, (3, 2), (4, 2, 2)),
    (4, (3, 3), (4, 2, 3)),
    (4, (3, 3), (4, 3, 2)),
    (4, (3, 3), (4, 3, 3)),
    (5, (4, 4), (5, 4, 4)),
    (8, (8, 8), (8, 8, 8)),
)
LMOST, RMOST, ZMOST = 8, 8, 8
LEFTS, CROSS, GIVE = 0, 16, 32
VMEM_LIMIT = 32 * 1024 * 1024


def from_root(x, axis, root):
    mine = lax.axis_index(axis) == root
    return lax.psum(jnp.where(mine, x, jnp.zeros_like(x)), axis)


def from_partner(x, axis, bit):
    return lax.ppermute(x, axis, [(i, i ^ 1 << bit) for i in range(lax.axis_size(axis))])


def shifted(value, axis, steps):
    count = lax.axis_size(axis)
    pairs = [(source, (source + steps) % count) for source in range(count)]
    return lax.ppermute(value, axis, pairs)


def section_product(panel, pair, out_rows, out_cols, depth):
    panel_vals, panel_rows, panel_cols = panel
    pair_vals, pair_inner, pair_cols = pair
    panel_iota = jnp.arange(panel_rows.shape[0], dtype=jnp.int32)
    pair_iota = jnp.arange(pair_inner.shape[0], dtype=jnp.int32)
    depth_iota = jnp.arange(depth, dtype=jnp.int32)
    panel_live = panel_rows >= 0
    earlier = (
        (panel_rows[None, :] == panel_rows[:, None])
        & panel_live[None, :]
        & (panel_iota[None, :] < panel_iota[:, None])
    )
    within = jnp.sum(earlier.astype(jnp.int32), axis=1)
    picked = (panel_rows[None, None, :] == out_rows[:, None, None]) & (
        within[None, None, :] == depth_iota[None, :, None]
    )
    picked = picked & panel_live[None, None, :] & (out_rows >= 0)[:, None, None]
    picked_int = picked.astype(jnp.int32)
    panel_slot = jnp.sum(picked_int * panel_iota[None, None, :], axis=2)
    found = jnp.sum(picked_int, axis=2) > 0
    inner = jnp.sum(picked_int * panel_cols[None, None, :], axis=2)
    matched = (pair_inner[None, None, :] == inner[:, :, None]) & (
        pair_cols[None, None, :] == out_cols[:, None, None]
    )
    matched = matched & (pair_inner >= 0)[None, None, :] & found[:, :, None]
    matched_int = matched.astype(jnp.int32)
    pair_slot = jnp.sum(matched_int * pair_iota[None, None, :], axis=2)
    weight = (jnp.sum(matched_int, axis=2) > 0).astype(jnp.float32)
    left = panel_vals[panel_slot] * weight[:, :, None, None]
    right = pair_vals[pair_slot]
    return jnp.einsum(
        "tqij,tqjk->tik",
        left,
        right,
        precision=lax.Precision.HIGHEST,
        preferred_element_type=jnp.float32,
    )


def make_pair(first, second, row_span):
    inner = jnp.concatenate([first[1], jnp.where(second[1] >= 0, second[1] + row_span, -1)])
    return (jnp.concatenate([first[0], second[0]]), inner, jnp.concatenate([first[2], second[2]]))


def order_pair(mine, other, is_even, row_span):
    first = tuple((jnp.where(is_even, one, two) for one, two in zip(mine, other)))
    second = tuple((jnp.where(is_even, two, one) for one, two in zip(mine, other)))
    return make_pair(first, second, row_span)


def fetch_panel(tile, row_index, col_count, section):
    root = (row_index // 2 + section) % col_count
    return tuple(from_root(one, "col", root) for one in tile)


def general_body(blocks, block_rows, block_cols):
    tile = (blocks[0, 0], block_rows[0, 0], block_cols[0, 0])
    row_count = lax.axis_size("row")
    col_count = lax.axis_size("col")
    row_span = NBLK // row_count
    row_index = lax.axis_index("row")
    is_even = row_index % 2 == 0
    depth = 2 * ACT
    total = jnp.zeros(blocks.shape[2:], jnp.float32)
    partner = from_partner((tile[0], tile[1], tile[2]), "row", 0)
    current = order_pair(tile, partner, is_even, row_span)
    for section in range(SECTIONS):
        panel = fetch_panel(tile, row_index, col_count, section)
        if section > 0:
            current = shifted((current[0], current[1], current[2]), "row", -2)
        total = total + section_product(panel, current, tile[1], tile[2], depth)
    return total[None, None]


COL = ("x", "core")
IN_PLANE = ("y", "x", "core")


def everything(x, axis):
    return lax.all_to_all(jnp.broadcast_to(x[None], (lax.axis_size(axis),) + x.shape), axis, 0, 0)


def whole_tiles(blocks, block_rows, block_cols):
    tile = (blocks[0, 0], block_rows[0, 0], block_cols[0, 0])
    row_span = NBLK // lax.axis_size(("z", "y"))
    col_count = lax.axis_size(COL)
    row_index = lax.axis_index(("z", "y"))
    panels = tuple(everything(one, COL) for one in tile)
    column = tuple(everything(one, ("z", "y")) for one in tile)

    def section(step, total):
        root = (row_index // 2 + step) % col_count
        take = lambda arrays, at: tuple(lax.dynamic_index_in_dim(a, at, 0, False) for a in arrays)
        pair = make_pair(take(column, 2 * root), take(column, 2 * root + 1), row_span)
        return total + section_product(take(panels, root), pair, tile[1], tile[2], 2 * ACT)

    total = lax.fori_loop(0, SECTIONS, section, jnp.zeros(blocks.shape[2:], jnp.float32))
    return total[None, None]


CHIP = 2 * SLOTS
GIVES = (0, 1, 4, 5)


def piece_of(p):
    return p % 2


def group_of(p):
    return p // 2


def bf(x):
    return x.astype(jnp.bfloat16)


def ind(x):
    return bf(jnp.where(x, 1.0, 0.0))


def mm(a, b, transposed=False):
    dims = (((1,), (1 if transposed else 0,)), ((), ()))
    return lax.dot_general(a, b, dims, preferred_element_type=jnp.float32)


def plan_kernel(rows, cols, idx_ref, table_ref, size_ref):
    devices = rows * cols
    plane = 2 * cols
    n = devices * SLOTS
    in_plane = plane * SLOTS
    rb = NBLK // rows
    cb = NBLK // cols
    per_row = cols * SLOTS
    my_plane, my_p = lax.axis_index("z"), lax.axis_index(IN_PLANE)
    my_row = 2 * my_plane + lax.axis_index("y")
    my_col = lax.axis_index(COL)
    me = my_row * cols + my_col

    sub = lax.broadcasted_iota(jnp.int32, (n, 1), 0)
    lane = lax.broadcasted_iota(jnp.int32, (1, n), 1)
    dev = lax.broadcasted_iota(jnp.int32, (devices, 1), 0)
    dev_r = lax.broadcasted_iota(jnp.int32, (1, devices), 1)
    slot = lax.broadcasted_iota(jnp.int32, (1, SLOTS), 1)
    diagonal = sub == lane

    def as_row(column):
        return jnp.sum(jnp.where(diagonal, column, 0.0), axis=0, keepdims=True)

    def as_column(row):
        return jnp.sum(jnp.where(diagonal, row, 0.0), axis=1, keepdims=True)

    chip = lax.broadcasted_iota(jnp.int32, (1, devices // 2), 1)
    other_core = ((sub // SLOTS) % 2) != lax.axis_index("core")
    from_chip = (sub // CHIP) == chip
    repeats = [ind(from_chip & jnp.logical_not(other_core)), ind(from_chip & other_core)]

    def column(k):
        parts = [bf(idx_ref[:, 2 * i + k, :].astype(jnp.float32)) for i in range(2)]
        values = mm(repeats[0], parts[0]) + mm(repeats[1], parts[1])
        return jnp.sum(jnp.where((sub % SLOTS) == slot, values, 0.0), axis=1, keepdims=True)

    up = ((sub // per_row) * rb).astype(jnp.float32)
    along = (((sub // SLOTS) % cols) * cb).astype(jnp.float32)
    row_c, col_c = column(0), column(1)
    row_c = jnp.where(row_c >= 0, row_c + up, -1.0)
    col_c = jnp.where(col_c >= 0, col_c + along, -2.0)
    row_r, col_r = as_row(row_c), as_row(col_c)

    slot_r = (lane % SLOTS).astype(jnp.float32)
    hit = mm(bf(jnp.where(col_c == col_r, 1.0 + 16.0 * slot_r, 0.0)), ind(row_c == row_r))
    product = (row_c == col_r) & (hit > 0)
    product_b = ind(product)

    in_row = (lane // per_row) == (dev // cols)
    in_col = ((lane // SLOTS) % cols) == (dev % cols)
    other = (lane // SLOTS) != dev
    left = in_row & other & (mm(ind(in_col), product_b) > 0)
    right = in_col & other & (mm(ind(in_row), product_b, transposed=True) > 0)
    before = sub < lane
    group_r = group_of((lane // SLOTS) % plane)
    same_group = group_of((sub // SLOTS) % plane) == group_r
    across = left & ((lane // CHIP) != (dev // 2))
    left_at = jnp.where(across, mm(ind(across), ind(before)), -1.0)
    right_at = jnp.where(right, mm(ind(right), ind(before & same_group)), -1.0)

    zed = lax.broadcasted_iota(jnp.int32, (8, 1), 0) - 4
    cross = (mm(ind((dev_r // plane) == zed), ind(right)) > 0) & ((lane // in_plane) != zed)
    together = same_group & ((sub // in_plane) == (lane // in_plane))
    cross_at = jnp.where(cross, mm(ind(cross), ind(before & together)), -1.0)

    left_top = jnp.max(left_at) + 1.0
    same_y = ((lane // per_row) % 2) == (dev // cols) % 2
    right_tops = [jnp.max(jnp.where(same_y == one, right_at, -1.0)) + 1.0 for one in (True, False)]
    step = (lane // in_plane) ^ zed
    cross_tops = [jnp.max(jnp.where(step == m + 1, cross_at, -1.0)) + 1.0 for m in range(rows // 2 - 1)]
    size = jnp.int32(len(SIZES))
    for i, (lmost, rmost, zmost) in reversed(list(enumerate(SIZES))):
        fits = left_top <= lmost
        for top, most in zip(right_tops + cross_tops, rmost + zmost):
            fits = fits & (top <= most)
        size = jnp.where(fits, i, size)
    size_ref[0, 0] = size

    lanes = lax.broadcasted_iota(jnp.int32, (1, BS), 1)
    out_sub = lax.broadcasted_iota(jnp.int32, (8, 1), 0)

    def listed(out, first, at, value, most):
        for k in range(most):
            one = jnp.sum(jnp.where(at == k, value + 1.0, 0.0), axis=1, keepdims=True)
            out = jnp.where((out_sub >= 4) & (lanes == first + k), one, out)
        return out

    out = jnp.zeros((8, BS), jnp.float32)
    zed = out_sub - 4
    mine = (lane // SLOTS) == me
    place = (lane % SLOTS + jnp.where(mine, 0, SLOTS)).astype(jnp.float32)
    to_across = jnp.sum(jnp.where(dev == (me ^ 2), left_at, 0.0), axis=0, keepdims=True)
    out = listed(out, LEFTS, jnp.where((lane // CHIP) == me // 2, to_across, -1.0), place, LMOST)
    here = (lane // CHIP) == me // 2
    out = listed(out, CROSS, jnp.where(here, cross_at, -1.0), place, ZMOST)
    came = jnp.sum(jnp.where(zed == my_plane, cross_at, 0.0), axis=0, keepdims=True)
    away = CHIP + ZMOST * (((lane // in_plane) ^ my_plane) - 1)
    source = jnp.where((lane // in_plane) == my_plane, place, away.astype(jnp.float32) + came)
    partners = jnp.zeros((8, devices), jnp.bool_)
    for g, mask in enumerate(GIVES):
        partners = partners | ((zed == g) & (dev_r == my_plane * plane + (my_p ^ mask)))
    out = listed(out, GIVE, jnp.where(group_r == group_of(my_p), mm(ind(partners), bf(right_at)), -1.0), source, RMOST)

    left_me = jnp.sum(jnp.where(dev == me, left_at, 0.0), axis=0, keepdims=True)
    right_me = jnp.sum(jnp.where(dev == me, right_at, 0.0), axis=0, keepdims=True)
    held_a = jnp.where(here, place, CHIP + left_me)
    other_y = jnp.where((lane // per_row) % 2 == my_row % 2, 0.0, float(RMOST))
    held_b = as_column(jnp.where(mine, slot_r, CHIP + LMOST + other_y + right_me))
    my_product = product & (((sub // SLOTS) % cols) == my_col) & ((lane // per_row) == my_row)
    rank = mm(ind(lane < sub), ind(my_product))
    code = (hit - 1.0) * 256.0 + held_a * 64.0 + held_b + 1.0
    for k in range(2 * ACT):
        one = jnp.sum(jnp.where(my_product & (rank == k), code, 0.0), axis=0, keepdims=True)
        one = sum(one[:, i : i + BS] for i in range(0, n, BS))
        out = jnp.where(out_sub == k, one, out)
    table_ref[...] = out.astype(jnp.int32) - 1


def copy_listed(table_ref, row, first_lane, most, height, sources, to_ref):
    for k in range(most):
        at = table_ref[4 + row, first_lane + k]

        @pl.when(at >= 0)
        def _():
            for ref, first, count, stride, skip in sources:

                @pl.when((at >= first) & (at < first + count))
                def _():
                    here = pl.ds(pl.multiple_of((at - first) * stride + skip, height), height)
                    to_ref[k * height : (k + 1) * height, :] = ref[here, :]


def chip_halves(blocks_ref, other_ref):
    skip = piece_of(lax.axis_index(IN_PLANE)) * (BS // 2)
    return [(blocks_ref, 0, SLOTS, BS, skip), (other_ref, SLOTS, SLOTS, BS, skip)]


def cross_kernel(most, table_ref, blocks_ref, other_ref, *outs):
    for m, out_ref in enumerate(outs):
        row = lax.axis_index("z") ^ (m + 1)
        copy_listed(table_ref, row, CROSS, most[m], BS // 2, chip_halves(blocks_ref, other_ref), out_ref)


def left_kernel(most, table_ref, blocks_ref, other_ref, out_ref):
    sources = [(blocks_ref, 0, SLOTS, BS, 0), (other_ref, SLOTS, SLOTS, BS, 0)]
    copy_listed(table_ref, 0, LEFTS, most, BS, sources, out_ref)


def give_kernel(planes, zmost, most, table_ref, blocks_ref, other_ref, *refs):
    sources = chip_halves(blocks_ref, other_ref)
    sources += [(ref, CHIP + m * ZMOST, zmost[m], BS // 2, 0) for m, ref in enumerate(refs[: planes - 1])]
    for g, out_ref in enumerate(refs[planes - 1 :]):
        copy_listed(table_ref, g, GIVE, most[g // 2], BS // 2, sources, out_ref)


def add_products(entries, table_ref, left_ref, first_left, right_ref, first_right, out_ref, wanted):

    def block(held_ref, at):
        x = held_ref[pl.ds(pl.multiple_of(at * BS, BS), BS), :]
        high = bf(x)
        return high, bf(x - high.astype(jnp.float32))

    def one(i, k):
        code = table_ref[k, i]
        a, b = (code // 64) % 64, code % 64

        @pl.when((code >= 0) & wanted(a, b))
        def _():
            a_high, a_low = block(left_ref, a - first_left)
            b_high, b_low = block(right_ref, b - first_right)
            at = pl.ds(pl.multiple_of((code // 4096) * BS, BS), BS)
            out_ref[at, :] += mm(
                jnp.concatenate([a_high, a_high, a_low], axis=1), jnp.concatenate([b_high, b_low, b_high], axis=0)
            )

        if k + 1 < 2 * ACT:

            @pl.when(code >= 0)
            def _():
                one(i, k + 1)

    def entry(i, carry):
        one(i, 0)
        return carry

    lax.fori_loop(*entries, entry, 0)


def first_entry(cols):
    return (2 * lax.axis_index("z") + lax.axis_index("y")) * cols * SLOTS % BS


def chip_entries(cols, cores):
    for core in cores:
        first = first_entry(cols) + (lax.axis_index(COL) ^ core) * SLOTS
        yield core, (first, first + SLOTS)


def own_kernel(cols, table_ref, blocks_ref, other_ref, out_ref):
    out_ref[...] = jnp.zeros_like(out_ref)
    wanted = lambda a, b: b < SLOTS
    for core, entries in chip_entries(cols, (0, 1)):
        left_ref = (blocks_ref, other_ref)[core]
        add_products(entries, table_ref, left_ref, core * SLOTS, blocks_ref, 0, out_ref, wanted)


def across_kernel(cols, table_ref, left_ref, blocks_ref, start_ref, out_ref):
    out_ref[...] = start_ref[...]
    wanted = lambda a, b: b < SLOTS
    for _, entries in chip_entries(cols, (2, 3)):
        add_products(entries, table_ref, left_ref, CHIP, blocks_ref, 0, out_ref, wanted)


def product_kernel(cols, rmost, table_ref, blocks_ref, other_ref, start_ref, left_ref, *refs):
    right_refs, (out_ref, held_ref) = refs[: len(GIVES)], refs[len(GIVES) :]
    half = BS // 2
    mine = piece_of(lax.axis_index(IN_PLANE))
    for g, ref in enumerate(right_refs):
        for k in range(rmost[g // 2]):
            to = (g // 2 * RMOST + k) * BS + (mine ^ (g % 2)) * half
            held_ref[pl.ds(pl.multiple_of(to, half), half), :] = ref[k * half : (k + 1) * half, :]
    out_ref[...] = start_ref[...]
    wanted = lambda a, b: b >= SLOTS
    for core, entries in chip_entries(cols, range(4)):
        left, first = ((blocks_ref, 0), (other_ref, SLOTS), (left_ref, CHIP), (left_ref, CHIP))[core]
        add_products(entries, table_ref, left, first, held_ref, CHIP + LMOST, out_ref, wanted)


def swapped(x, axis, mask):
    return lax.ppermute(x, axis, [(i, i ^ mask) for i in range(lax.axis_size(axis))])


def packed_body(blocks, block_rows, block_cols):
    planes, cols = lax.axis_size("z"), lax.axis_size(COL)
    rows = 2 * planes
    plane = 2 * cols
    devices = rows * cols
    n = devices * SLOTS
    half = BS // 2
    flat = blocks.reshape(SLOTS * BS, BS)
    params = pltpu.CompilerParams(vmem_limit_bytes=VMEM_LIMIT)
    vmem = pl.BlockSpec(memory_space=pltpu.VMEM)
    smem = pl.BlockSpec(memory_space=pltpu.SMEM)

    long = pl.CostEstimate(flops=20_000_000_000, bytes_accessed=100_000, transcendentals=0)

    def floats(height):
        return jax.ShapeDtypeStruct((height, BS), jnp.float32)

    def ints(*shape):
        return jax.ShapeDtypeStruct(shape, jnp.int32)

    def call(kernel, name, ins, outs, scratch=(), specs=None, cost=None):
        return pl.pallas_call(
            kernel,
            out_shape=outs,
            in_specs=ins,
            out_specs=[vmem] * len(outs) if specs is None else specs,
            scratch_shapes=scratch,
            compiler_params=params,
            cost_estimate=cost,
            name=name,
        )

    idx = jnp.concatenate([block_rows[0], block_cols[0]])
    idx = jnp.concatenate([idx, swapped(idx, "core", 1)])
    idx = jnp.broadcast_to(idx[None], (devices // 2, 4, SLOTS))
    idx, source = lax.optimization_barrier((idx, flat))
    other = swapped(source, IN_PLANE, 1)
    idx = lax.all_to_all(idx, ("z", "y", "x"), 0, 0)
    table, size = call(
        lambda *refs: plan_kernel(rows, cols, *refs),
        "plan",
        [vmem],
        [ints(8, BS), ints(1, 1)],
        specs=[vmem, smem],
        cost=long,
    )(idx)

    def packed(lmost, rmost, zmost):
        crossing = call(
            lambda *refs: cross_kernel(zmost, *refs),
            "cross",
            [smem] + [vmem] * 2,
            [floats(most * half) for most in zmost],
        )(table, flat, other)
        later, *crossing = lax.optimization_barrier((table, *crossing))
        crossed = [swapped(crossing[m], "z", m + 1) for m in reversed(range(planes - 1))][::-1]
        own = call(lambda *refs: own_kernel(cols, *refs), "own", [smem] + [vmem] * 2, [floats(SLOTS * BS)])(
            later, flat, other
        )
        leaving = call(
            lambda *refs: left_kernel(lmost, *refs), "left", [smem] + [vmem] * 2, [floats(lmost * BS)]
        )(later, flat, other)
        later, own, *leaving = lax.optimization_barrier((later, own[0], *leaving))
        lefts = swapped(leaving[0], IN_PLANE, 2)
        giving = call(
            lambda *refs: give_kernel(planes, zmost, rmost, *refs),
            "give",
            [smem] + [vmem] * (2 + planes - 1),
            [floats(rmost[g // 2] * half) for g in range(len(GIVES))],
            cost=long,
        )(later, flat, other, *crossed)
        rights = [swapped(x, IN_PLANE, mask) if mask else x for x, mask in reversed(list(zip(giving, GIVES)))][::-1]
        own = call(
            lambda *refs: across_kernel(cols, *refs), "across", [smem] + [vmem] * 3, [floats(SLOTS * BS)]
        )(later, lefts, flat, own)
        out = call(
            lambda *refs: product_kernel(cols, rmost, *refs),
            "products",
            [smem] + [vmem] * (4 + len(GIVES)),
            [floats(SLOTS * BS)],
            [pltpu.VMEM(((RMOST + rmost[1]) * BS, BS), jnp.float32)],
        )(later, flat, other, *own, lefts, *rights)
        return out[0].reshape(blocks.shape)

    branches = [lambda most=most: packed(*most) for most in SIZES]
    return lax.switch(size[0, 0], branches + [lambda: whole_tiles(blocks, block_rows, block_cols)])


def solution(mesh):
    rows, cols = mesh.devices.shape
    if cols == SECTIONS and rows == 2 * SECTIONS:
        body, row, col = packed_body, ("z", "y"), COL
        mesh = jax.sharding.Mesh(mesh.devices.reshape(rows // 2, 2, cols // 2, 2), ("z", "y", "x", "core"))
    else:
        body, row, col = general_body, "row", "col"
    return jax.shard_map(
        body,
        mesh=mesh,
        in_specs=(P(row, col, None, None, None), P(row, col, None), P(row, col, None)),
        out_specs=P(row, col, None, None, None),
        check_vma=False,
    )
```

```python
import jax
import jax.numpy as jnp
from jax import lax
from jax.experimental import pallas as pl
from jax.experimental.pallas import tpu as pltpu
from jax.sharding import PartitionSpec as P

NBLK = 512
ACT = 2
SECTIONS = 4
BS = 128
SLOTS = 8
SIZES = (
    (4, (3, 2), (4, 2, 2)),
    (4, (3, 2), (4, 2, 3)),
    (4, (3, 2), (4, 3, 2)),
    (4, (3, 3), (4, 3, 3)),
    (5, (4, 4), (5, 4, 4)),
    (8, (8, 8), (8, 8, 8)),
)
LMOST, RMOST, ZMOST = 8, 8, 8
LEFTS, CROSS, GIVE = 0, 16, 32
VMEM_LIMIT = 32 * 1024 * 1024


def from_root(x, axis, root):
    mine = lax.axis_index(axis) == root
    return lax.psum(jnp.where(mine, x, jnp.zeros_like(x)), axis)


def from_partner(x, axis, bit):
    return lax.ppermute(x, axis, [(i, i ^ 1 << bit) for i in range(lax.axis_size(axis))])


def shifted(value, axis, steps):
    count = lax.axis_size(axis)
    pairs = [(source, (source + steps) % count) for source in range(count)]
    return lax.ppermute(value, axis, pairs)


def section_product(panel, pair, out_rows, out_cols, depth):
    panel_vals, panel_rows, panel_cols = panel
    pair_vals, pair_inner, pair_cols = pair
    panel_iota = jnp.arange(panel_rows.shape[0], dtype=jnp.int32)
    pair_iota = jnp.arange(pair_inner.shape[0], dtype=jnp.int32)
    depth_iota = jnp.arange(depth, dtype=jnp.int32)
    panel_live = panel_rows >= 0
    earlier = (
        (panel_rows[None, :] == panel_rows[:, None])
        & panel_live[None, :]
        & (panel_iota[None, :] < panel_iota[:, None])
    )
    within = jnp.sum(earlier.astype(jnp.int32), axis=1)
    picked = (panel_rows[None, None, :] == out_rows[:, None, None]) & (
        within[None, None, :] == depth_iota[None, :, None]
    )
    picked = picked & panel_live[None, None, :] & (out_rows >= 0)[:, None, None]
    picked_int = picked.astype(jnp.int32)
    panel_slot = jnp.sum(picked_int * panel_iota[None, None, :], axis=2)
    found = jnp.sum(picked_int, axis=2) > 0
    inner = jnp.sum(picked_int * panel_cols[None, None, :], axis=2)
    matched = (pair_inner[None, None, :] == inner[:, :, None]) & (
        pair_cols[None, None, :] == out_cols[:, None, None]
    )
    matched = matched & (pair_inner >= 0)[None, None, :] & found[:, :, None]
    matched_int = matched.astype(jnp.int32)
    pair_slot = jnp.sum(matched_int * pair_iota[None, None, :], axis=2)
    weight = (jnp.sum(matched_int, axis=2) > 0).astype(jnp.float32)
    left = panel_vals[panel_slot] * weight[:, :, None, None]
    right = pair_vals[pair_slot]
    return jnp.einsum(
        "tqij,tqjk->tik",
        left,
        right,
        precision=lax.Precision.HIGHEST,
        preferred_element_type=jnp.float32,
    )


def make_pair(first, second, row_span):
    inner = jnp.concatenate([first[1], jnp.where(second[1] >= 0, second[1] + row_span, -1)])
    return (jnp.concatenate([first[0], second[0]]), inner, jnp.concatenate([first[2], second[2]]))


def order_pair(mine, other, is_even, row_span):
    first = tuple((jnp.where(is_even, one, two) for one, two in zip(mine, other)))
    second = tuple((jnp.where(is_even, two, one) for one, two in zip(mine, other)))
    return make_pair(first, second, row_span)


def fetch_panel(tile, row_index, col_count, section):
    root = (row_index // 2 + section) % col_count
    return tuple(from_root(one, "col", root) for one in tile)


def general_body(blocks, block_rows, block_cols):
    tile = (blocks[0, 0], block_rows[0, 0], block_cols[0, 0])
    row_count = lax.axis_size("row")
    col_count = lax.axis_size("col")
    row_span = NBLK // row_count
    row_index = lax.axis_index("row")
    is_even = row_index % 2 == 0
    depth = 2 * ACT
    total = jnp.zeros(blocks.shape[2:], jnp.float32)
    partner = from_partner((tile[0], tile[1], tile[2]), "row", 0)
    current = order_pair(tile, partner, is_even, row_span)
    for section in range(SECTIONS):
        panel = fetch_panel(tile, row_index, col_count, section)
        if section > 0:
            current = shifted((current[0], current[1], current[2]), "row", -2)
        total = total + section_product(panel, current, tile[1], tile[2], depth)
    return total[None, None]


def everything(x, axis):
    return lax.all_to_all(jnp.broadcast_to(x[None], (lax.axis_size(axis),) + x.shape), axis, 0, 0)


def whole_tiles(blocks, block_rows, block_cols):
    tile = (blocks[0, 0], block_rows[0, 0], block_cols[0, 0])
    row_span = NBLK // lax.axis_size(("z", "y"))
    col_count = lax.axis_size("col")
    row_index = lax.axis_index(("z", "y"))
    panels = tuple(everything(one, "col") for one in tile)
    column = tuple(everything(one, ("z", "y")) for one in tile)

    def section(step, total):
        root = (row_index // 2 + step) % col_count
        take = lambda arrays, at: tuple(lax.dynamic_index_in_dim(a, at, 0, False) for a in arrays)
        pair = make_pair(take(column, 2 * root), take(column, 2 * root + 1), row_span)
        return total + section_product(take(panels, root), pair, tile[1], tile[2], 2 * ACT)

    total = lax.fori_loop(0, SECTIONS, section, jnp.zeros(blocks.shape[2:], jnp.float32))
    return total[None, None]


CHIP = 2 * SLOTS
GIVES = (0, 1, 4, 5)


def piece_of(p):
    return p % 2


def group_of(p):
    return p // 2


def bf(x):
    return x.astype(jnp.bfloat16)


def ind(x):
    return bf(jnp.where(x, 1.0, 0.0))


def mm(a, b, transposed=False):
    dims = (((1,), (1 if transposed else 0,)), ((), ()))
    return lax.dot_general(a, b, dims, preferred_element_type=jnp.float32)


def plan_kernel(rows, cols, idx_ref, table_ref, size_ref):
    devices = rows * cols
    plane = 2 * cols
    n = devices * SLOTS
    in_plane = plane * SLOTS
    rb = NBLK // rows
    cb = NBLK // cols
    per_row = cols * SLOTS
    my_plane, my_p = lax.axis_index("z"), lax.axis_index(("y", "col"))
    my_row = 2 * my_plane + lax.axis_index("y")
    my_col = lax.axis_index("col")
    me = my_row * cols + my_col

    sub = lax.broadcasted_iota(jnp.int32, (n, 1), 0)
    lane = lax.broadcasted_iota(jnp.int32, (1, n), 1)
    dev = lax.broadcasted_iota(jnp.int32, (devices, 1), 0)
    dev_r = lax.broadcasted_iota(jnp.int32, (1, devices), 1)
    slot = lax.broadcasted_iota(jnp.int32, (1, SLOTS), 1)
    diagonal = sub == lane

    def as_row(column):
        return jnp.sum(jnp.where(diagonal, column, 0.0), axis=0, keepdims=True)

    def as_column(row):
        return jnp.sum(jnp.where(diagonal, row, 0.0), axis=1, keepdims=True)

    repeat = ind((sub // SLOTS) == dev_r)

    def column(k):
        values = mm(repeat, bf(idx_ref[:, k, :].astype(jnp.float32)))
        return jnp.sum(jnp.where((sub % SLOTS) == slot, values, 0.0), axis=1, keepdims=True)

    up = ((sub // per_row) * rb).astype(jnp.float32)
    along = (((sub // SLOTS) % cols) * cb).astype(jnp.float32)
    row_c, col_c = column(0), column(1)
    row_c = jnp.where(row_c >= 0, row_c + up, -1.0)
    col_c = jnp.where(col_c >= 0, col_c + along, -2.0)
    row_r, col_r = as_row(row_c), as_row(col_c)

    slot_r = (lane % SLOTS).astype(jnp.float32)
    hit = mm(bf(jnp.where(col_c == col_r, 1.0 + 16.0 * slot_r, 0.0)), ind(row_c == row_r))
    product = (row_c == col_r) & (hit > 0)
    product_b = ind(product)

    in_row = (lane // per_row) == (dev // cols)
    in_col = ((lane // SLOTS) % cols) == (dev % cols)
    other = (lane // SLOTS) != dev
    left = in_row & other & (mm(ind(in_col), product_b) > 0)
    right = in_col & other & (mm(ind(in_row), product_b, transposed=True) > 0)
    before = sub < lane
    group_r = group_of((lane // SLOTS) % plane)
    same_group = group_of((sub // SLOTS) % plane) == group_r
    across = left & ((lane // CHIP) != (dev // 2))
    left_at = jnp.where(across, mm(ind(across), ind(before)), -1.0)
    right_at = jnp.where(right, mm(ind(right), ind(before & same_group)), -1.0)

    zed = lax.broadcasted_iota(jnp.int32, (8, 1), 0) - 4
    cross = (mm(ind((dev_r // plane) == zed), ind(right)) > 0) & ((lane // in_plane) != zed)
    together = same_group & ((sub // in_plane) == (lane // in_plane))
    cross_at = jnp.where(cross, mm(ind(cross), ind(before & together)), -1.0)

    left_top = jnp.max(left_at) + 1.0
    same_y = ((lane // per_row) % 2) == (dev // cols) % 2
    right_tops = [jnp.max(jnp.where(same_y == one, right_at, -1.0)) + 1.0 for one in (True, False)]
    step = (lane // in_plane) ^ zed
    cross_tops = [jnp.max(jnp.where(step == m + 1, cross_at, -1.0)) + 1.0 for m in range(rows // 2 - 1)]
    size = jnp.int32(len(SIZES))
    for i, (lmost, rmost, zmost) in reversed(list(enumerate(SIZES))):
        fits = left_top <= lmost
        for top, most in zip(right_tops + cross_tops, rmost + zmost):
            fits = fits & (top <= most)
        size = jnp.where(fits, i, size)
    size_ref[0, 0] = size

    lanes = lax.broadcasted_iota(jnp.int32, (1, BS), 1)
    out_sub = lax.broadcasted_iota(jnp.int32, (8, 1), 0)

    def listed(out, first, at, value, most):
        for k in range(most):
            one = jnp.sum(jnp.where(at == k, value + 1.0, 0.0), axis=1, keepdims=True)
            out = jnp.where((out_sub >= 4) & (lanes == first + k), one, out)
        return out

    out = jnp.zeros((8, BS), jnp.float32)
    zed = out_sub - 4
    mine = (lane // SLOTS) == me
    place = (lane % SLOTS + jnp.where(mine, 0, SLOTS)).astype(jnp.float32)
    to_across = jnp.sum(jnp.where(dev == (me ^ 2), left_at, 0.0), axis=0, keepdims=True)
    out = listed(out, LEFTS, jnp.where((lane // CHIP) == me // 2, to_across, -1.0), place, LMOST)
    here = (lane // CHIP) == me // 2
    out = listed(out, CROSS, jnp.where(here, cross_at, -1.0), place, ZMOST)
    came = jnp.sum(jnp.where(zed == my_plane, cross_at, 0.0), axis=0, keepdims=True)
    away = CHIP + ZMOST * (((lane // in_plane) ^ my_plane) - 1)
    source = jnp.where((lane // in_plane) == my_plane, place, away.astype(jnp.float32) + came)
    partners = jnp.zeros((8, devices), jnp.bool_)
    for g, mask in enumerate(GIVES):
        partners = partners | ((zed == g) & (dev_r == my_plane * plane + (my_p ^ mask)))
    out = listed(out, GIVE, jnp.where(group_r == group_of(my_p), mm(ind(partners), bf(right_at)), -1.0), source, RMOST)

    left_me = jnp.sum(jnp.where(dev == me, left_at, 0.0), axis=0, keepdims=True)
    right_me = jnp.sum(jnp.where(dev == me, right_at, 0.0), axis=0, keepdims=True)
    held_a = jnp.where(here, place, CHIP + left_me)
    other_y = jnp.where((lane // per_row) % 2 == my_row % 2, 0.0, float(RMOST))
    held_b = as_column(jnp.where(mine, slot_r, CHIP + LMOST + other_y + right_me))
    my_product = product & (((sub // SLOTS) % cols) == my_col) & ((lane // per_row) == my_row)
    rank = mm(ind(lane < sub), ind(my_product))
    code = (hit - 1.0) * 256.0 + held_a * 64.0 + held_b + 1.0
    for k in range(2 * ACT):
        one = jnp.sum(jnp.where(my_product & (rank == k), code, 0.0), axis=0, keepdims=True)
        one = sum(one[:, i : i + BS] for i in range(0, n, BS))
        out = jnp.where(out_sub == k, one, out)
    table_ref[...] = out.astype(jnp.int32) - 1


def copy_listed(table_ref, row, first_lane, most, height, sources, to_ref):
    for k in range(most):
        at = table_ref[4 + row, first_lane + k]

        @pl.when(at >= 0)
        def _():
            for ref, first, count, stride, skip in sources:

                @pl.when((at >= first) & (at < first + count))
                def _():
                    here = pl.ds(pl.multiple_of((at - first) * stride + skip, height), height)
                    to_ref[k * height : (k + 1) * height, :] = ref[here, :]


def chip_halves(blocks_ref, other_ref):
    skip = piece_of(lax.axis_index(("y", "col"))) * (BS // 2)
    return [(blocks_ref, 0, SLOTS, BS, skip), (other_ref, SLOTS, SLOTS, BS, skip)]


def cross_kernel(most, table_ref, blocks_ref, other_ref, *outs):
    for m, out_ref in enumerate(outs):
        row = lax.axis_index("z") ^ (m + 1)
        copy_listed(table_ref, row, CROSS, most[m], BS // 2, chip_halves(blocks_ref, other_ref), out_ref)


def left_kernel(most, table_ref, blocks_ref, other_ref, out_ref):
    sources = [(blocks_ref, 0, SLOTS, BS, 0), (other_ref, SLOTS, SLOTS, BS, 0)]
    copy_listed(table_ref, 0, LEFTS, most, BS, sources, out_ref)


def give_kernel(planes, zmost, most, table_ref, blocks_ref, other_ref, *refs):
    sources = chip_halves(blocks_ref, other_ref)
    sources += [(ref, CHIP + m * ZMOST, zmost[m], BS // 2, 0) for m, ref in enumerate(refs[: planes - 1])]
    for g, out_ref in enumerate(refs[planes - 1 :]):
        copy_listed(table_ref, g, GIVE, most[g // 2], BS // 2, sources, out_ref)


def add_products(entries, table_ref, left_ref, first_left, right_ref, first_right, out_ref, wanted):

    def block(held_ref, at):
        x = held_ref[pl.ds(pl.multiple_of(at * BS, BS), BS), :]
        high = bf(x)
        return high, bf(x - high.astype(jnp.float32))

    def one(i, k):
        code = table_ref[k, i]
        a, b = (code // 64) % 64, code % 64

        @pl.when((code >= 0) & wanted(a, b))
        def _():
            a_high, a_low = block(left_ref, a - first_left)
            b_high, b_low = block(right_ref, b - first_right)
            at = pl.ds(pl.multiple_of((code // 4096) * BS, BS), BS)
            out_ref[at, :] += mm(
                jnp.concatenate([a_high, a_high, a_low], axis=1), jnp.concatenate([b_high, b_low, b_high], axis=0)
            )

        if k + 1 < 2 * ACT:

            @pl.when(code >= 0)
            def _():
                one(i, k + 1)

    def entry(i, carry):
        one(i, 0)
        return carry

    lax.fori_loop(*entries, entry, 0)


def first_entry(cols):
    return (2 * lax.axis_index("z") + lax.axis_index("y")) * cols * SLOTS % BS


def chip_entries(cols, cores):
    for core in cores:
        first = first_entry(cols) + (lax.axis_index("col") ^ core) * SLOTS
        yield core, (first, first + SLOTS)


def own_kernel(cols, table_ref, blocks_ref, other_ref, out_ref):
    out_ref[...] = jnp.zeros_like(out_ref)
    wanted = lambda a, b: b < SLOTS
    for core, entries in chip_entries(cols, (0, 1)):
        left_ref = (blocks_ref, other_ref)[core]
        add_products(entries, table_ref, left_ref, core * SLOTS, blocks_ref, 0, out_ref, wanted)


def across_kernel(cols, table_ref, left_ref, blocks_ref, start_ref, out_ref):
    out_ref[...] = start_ref[...]
    wanted = lambda a, b: b < SLOTS
    for _, entries in chip_entries(cols, (2, 3)):
        add_products(entries, table_ref, left_ref, CHIP, blocks_ref, 0, out_ref, wanted)


def product_kernel(cols, rmost, table_ref, blocks_ref, other_ref, start_ref, left_ref, *refs):
    right_refs, (out_ref, held_ref) = refs[: len(GIVES)], refs[len(GIVES) :]
    half = BS // 2
    mine = piece_of(lax.axis_index(("y", "col")))
    for g, ref in enumerate(right_refs):
        for k in range(rmost[g // 2]):
            to = (g // 2 * RMOST + k) * BS + (mine ^ (g % 2)) * half
            held_ref[pl.ds(pl.multiple_of(to, half), half), :] = ref[k * half : (k + 1) * half, :]
    out_ref[...] = start_ref[...]
    wanted = lambda a, b: b >= SLOTS
    for core, entries in chip_entries(cols, range(4)):
        left, first = ((blocks_ref, 0), (other_ref, SLOTS), (left_ref, CHIP), (left_ref, CHIP))[core]
        add_products(entries, table_ref, left, first, held_ref, CHIP + LMOST, out_ref, wanted)


def swapped(x, axis, mask):
    return lax.ppermute(x, axis, [(i, i ^ mask) for i in range(lax.axis_size(axis))])


def packed_body(blocks, block_rows, block_cols):
    planes, cols = lax.axis_size("z"), lax.axis_size("col")
    rows = 2 * planes
    plane = 2 * cols
    devices = rows * cols
    n = devices * SLOTS
    half = BS // 2
    in_plane = ("y", "col")
    flat = blocks.reshape(SLOTS * BS, BS)
    params = pltpu.CompilerParams(vmem_limit_bytes=VMEM_LIMIT)
    vmem = pl.BlockSpec(memory_space=pltpu.VMEM)
    smem = pl.BlockSpec(memory_space=pltpu.SMEM)

    long = pl.CostEstimate(flops=20_000_000_000, bytes_accessed=100_000, transcendentals=0)

    def floats(height):
        return jax.ShapeDtypeStruct((height, BS), jnp.float32)

    def ints(*shape):
        return jax.ShapeDtypeStruct(shape, jnp.int32)

    def call(kernel, name, ins, outs, scratch=(), specs=None, cost=None):
        return pl.pallas_call(
            kernel,
            out_shape=outs,
            in_specs=ins,
            out_specs=[vmem] * len(outs) if specs is None else specs,
            scratch_shapes=scratch,
            compiler_params=params,
            cost_estimate=cost,
            name=name,
        )

    idx = jnp.concatenate([block_rows[0], block_cols[0]])
    idx = jnp.broadcast_to(idx[None], (devices, 2, SLOTS))
    idx, source = lax.optimization_barrier((idx, flat))
    other = swapped(source, in_plane, 1)
    idx = lax.all_to_all(idx, ("z", "y", "col"), 0, 0)
    table, size = call(
        lambda *refs: plan_kernel(rows, cols, *refs),
        "plan",
        [vmem],
        [ints(8, BS), ints(1, 1)],
        specs=[vmem, smem],
        cost=long,
    )(idx)

    def packed(lmost, rmost, zmost):
        crossing = call(
            lambda *refs: cross_kernel(zmost, *refs),
            "cross",
            [smem] + [vmem] * 2,
            [floats(most * half) for most in zmost],
        )(table, flat, other)
        later, *crossing = lax.optimization_barrier((table, *crossing))
        crossed = [swapped(crossing[m], "z", m + 1) for m in reversed(range(planes - 1))][::-1]
        own = call(lambda *refs: own_kernel(cols, *refs), "own", [smem] + [vmem] * 2, [floats(SLOTS * BS)])(
            later, flat, other
        )
        leaving = call(
            lambda *refs: left_kernel(lmost, *refs), "left", [smem] + [vmem] * 2, [floats(lmost * BS)]
        )(later, flat, other)
        later, own, *leaving = lax.optimization_barrier((later, own[0], *leaving))
        lefts = swapped(leaving[0], in_plane, 2)
        giving = call(
            lambda *refs: give_kernel(planes, zmost, rmost, *refs),
            "give",
            [smem] + [vmem] * (2 + planes - 1),
            [floats(rmost[g // 2] * half) for g in range(len(GIVES))],
            cost=long,
        )(later, flat, other, *crossed)
        rights = [swapped(x, in_plane, mask) if mask else x for x, mask in reversed(list(zip(giving, GIVES)))][::-1]
        own = call(
            lambda *refs: across_kernel(cols, *refs), "across", [smem] + [vmem] * 3, [floats(SLOTS * BS)]
        )(later, lefts, flat, own)
        out = call(
            lambda *refs: product_kernel(cols, rmost, *refs),
            "products",
            [smem] + [vmem] * (4 + len(GIVES)),
            [floats(SLOTS * BS)],
            [pltpu.VMEM(((RMOST + rmost[1]) * BS, BS), jnp.float32)],
        )(later, flat, other, *own, lefts, *rights)
        return out[0].reshape(blocks.shape)

    branches = [lambda most=most: packed(*most) for most in SIZES]
    return lax.switch(size[0, 0], branches + [lambda: whole_tiles(blocks, block_rows, block_cols)])


def solution(mesh):
    rows, cols = mesh.devices.shape
    if cols == SECTIONS and rows == 2 * SECTIONS:
        body, row = packed_body, ("z", "y")
        mesh = jax.sharding.Mesh(mesh.devices.reshape(rows // 2, 2, cols), ("z", "y", "col"))
    else:
        body, row = general_body, "row"
    return jax.shard_map(
        body,
        mesh=mesh,
        in_specs=(P(row, "col", None, None, None), P(row, "col", None), P(row, "col", None)),
        out_specs=P(row, "col", None, None, None),
        check_vma=False,
    )
```

```python
import jax
import jax.numpy as jnp
from jax import lax
from jax.experimental import pallas as pl
from jax.experimental.pallas import tpu as pltpu
from jax.sharding import PartitionSpec as P

NBLK = 512
ACT = 2
SECTIONS = 4
BS = 128
SLOTS = 8
SIZES = (
    (4, (3, 2), (4, 2, 2)),
    (4, (3, 2), (4, 2, 3)),
    (4, (3, 2), (4, 3, 2)),
    (4, (3, 3), (4, 3, 3)),
    (5, (4, 4), (5, 4, 4)),
    (8, (8, 8), (8, 8, 8)),
)
LMOST, RMOST, ZMOST = 8, 8, 8
LEFTS, CROSS, GIVE = 0, 16, 32
VMEM_LIMIT = 32 * 1024 * 1024


def from_root(x, axis, root):
    mine = lax.axis_index(axis) == root
    return lax.psum(jnp.where(mine, x, jnp.zeros_like(x)), axis)


def from_partner(x, axis, bit):
    return lax.ppermute(x, axis, [(i, i ^ 1 << bit) for i in range(lax.axis_size(axis))])


def shifted(value, axis, steps):
    count = lax.axis_size(axis)
    pairs = [(source, (source + steps) % count) for source in range(count)]
    return lax.ppermute(value, axis, pairs)


def section_product(panel, pair, out_rows, out_cols, depth):
    panel_vals, panel_rows, panel_cols = panel
    pair_vals, pair_inner, pair_cols = pair
    panel_iota = jnp.arange(panel_rows.shape[0], dtype=jnp.int32)
    pair_iota = jnp.arange(pair_inner.shape[0], dtype=jnp.int32)
    depth_iota = jnp.arange(depth, dtype=jnp.int32)
    panel_live = panel_rows >= 0
    earlier = (
        (panel_rows[None, :] == panel_rows[:, None])
        & panel_live[None, :]
        & (panel_iota[None, :] < panel_iota[:, None])
    )
    within = jnp.sum(earlier.astype(jnp.int32), axis=1)
    picked = (panel_rows[None, None, :] == out_rows[:, None, None]) & (
        within[None, None, :] == depth_iota[None, :, None]
    )
    picked = picked & panel_live[None, None, :] & (out_rows >= 0)[:, None, None]
    picked_int = picked.astype(jnp.int32)
    panel_slot = jnp.sum(picked_int * panel_iota[None, None, :], axis=2)
    found = jnp.sum(picked_int, axis=2) > 0
    inner = jnp.sum(picked_int * panel_cols[None, None, :], axis=2)
    matched = (pair_inner[None, None, :] == inner[:, :, None]) & (
        pair_cols[None, None, :] == out_cols[:, None, None]
    )
    matched = matched & (pair_inner >= 0)[None, None, :] & found[:, :, None]
    matched_int = matched.astype(jnp.int32)
    pair_slot = jnp.sum(matched_int * pair_iota[None, None, :], axis=2)
    weight = (jnp.sum(matched_int, axis=2) > 0).astype(jnp.float32)
    left = panel_vals[panel_slot] * weight[:, :, None, None]
    right = pair_vals[pair_slot]
    return jnp.einsum(
        "tqij,tqjk->tik",
        left,
        right,
        precision=lax.Precision.HIGHEST,
        preferred_element_type=jnp.float32,
    )


def make_pair(first, second, row_span):
    inner = jnp.concatenate([first[1], jnp.where(second[1] >= 0, second[1] + row_span, -1)])
    return (jnp.concatenate([first[0], second[0]]), inner, jnp.concatenate([first[2], second[2]]))


def order_pair(mine, other, is_even, row_span):
    first = tuple((jnp.where(is_even, one, two) for one, two in zip(mine, other)))
    second = tuple((jnp.where(is_even, two, one) for one, two in zip(mine, other)))
    return make_pair(first, second, row_span)


def fetch_panel(tile, row_index, col_count, section):
    root = (row_index // 2 + section) % col_count
    return tuple(from_root(one, "col", root) for one in tile)


def general_body(blocks, block_rows, block_cols):
    tile = (blocks[0, 0], block_rows[0, 0], block_cols[0, 0])
    row_count = lax.axis_size("row")
    col_count = lax.axis_size("col")
    row_span = NBLK // row_count
    row_index = lax.axis_index("row")
    is_even = row_index % 2 == 0
    depth = 2 * ACT
    total = jnp.zeros(blocks.shape[2:], jnp.float32)
    partner = from_partner((tile[0], tile[1], tile[2]), "row", 0)
    current = order_pair(tile, partner, is_even, row_span)
    for section in range(SECTIONS):
        panel = fetch_panel(tile, row_index, col_count, section)
        if section > 0:
            current = shifted((current[0], current[1], current[2]), "row", -2)
        total = total + section_product(panel, current, tile[1], tile[2], depth)
    return total[None, None]


def everything(x, axis):
    return lax.all_to_all(jnp.broadcast_to(x[None], (lax.axis_size(axis),) + x.shape), axis, 0, 0)


def whole_tiles(blocks, block_rows, block_cols):
    tile = (blocks[0, 0], block_rows[0, 0], block_cols[0, 0])
    row_span = NBLK // lax.axis_size(("z", "y"))
    col_count = lax.axis_size("col")
    row_index = lax.axis_index(("z", "y"))
    panels = tuple(everything(one, "col") for one in tile)
    column = tuple(everything(one, ("z", "y")) for one in tile)

    def section(step, total):
        root = (row_index // 2 + step) % col_count
        take = lambda arrays, at: tuple(lax.dynamic_index_in_dim(a, at, 0, False) for a in arrays)
        pair = make_pair(take(column, 2 * root), take(column, 2 * root + 1), row_span)
        return total + section_product(take(panels, root), pair, tile[1], tile[2], 2 * ACT)

    total = lax.fori_loop(0, SECTIONS, section, jnp.zeros(blocks.shape[2:], jnp.float32))
    return total[None, None]


CHIP = 2 * SLOTS
GIVES = (0, 1, 4, 5)


def piece_of(p):
    return p % 2


def group_of(p):
    return p // 2


def bf(x):
    return x.astype(jnp.bfloat16)


def ind(x):
    return bf(jnp.where(x, 1.0, 0.0))


def mm(a, b, transposed=False):
    dims = (((1,), (1 if transposed else 0,)), ((), ()))
    return lax.dot_general(a, b, dims, preferred_element_type=jnp.float32)


def plan_kernel(rows, cols, idx_ref, table_ref, size_ref):
    devices = rows * cols
    plane = 2 * cols
    n = devices * SLOTS
    in_plane = plane * SLOTS
    rb = NBLK // rows
    cb = NBLK // cols
    per_row = cols * SLOTS
    my_plane, my_p = lax.axis_index("z"), lax.axis_index(("y", "col"))
    my_row = 2 * my_plane + lax.axis_index("y")
    my_col = lax.axis_index("col")
    me = my_row * cols + my_col

    sub = lax.broadcasted_iota(jnp.int32, (n, 1), 0)
    lane = lax.broadcasted_iota(jnp.int32, (1, n), 1)
    dev = lax.broadcasted_iota(jnp.int32, (devices, 1), 0)
    dev_r = lax.broadcasted_iota(jnp.int32, (1, devices), 1)
    slot = lax.broadcasted_iota(jnp.int32, (1, SLOTS), 1)
    diagonal = sub == lane

    def as_row(column):
        return jnp.sum(jnp.where(diagonal, column, 0.0), axis=0, keepdims=True)

    def as_column(row):
        return jnp.sum(jnp.where(diagonal, row, 0.0), axis=1, keepdims=True)

    repeat = ind((sub // SLOTS) == dev_r)

    def column(k):
        values = mm(repeat, bf(idx_ref[:, k, :].astype(jnp.float32)))
        return jnp.sum(jnp.where((sub % SLOTS) == slot, values, 0.0), axis=1, keepdims=True)

    up = ((sub // per_row) * rb).astype(jnp.float32)
    along = (((sub // SLOTS) % cols) * cb).astype(jnp.float32)
    row_c, col_c = column(0), column(1)
    row_c = jnp.where(row_c >= 0, row_c + up, -1.0)
    col_c = jnp.where(col_c >= 0, col_c + along, -2.0)
    row_r, col_r = as_row(row_c), as_row(col_c)

    slot_r = (lane % SLOTS).astype(jnp.float32)
    hit = mm(bf(jnp.where(col_c == col_r, 1.0 + 16.0 * slot_r, 0.0)), ind(row_c == row_r))
    product = (row_c == col_r) & (hit > 0)
    product_b = ind(product)

    in_row = (lane // per_row) == (dev // cols)
    in_col = ((lane // SLOTS) % cols) == (dev % cols)
    other = (lane // SLOTS) != dev
    left = in_row & other & (mm(ind(in_col), product_b) > 0)
    right = in_col & other & (mm(ind(in_row), product_b, transposed=True) > 0)
    before = sub < lane
    group_r = group_of((lane // SLOTS) % plane)
    same_group = group_of((sub // SLOTS) % plane) == group_r
    across = left & ((lane // CHIP) != (dev // 2))
    left_at = jnp.where(across, mm(ind(across), ind(before)), -1.0)
    right_at = jnp.where(right, mm(ind(right), ind(before & same_group)), -1.0)

    zed = lax.broadcasted_iota(jnp.int32, (8, 1), 0) - 4
    cross = (mm(ind((dev_r // plane) == zed), ind(right)) > 0) & ((lane // in_plane) != zed)
    together = same_group & ((sub // in_plane) == (lane // in_plane))
    cross_at = jnp.where(cross, mm(ind(cross), ind(before & together)), -1.0)

    left_top = jnp.max(left_at) + 1.0
    same_y = ((lane // per_row) % 2) == (dev // cols) % 2
    right_tops = [jnp.max(jnp.where(same_y == one, right_at, -1.0)) + 1.0 for one in (True, False)]
    step = (lane // in_plane) ^ zed
    cross_tops = [jnp.max(jnp.where(step == m + 1, cross_at, -1.0)) + 1.0 for m in range(rows // 2 - 1)]
    size = jnp.int32(len(SIZES))
    for i, (lmost, rmost, zmost) in reversed(list(enumerate(SIZES))):
        fits = left_top <= lmost
        for top, most in zip(right_tops + cross_tops, rmost + zmost):
            fits = fits & (top <= most)
        size = jnp.where(fits, i, size)
    size_ref[0, 0] = size

    lanes = lax.broadcasted_iota(jnp.int32, (1, BS), 1)
    out_sub = lax.broadcasted_iota(jnp.int32, (8, 1), 0)

    def listed(out, first, at, value, most):
        for k in range(most):
            one = jnp.sum(jnp.where(at == k, value + 1.0, 0.0), axis=1, keepdims=True)
            out = jnp.where((out_sub >= 4) & (lanes == first + k), one, out)
        return out

    out = jnp.zeros((8, BS), jnp.float32)
    zed = out_sub - 4
    mine = (lane // SLOTS) == me
    place = (lane % SLOTS + jnp.where(mine, 0, SLOTS)).astype(jnp.float32)
    to_across = jnp.sum(jnp.where(dev == (me ^ 2), left_at, 0.0), axis=0, keepdims=True)
    out = listed(out, LEFTS, jnp.where((lane // CHIP) == me // 2, to_across, -1.0), place, LMOST)
    here = (lane // CHIP) == me // 2
    out = listed(out, CROSS, jnp.where(here, cross_at, -1.0), place, ZMOST)
    came = jnp.sum(jnp.where(zed == my_plane, cross_at, 0.0), axis=0, keepdims=True)
    away = CHIP + ZMOST * (((lane // in_plane) ^ my_plane) - 1)
    source = jnp.where((lane // in_plane) == my_plane, place, away.astype(jnp.float32) + came)
    partners = jnp.zeros((8, devices), jnp.bool_)
    for g, mask in enumerate(GIVES):
        partners = partners | ((zed == g) & (dev_r == my_plane * plane + (my_p ^ mask)))
    out = listed(out, GIVE, jnp.where(group_r == group_of(my_p), mm(ind(partners), bf(right_at)), -1.0), source, RMOST)

    left_me = jnp.sum(jnp.where(dev == me, left_at, 0.0), axis=0, keepdims=True)
    right_me = jnp.sum(jnp.where(dev == me, right_at, 0.0), axis=0, keepdims=True)
    held_a = jnp.where(here, place, CHIP + left_me)
    other_y = jnp.where((lane // per_row) % 2 == my_row % 2, 0.0, float(RMOST))
    held_b = as_column(jnp.where(mine, slot_r, CHIP + LMOST + other_y + right_me))
    my_product = product & (((sub // SLOTS) % cols) == my_col) & ((lane // per_row) == my_row)
    rank = mm(ind(lane < sub), ind(my_product))
    code = (hit - 1.0) * 256.0 + held_a * 64.0 + held_b + 1.0
    for k in range(2 * ACT):
        one = jnp.sum(jnp.where(my_product & (rank == k), code, 0.0), axis=0, keepdims=True)
        one = sum(one[:, i : i + BS] for i in range(0, n, BS))
        out = jnp.where(out_sub == k, one, out)
    table_ref[...] = out.astype(jnp.int32) - 1


def copy_listed(table_ref, row, first_lane, most, height, sources, to_ref):
    for k in range(most):
        at = table_ref[4 + row, first_lane + k]

        @pl.when(at >= 0)
        def _():
            for ref, first, count, stride, skip in sources:

                @pl.when((at >= first) & (at < first + count))
                def _():
                    here = pl.ds(pl.multiple_of((at - first) * stride + skip, height), height)
                    to_ref[k * height : (k + 1) * height, :] = ref[here, :]


def chip_halves(blocks_ref, other_ref):
    skip = piece_of(lax.axis_index(("y", "col"))) * (BS // 2)
    return [(blocks_ref, 0, SLOTS, BS, skip), (other_ref, SLOTS, SLOTS, BS, skip)]


def cross_kernel(most, table_ref, blocks_ref, other_ref, *outs):
    for m, out_ref in enumerate(outs):
        row = lax.axis_index("z") ^ (m + 1)
        copy_listed(table_ref, row, CROSS, most[m], BS // 2, chip_halves(blocks_ref, other_ref), out_ref)


def left_kernel(most, table_ref, blocks_ref, other_ref, out_ref):
    sources = [(blocks_ref, 0, SLOTS, BS, 0), (other_ref, SLOTS, SLOTS, BS, 0)]
    copy_listed(table_ref, 0, LEFTS, most, BS, sources, out_ref)


def give_kernel(planes, zmost, most, table_ref, blocks_ref, other_ref, *refs):
    sources = chip_halves(blocks_ref, other_ref)
    sources += [(ref, CHIP + m * ZMOST, zmost[m], BS // 2, 0) for m, ref in enumerate(refs[: planes - 1])]
    for g, out_ref in enumerate(refs[planes - 1 :]):
        copy_listed(table_ref, g, GIVE, most[g // 2], BS // 2, sources, out_ref)


def add_products(entries, table_ref, left_ref, first_left, right_ref, first_right, out_ref, wanted):

    def block(held_ref, at):
        x = held_ref[pl.ds(pl.multiple_of(at * BS, BS), BS), :]
        high = bf(x)
        return high, bf(x - high.astype(jnp.float32))

    def one(i, k):
        code = table_ref[k, i]
        a, b = (code // 64) % 64, code % 64

        @pl.when((code >= 0) & wanted(a, b))
        def _():
            a_high, a_low = block(left_ref, a - first_left)
            b_high, b_low = block(right_ref, b - first_right)
            at = pl.ds(pl.multiple_of((code // 4096) * BS, BS), BS)
            out_ref[at, :] += mm(
                jnp.concatenate([a_high, a_high, a_low], axis=1), jnp.concatenate([b_high, b_low, b_high], axis=0)
            )

        if k + 1 < 2 * ACT:

            @pl.when(code >= 0)
            def _():
                one(i, k + 1)

    def entry(i, carry):
        one(i, 0)
        return carry

    lax.fori_loop(*entries, entry, 0)


def first_entry(cols):
    return (2 * lax.axis_index("z") + lax.axis_index("y")) * cols * SLOTS % BS


def chip_entries(cols, cores):
    for core in cores:
        first = first_entry(cols) + (lax.axis_index("col") ^ core) * SLOTS
        yield core, (first, first + SLOTS)


def own_kernel(cols, table_ref, blocks_ref, other_ref, out_ref):
    out_ref[...] = jnp.zeros_like(out_ref)
    wanted = lambda a, b: b < SLOTS
    for core, entries in chip_entries(cols, (0, 1)):
        left_ref = (blocks_ref, other_ref)[core]
        add_products(entries, table_ref, left_ref, core * SLOTS, blocks_ref, 0, out_ref, wanted)


def across_kernel(cols, table_ref, left_ref, blocks_ref, start_ref, out_ref):
    out_ref[...] = start_ref[...]
    wanted = lambda a, b: b < SLOTS
    for _, entries in chip_entries(cols, (2, 3)):
        add_products(entries, table_ref, left_ref, CHIP, blocks_ref, 0, out_ref, wanted)


def product_kernel(cols, rmost, table_ref, blocks_ref, other_ref, start_ref, left_ref, *refs):
    right_refs, (out_ref, held_ref) = refs[: len(GIVES)], refs[len(GIVES) :]
    half = BS // 2
    mine = piece_of(lax.axis_index(("y", "col")))
    for g, ref in enumerate(right_refs):
        for k in range(rmost[g // 2]):
            to = (g // 2 * RMOST + k) * BS + (mine ^ (g % 2)) * half
            held_ref[pl.ds(pl.multiple_of(to, half), half), :] = ref[k * half : (k + 1) * half, :]
    out_ref[...] = start_ref[...]
    wanted = lambda a, b: b >= SLOTS
    for core, entries in chip_entries(cols, range(4)):
        left, first = ((blocks_ref, 0), (other_ref, SLOTS), (left_ref, CHIP), (left_ref, CHIP))[core]
        add_products(entries, table_ref, left, first, held_ref, CHIP + LMOST, out_ref, wanted)


def swapped(x, axis, mask):
    return lax.ppermute(x, axis, [(i, i ^ mask) for i in range(lax.axis_size(axis))])


def packed_body(blocks, block_rows, block_cols):
    planes, cols = lax.axis_size("z"), lax.axis_size("col")
    rows = 2 * planes
    plane = 2 * cols
    devices = rows * cols
    n = devices * SLOTS
    half = BS // 2
    in_plane = ("y", "col")
    flat = blocks.reshape(SLOTS * BS, BS)
    params = pltpu.CompilerParams(vmem_limit_bytes=VMEM_LIMIT)
    vmem = pl.BlockSpec(memory_space=pltpu.VMEM)
    smem = pl.BlockSpec(memory_space=pltpu.SMEM)

    long = pl.CostEstimate(flops=20_000_000_000, bytes_accessed=100_000, transcendentals=0)

    def floats(height):
        return jax.ShapeDtypeStruct((height, BS), jnp.float32)

    def ints(*shape):
        return jax.ShapeDtypeStruct(shape, jnp.int32)

    def call(kernel, name, ins, outs, scratch=(), specs=None, cost=None):
        return pl.pallas_call(
            kernel,
            out_shape=outs,
            in_specs=ins,
            out_specs=[vmem] * len(outs) if specs is None else specs,
            scratch_shapes=scratch,
            compiler_params=params,
            cost_estimate=cost,
            name=name,
        )

    idx = jnp.concatenate([block_rows[0], block_cols[0]])
    idx = jnp.broadcast_to(idx[None], (devices, 2, SLOTS))
    idx, source = lax.optimization_barrier((idx, flat))
    other = swapped(source, in_plane, 1)
    idx = lax.all_to_all(idx, ("z", "y", "col"), 0, 0)
    table, size = call(
        lambda *refs: plan_kernel(rows, cols, *refs),
        "plan",
        [vmem],
        [ints(8, BS), ints(1, 1)],
        specs=[vmem, smem],
        cost=long,
    )(idx)

    def packed(lmost, rmost, zmost):
        crossing = call(
            lambda *refs: cross_kernel(zmost, *refs),
            "cross",
            [smem] + [vmem] * 2,
            [floats(most * half) for most in zmost],
        )(table, flat, other)
        later, *crossing = lax.optimization_barrier((table, *crossing))
        crossed = [swapped(crossing[m], "z", m + 1) for m in reversed(range(planes - 1))][::-1]
        leaving = call(
            lambda *refs: left_kernel(lmost, *refs), "left", [smem] + [vmem] * 2, [floats(lmost * BS)]
        )(later, flat, other)
        later, *leaving = lax.optimization_barrier((later, *leaving))
        own = call(lambda *refs: own_kernel(cols, *refs), "own", [smem] + [vmem] * 2, [floats(SLOTS * BS)])(
            later, flat, other
        )
        later, own = lax.optimization_barrier((later, own[0]))
        lefts = swapped(leaving[0], in_plane, 2)
        giving = call(
            lambda *refs: give_kernel(planes, zmost, rmost, *refs),
            "give",
            [smem] + [vmem] * (2 + planes - 1),
            [floats(rmost[g // 2] * half) for g in range(len(GIVES))],
            cost=long,
        )(later, flat, other, *crossed)
        rights = [swapped(x, in_plane, mask) if mask else x for x, mask in reversed(list(zip(giving, GIVES)))][::-1]
        own = call(
            lambda *refs: across_kernel(cols, *refs), "across", [smem] + [vmem] * 3, [floats(SLOTS * BS)]
        )(later, lefts, flat, own)
        out = call(
            lambda *refs: product_kernel(cols, rmost, *refs),
            "products",
            [smem] + [vmem] * (4 + len(GIVES)),
            [floats(SLOTS * BS)],
            [pltpu.VMEM(((RMOST + rmost[1]) * BS, BS), jnp.float32)],
        )(later, flat, other, *own, lefts, *rights)
        return out[0].reshape(blocks.shape)

    branches = [lambda most=most: packed(*most) for most in SIZES]
    return lax.switch(size[0, 0], branches + [lambda: whole_tiles(blocks, block_rows, block_cols)])


def solution(mesh):
    rows, cols = mesh.devices.shape
    if cols == SECTIONS and rows == 2 * SECTIONS:
        body, row = packed_body, ("z", "y")
        mesh = jax.sharding.Mesh(mesh.devices.reshape(rows // 2, 2, cols), ("z", "y", "col"))
    else:
        body, row = general_body, "row"
    return jax.shard_map(
        body,
        mesh=mesh,
        in_specs=(P(row, "col", None, None, None), P(row, "col", None), P(row, "col", None)),
        out_specs=P(row, "col", None, None, None),
        check_vma=False,
    )
```

```python
import jax
import jax.numpy as jnp
from jax import lax
from jax.experimental import pallas as pl
from jax.experimental.pallas import tpu as pltpu
from jax.sharding import PartitionSpec as P

NBLK = 512
ACT = 2
SECTIONS = 4
BS = 128
SLOTS = 8
SIZES = (
    (4, (3, 2), (4, 2, 2)),
    (4, (3, 2), (4, 2, 3)),
    (4, (3, 2), (4, 3, 2)),
    (4, (3, 3), (4, 3, 3)),
    (5, (4, 3), (5, 3, 4)),
    (5, (4, 3), (5, 4, 3)),
    (5, (4, 4), (5, 4, 4)),
    (8, (8, 8), (8, 8, 8)),
)
LMOST, RMOST, ZMOST = 8, 8, 8
LEFTS, CROSS, GIVE = 0, 16, 32
VMEM_LIMIT = 32 * 1024 * 1024


def from_root(x, axis, root):
    mine = lax.axis_index(axis) == root
    return lax.psum(jnp.where(mine, x, jnp.zeros_like(x)), axis)


def from_partner(x, axis, bit):
    return lax.ppermute(x, axis, [(i, i ^ 1 << bit) for i in range(lax.axis_size(axis))])


def shifted(value, axis, steps):
    count = lax.axis_size(axis)
    pairs = [(source, (source + steps) % count) for source in range(count)]
    return lax.ppermute(value, axis, pairs)


def section_product(panel, pair, out_rows, out_cols, depth):
    panel_vals, panel_rows, panel_cols = panel
    pair_vals, pair_inner, pair_cols = pair
    panel_iota = jnp.arange(panel_rows.shape[0], dtype=jnp.int32)
    pair_iota = jnp.arange(pair_inner.shape[0], dtype=jnp.int32)
    depth_iota = jnp.arange(depth, dtype=jnp.int32)
    panel_live = panel_rows >= 0
    earlier = (
        (panel_rows[None, :] == panel_rows[:, None])
        & panel_live[None, :]
        & (panel_iota[None, :] < panel_iota[:, None])
    )
    within = jnp.sum(earlier.astype(jnp.int32), axis=1)
    picked = (panel_rows[None, None, :] == out_rows[:, None, None]) & (
        within[None, None, :] == depth_iota[None, :, None]
    )
    picked = picked & panel_live[None, None, :] & (out_rows >= 0)[:, None, None]
    picked_int = picked.astype(jnp.int32)
    panel_slot = jnp.sum(picked_int * panel_iota[None, None, :], axis=2)
    found = jnp.sum(picked_int, axis=2) > 0
    inner = jnp.sum(picked_int * panel_cols[None, None, :], axis=2)
    matched = (pair_inner[None, None, :] == inner[:, :, None]) & (
        pair_cols[None, None, :] == out_cols[:, None, None]
    )
    matched = matched & (pair_inner >= 0)[None, None, :] & found[:, :, None]
    matched_int = matched.astype(jnp.int32)
    pair_slot = jnp.sum(matched_int * pair_iota[None, None, :], axis=2)
    weight = (jnp.sum(matched_int, axis=2) > 0).astype(jnp.float32)
    left = panel_vals[panel_slot] * weight[:, :, None, None]
    right = pair_vals[pair_slot]
    return jnp.einsum(
        "tqij,tqjk->tik",
        left,
        right,
        precision=lax.Precision.HIGHEST,
        preferred_element_type=jnp.float32,
    )


def make_pair(first, second, row_span):
    inner = jnp.concatenate([first[1], jnp.where(second[1] >= 0, second[1] + row_span, -1)])
    return (jnp.concatenate([first[0], second[0]]), inner, jnp.concatenate([first[2], second[2]]))


def order_pair(mine, other, is_even, row_span):
    first = tuple((jnp.where(is_even, one, two) for one, two in zip(mine, other)))
    second = tuple((jnp.where(is_even, two, one) for one, two in zip(mine, other)))
    return make_pair(first, second, row_span)


def fetch_panel(tile, row_index, col_count, section):
    root = (row_index // 2 + section) % col_count
    return tuple(from_root(one, "col", root) for one in tile)


def general_body(blocks, block_rows, block_cols):
    tile = (blocks[0, 0], block_rows[0, 0], block_cols[0, 0])
    row_count = lax.axis_size("row")
    col_count = lax.axis_size("col")
    row_span = NBLK // row_count
    row_index = lax.axis_index("row")
    is_even = row_index % 2 == 0
    depth = 2 * ACT
    total = jnp.zeros(blocks.shape[2:], jnp.float32)
    partner = from_partner((tile[0], tile[1], tile[2]), "row", 0)
    current = order_pair(tile, partner, is_even, row_span)
    for section in range(SECTIONS):
        panel = fetch_panel(tile, row_index, col_count, section)
        if section > 0:
            current = shifted((current[0], current[1], current[2]), "row", -2)
        total = total + section_product(panel, current, tile[1], tile[2], depth)
    return total[None, None]


def everything(x, axis):
    return lax.all_to_all(jnp.broadcast_to(x[None], (lax.axis_size(axis),) + x.shape), axis, 0, 0)


def whole_tiles(blocks, block_rows, block_cols):
    tile = (blocks[0, 0], block_rows[0, 0], block_cols[0, 0])
    row_span = NBLK // lax.axis_size(("z", "y"))
    col_count = lax.axis_size("col")
    row_index = lax.axis_index(("z", "y"))
    panels = tuple(everything(one, "col") for one in tile)
    column = tuple(everything(one, ("z", "y")) for one in tile)

    def section(step, total):
        root = (row_index // 2 + step) % col_count
        take = lambda arrays, at: tuple(lax.dynamic_index_in_dim(a, at, 0, False) for a in arrays)
        pair = make_pair(take(column, 2 * root), take(column, 2 * root + 1), row_span)
        return total + section_product(take(panels, root), pair, tile[1], tile[2], 2 * ACT)

    total = lax.fori_loop(0, SECTIONS, section, jnp.zeros(blocks.shape[2:], jnp.float32))
    return total[None, None]


CHIP = 2 * SLOTS
GIVES = (0, 1, 4, 5)


def piece_of(p):
    return p % 2


def group_of(p):
    return p // 2


def bf(x):
    return x.astype(jnp.bfloat16)


def ind(x):
    return bf(jnp.where(x, 1.0, 0.0))


def mm(a, b, transposed=False):
    dims = (((1,), (1 if transposed else 0,)), ((), ()))
    return lax.dot_general(a, b, dims, preferred_element_type=jnp.float32)


def plan_kernel(rows, cols, idx_ref, table_ref, size_ref):
    devices = rows * cols
    plane = 2 * cols
    n = devices * SLOTS
    in_plane = plane * SLOTS
    rb = NBLK // rows
    cb = NBLK // cols
    per_row = cols * SLOTS
    my_plane, my_p = lax.axis_index("z"), lax.axis_index(("y", "col"))
    my_row = 2 * my_plane + lax.axis_index("y")
    my_col = lax.axis_index("col")
    me = my_row * cols + my_col

    sub = lax.broadcasted_iota(jnp.int32, (n, 1), 0)
    lane = lax.broadcasted_iota(jnp.int32, (1, n), 1)
    dev = lax.broadcasted_iota(jnp.int32, (devices, 1), 0)
    dev_r = lax.broadcasted_iota(jnp.int32, (1, devices), 1)
    slot = lax.broadcasted_iota(jnp.int32, (1, SLOTS), 1)
    diagonal = sub == lane

    def as_row(column):
        return jnp.sum(jnp.where(diagonal, column, 0.0), axis=0, keepdims=True)

    def as_column(row):
        return jnp.sum(jnp.where(diagonal, row, 0.0), axis=1, keepdims=True)

    repeat = ind((sub // SLOTS) == dev_r)

    def column(k):
        values = mm(repeat, bf(idx_ref[:, k, :].astype(jnp.float32)))
        return jnp.sum(jnp.where((sub % SLOTS) == slot, values, 0.0), axis=1, keepdims=True)

    up = ((sub // per_row) * rb).astype(jnp.float32)
    along = (((sub // SLOTS) % cols) * cb).astype(jnp.float32)
    row_c, col_c = column(0), column(1)
    row_c = jnp.where(row_c >= 0, row_c + up, -1.0)
    col_c = jnp.where(col_c >= 0, col_c + along, -2.0)
    row_r, col_r = as_row(row_c), as_row(col_c)

    slot_r = (lane % SLOTS).astype(jnp.float32)
    hit = mm(bf(jnp.where(col_c == col_r, 1.0 + 16.0 * slot_r, 0.0)), ind(row_c == row_r))
    product = (row_c == col_r) & (hit > 0)
    product_b = ind(product)

    in_row = (lane // per_row) == (dev // cols)
    in_col = ((lane // SLOTS) % cols) == (dev % cols)
    other = (lane // SLOTS) != dev
    left = in_row & other & (mm(ind(in_col), product_b) > 0)
    right = in_col & other & (mm(ind(in_row), product_b, transposed=True) > 0)
    before = sub < lane
    group_r = group_of((lane // SLOTS) % plane)
    same_group = group_of((sub // SLOTS) % plane) == group_r
    across = left & ((lane // CHIP) != (dev // 2))
    left_at = jnp.where(across, mm(ind(across), ind(before)), -1.0)
    right_at = jnp.where(right, mm(ind(right), ind(before & same_group)), -1.0)

    zed = lax.broadcasted_iota(jnp.int32, (8, 1), 0) - 4
    cross = (mm(ind((dev_r // plane) == zed), ind(right)) > 0) & ((lane // in_plane) != zed)
    together = same_group & ((sub // in_plane) == (lane // in_plane))
    cross_at = jnp.where(cross, mm(ind(cross), ind(before & together)), -1.0)

    left_top = jnp.max(left_at) + 1.0
    same_y = ((lane // per_row) % 2) == (dev // cols) % 2
    right_tops = [jnp.max(jnp.where(same_y == one, right_at, -1.0)) + 1.0 for one in (True, False)]
    step = (lane // in_plane) ^ zed
    cross_tops = [jnp.max(jnp.where(step == m + 1, cross_at, -1.0)) + 1.0 for m in range(rows // 2 - 1)]
    size = jnp.int32(len(SIZES))
    for i, (lmost, rmost, zmost) in reversed(list(enumerate(SIZES))):
        fits = left_top <= lmost
        for top, most in zip(right_tops + cross_tops, rmost + zmost):
            fits = fits & (top <= most)
        size = jnp.where(fits, i, size)
    size_ref[0, 0] = size

    lanes = lax.broadcasted_iota(jnp.int32, (1, BS), 1)
    out_sub = lax.broadcasted_iota(jnp.int32, (8, 1), 0)

    def listed(out, first, at, value, most):
        for k in range(most):
            one = jnp.sum(jnp.where(at == k, value + 1.0, 0.0), axis=1, keepdims=True)
            out = jnp.where((out_sub >= 4) & (lanes == first + k), one, out)
        return out

    out = jnp.zeros((8, BS), jnp.float32)
    zed = out_sub - 4
    mine = (lane // SLOTS) == me
    place = (lane % SLOTS + jnp.where(mine, 0, SLOTS)).astype(jnp.float32)
    to_across = jnp.sum(jnp.where(dev == (me ^ 2), left_at, 0.0), axis=0, keepdims=True)
    out = listed(out, LEFTS, jnp.where((lane // CHIP) == me // 2, to_across, -1.0), place, LMOST)
    here = (lane // CHIP) == me // 2
    out = listed(out, CROSS, jnp.where(here, cross_at, -1.0), place, ZMOST)
    came = jnp.sum(jnp.where(zed == my_plane, cross_at, 0.0), axis=0, keepdims=True)
    away = CHIP + ZMOST * (((lane // in_plane) ^ my_plane) - 1)
    source = jnp.where((lane // in_plane) == my_plane, place, away.astype(jnp.float32) + came)
    partners = jnp.zeros((8, devices), jnp.bool_)
    for g, mask in enumerate(GIVES):
        partners = partners | ((zed == g) & (dev_r == my_plane * plane + (my_p ^ mask)))
    out = listed(out, GIVE, jnp.where(group_r == group_of(my_p), mm(ind(partners), bf(right_at)), -1.0), source, RMOST)

    left_me = jnp.sum(jnp.where(dev == me, left_at, 0.0), axis=0, keepdims=True)
    right_me = jnp.sum(jnp.where(dev == me, right_at, 0.0), axis=0, keepdims=True)
    held_a = jnp.where(here, place, CHIP + left_me)
    other_y = jnp.where((lane // per_row) % 2 == my_row % 2, 0.0, float(RMOST))
    held_b = as_column(jnp.where(mine, slot_r, CHIP + LMOST + other_y + right_me))
    my_product = product & (((sub // SLOTS) % cols) == my_col) & ((lane // per_row) == my_row)
    rank = mm(ind(lane < sub), ind(my_product))
    code = (hit - 1.0) * 256.0 + held_a * 64.0 + held_b + 1.0
    for k in range(2 * ACT):
        one = jnp.sum(jnp.where(my_product & (rank == k), code, 0.0), axis=0, keepdims=True)
        one = sum(one[:, i : i + BS] for i in range(0, n, BS))
        out = jnp.where(out_sub == k, one, out)
    table_ref[...] = out.astype(jnp.int32) - 1


def copy_listed(table_ref, row, first_lane, most, height, sources, to_ref):
    for k in range(most):
        at = table_ref[4 + row, first_lane + k]

        @pl.when(at >= 0)
        def _():
            for ref, first, count, stride, skip in sources:

                @pl.when((at >= first) & (at < first + count))
                def _():
                    here = pl.ds(pl.multiple_of((at - first) * stride + skip, height), height)
                    to_ref[k * height : (k + 1) * height, :] = ref[here, :]


def chip_halves(blocks_ref, other_ref):
    skip = piece_of(lax.axis_index(("y", "col"))) * (BS // 2)
    return [(blocks_ref, 0, SLOTS, BS, skip), (other_ref, SLOTS, SLOTS, BS, skip)]


def cross_kernel(most, table_ref, blocks_ref, other_ref, *outs):
    for m, out_ref in enumerate(outs):
        row = lax.axis_index("z") ^ (m + 1)
        copy_listed(table_ref, row, CROSS, most[m], BS // 2, chip_halves(blocks_ref, other_ref), out_ref)


def left_kernel(most, table_ref, blocks_ref, other_ref, out_ref):
    sources = [(blocks_ref, 0, SLOTS, BS, 0), (other_ref, SLOTS, SLOTS, BS, 0)]
    copy_listed(table_ref, 0, LEFTS, most, BS, sources, out_ref)


def give_kernel(planes, zmost, most, table_ref, blocks_ref, other_ref, *refs):
    sources = chip_halves(blocks_ref, other_ref)
    sources += [(ref, CHIP + m * ZMOST, zmost[m], BS // 2, 0) for m, ref in enumerate(refs[: planes - 1])]
    for g, out_ref in enumerate(refs[planes - 1 :]):
        copy_listed(table_ref, g, GIVE, most[g // 2], BS // 2, sources, out_ref)


def add_products(entries, table_ref, left_ref, first_left, right_ref, first_right, out_ref, wanted):

    def block(held_ref, at):
        x = held_ref[pl.ds(pl.multiple_of(at * BS, BS), BS), :]
        high = bf(x)
        return high, bf(x - high.astype(jnp.float32))

    def one(i, k):
        code = table_ref[k, i]
        a, b = (code // 64) % 64, code % 64

        @pl.when((code >= 0) & wanted(a, b))
        def _():
            a_high, a_low = block(left_ref, a - first_left)
            b_high, b_low = block(right_ref, b - first_right)
            at = pl.ds(pl.multiple_of((code // 4096) * BS, BS), BS)
            out_ref[at, :] += mm(
                jnp.concatenate([a_high, a_high, a_low], axis=1), jnp.concatenate([b_high, b_low, b_high], axis=0)
            )

        if k + 1 < 2 * ACT:

            @pl.when(code >= 0)
            def _():
                one(i, k + 1)

    def entry(i, carry):
        one(i, 0)
        return carry

    lax.fori_loop(*entries, entry, 0)


def first_entry(cols):
    return (2 * lax.axis_index("z") + lax.axis_index("y")) * cols * SLOTS % BS


def chip_entries(cols, cores):
    for core in cores:
        first = first_entry(cols) + (lax.axis_index("col") ^ core) * SLOTS
        yield core, (first, first + SLOTS)


def own_kernel(cols, table_ref, blocks_ref, other_ref, out_ref):
    out_ref[...] = jnp.zeros_like(out_ref)
    wanted = lambda a, b: b < SLOTS
    for core, entries in chip_entries(cols, (0, 1)):
        left_ref = (blocks_ref, other_ref)[core]
        add_products(entries, table_ref, left_ref, core * SLOTS, blocks_ref, 0, out_ref, wanted)


def across_kernel(cols, table_ref, left_ref, blocks_ref, start_ref, out_ref):
    out_ref[...] = start_ref[...]
    wanted = lambda a, b: b < SLOTS
    for _, entries in chip_entries(cols, (2, 3)):
        add_products(entries, table_ref, left_ref, CHIP, blocks_ref, 0, out_ref, wanted)


def product_kernel(cols, rmost, table_ref, blocks_ref, other_ref, start_ref, left_ref, *refs):
    right_refs, (out_ref, held_ref) = refs[: len(GIVES)], refs[len(GIVES) :]
    half = BS // 2
    mine = piece_of(lax.axis_index(("y", "col")))
    for g, ref in enumerate(right_refs):
        for k in range(rmost[g // 2]):
            to = (g // 2 * RMOST + k) * BS + (mine ^ (g % 2)) * half
            held_ref[pl.ds(pl.multiple_of(to, half), half), :] = ref[k * half : (k + 1) * half, :]
    out_ref[...] = start_ref[...]
    wanted = lambda a, b: b >= SLOTS
    for core, entries in chip_entries(cols, range(4)):
        left, first = ((blocks_ref, 0), (other_ref, SLOTS), (left_ref, CHIP), (left_ref, CHIP))[core]
        add_products(entries, table_ref, left, first, held_ref, CHIP + LMOST, out_ref, wanted)


def swapped(x, axis, mask):
    return lax.ppermute(x, axis, [(i, i ^ mask) for i in range(lax.axis_size(axis))])


def packed_body(blocks, block_rows, block_cols):
    planes, cols = lax.axis_size("z"), lax.axis_size("col")
    rows = 2 * planes
    plane = 2 * cols
    devices = rows * cols
    n = devices * SLOTS
    half = BS // 2
    in_plane = ("y", "col")
    flat = blocks.reshape(SLOTS * BS, BS)
    params = pltpu.CompilerParams(vmem_limit_bytes=VMEM_LIMIT)
    vmem = pl.BlockSpec(memory_space=pltpu.VMEM)
    smem = pl.BlockSpec(memory_space=pltpu.SMEM)

    long = pl.CostEstimate(flops=20_000_000_000, bytes_accessed=100_000, transcendentals=0)

    def floats(height):
        return jax.ShapeDtypeStruct((height, BS), jnp.float32)

    def ints(*shape):
        return jax.ShapeDtypeStruct(shape, jnp.int32)

    def call(kernel, name, ins, outs, scratch=(), specs=None, cost=None):
        return pl.pallas_call(
            kernel,
            out_shape=outs,
            in_specs=ins,
            out_specs=[vmem] * len(outs) if specs is None else specs,
            scratch_shapes=scratch,
            compiler_params=params,
            cost_estimate=cost,
            name=name,
        )

    idx = jnp.concatenate([block_rows[0], block_cols[0]])
    idx = jnp.broadcast_to(idx[None], (devices, 2, SLOTS))
    idx, source = lax.optimization_barrier((idx, flat))
    other = swapped(source, in_plane, 1)
    idx = lax.all_to_all(idx, ("z", "y", "col"), 0, 0)
    table, size = call(
        lambda *refs: plan_kernel(rows, cols, *refs),
        "plan",
        [vmem],
        [ints(8, BS), ints(1, 1)],
        specs=[vmem, smem],
        cost=long,
    )(idx)

    def packed(lmost, rmost, zmost):
        crossing = call(
            lambda *refs: cross_kernel(zmost, *refs),
            "cross",
            [smem] + [vmem] * 2,
            [floats(most * half) for most in zmost],
        )(table, flat, other)
        later, *crossing = lax.optimization_barrier((table, *crossing))
        crossed = [swapped(crossing[m], "z", m + 1) for m in reversed(range(planes - 1))][::-1]
        leaving = call(
            lambda *refs: left_kernel(lmost, *refs), "left", [smem] + [vmem] * 2, [floats(lmost * BS)]
        )(later, flat, other)
        later, *leaving = lax.optimization_barrier((later, *leaving))
        own = call(lambda *refs: own_kernel(cols, *refs), "own", [smem] + [vmem] * 2, [floats(SLOTS * BS)])(
            later, flat, other
        )
        later, own = lax.optimization_barrier((later, own[0]))
        lefts = swapped(leaving[0], in_plane, 2)
        giving = call(
            lambda *refs: give_kernel(planes, zmost, rmost, *refs),
            "give",
            [smem] + [vmem] * (2 + planes - 1),
            [floats(rmost[g // 2] * half) for g in range(len(GIVES))],
            cost=long,
        )(later, flat, other, *crossed)
        rights = [swapped(x, in_plane, mask) if mask else x for x, mask in reversed(list(zip(giving, GIVES)))][::-1]
        own = call(
            lambda *refs: across_kernel(cols, *refs), "across", [smem] + [vmem] * 3, [floats(SLOTS * BS)]
        )(later, lefts, flat, own)
        out = call(
            lambda *refs: product_kernel(cols, rmost, *refs),
            "products",
            [smem] + [vmem] * (4 + len(GIVES)),
            [floats(SLOTS * BS)],
            [pltpu.VMEM(((RMOST + rmost[1]) * BS, BS), jnp.float32)],
        )(later, flat, other, *own, lefts, *rights)
        return out[0].reshape(blocks.shape)

    branches = [lambda most=most: packed(*most) for most in SIZES]
    return lax.switch(size[0, 0], branches + [lambda: whole_tiles(blocks, block_rows, block_cols)])


def solution(mesh):
    rows, cols = mesh.devices.shape
    if cols == SECTIONS and rows == 2 * SECTIONS:
        body, row = packed_body, ("z", "y")
        mesh = jax.sharding.Mesh(mesh.devices.reshape(rows // 2, 2, cols), ("z", "y", "col"))
    else:
        body, row = general_body, "row"
    return jax.shard_map(
        body,
        mesh=mesh,
        in_specs=(P(row, "col", None, None, None), P(row, "col", None), P(row, "col", None)),
        out_specs=P(row, "col", None, None, None),
        check_vma=False,
    )
```

```python
import jax
import jax.numpy as jnp
from jax import lax
from jax.experimental import pallas as pl
from jax.experimental.pallas import tpu as pltpu
from jax.sharding import PartitionSpec as P

NBLK = 512
ACT = 2
SECTIONS = 4
BS = 128
SLOTS = 8
SIZES = (
    (4, (3, 2), (4, 2, 2)),
    (4, (3, 2), (4, 2, 3)),
    (4, (3, 2), (4, 3, 2)),
    (4, (3, 3), (4, 3, 3)),
    (5, (4, 3), (5, 4, 4)),
    (6, (5, 5), (6, 5, 5)),
)
LMOST, RMOST, ZMOST = 6, 5, 6
LEFTS, CROSS, GIVE = 0, 16, 32
VMEM_LIMIT = 32 * 1024 * 1024


def from_root(x, axis, root):
    mine = lax.axis_index(axis) == root
    return lax.psum(jnp.where(mine, x, jnp.zeros_like(x)), axis)


def from_partner(x, axis, bit):
    return lax.ppermute(x, axis, [(i, i ^ 1 << bit) for i in range(lax.axis_size(axis))])


def shifted(value, axis, steps):
    count = lax.axis_size(axis)
    pairs = [(source, (source + steps) % count) for source in range(count)]
    return lax.ppermute(value, axis, pairs)


def section_product(panel, pair, out_rows, out_cols, depth):
    panel_vals, panel_rows, panel_cols = panel
    pair_vals, pair_inner, pair_cols = pair
    panel_iota = jnp.arange(panel_rows.shape[0], dtype=jnp.int32)
    pair_iota = jnp.arange(pair_inner.shape[0], dtype=jnp.int32)
    depth_iota = jnp.arange(depth, dtype=jnp.int32)
    panel_live = panel_rows >= 0
    earlier = (
        (panel_rows[None, :] == panel_rows[:, None])
        & panel_live[None, :]
        & (panel_iota[None, :] < panel_iota[:, None])
    )
    within = jnp.sum(earlier.astype(jnp.int32), axis=1)
    picked = (panel_rows[None, None, :] == out_rows[:, None, None]) & (
        within[None, None, :] == depth_iota[None, :, None]
    )
    picked = picked & panel_live[None, None, :] & (out_rows >= 0)[:, None, None]
    picked_int = picked.astype(jnp.int32)
    panel_slot = jnp.sum(picked_int * panel_iota[None, None, :], axis=2)
    found = jnp.sum(picked_int, axis=2) > 0
    inner = jnp.sum(picked_int * panel_cols[None, None, :], axis=2)
    matched = (pair_inner[None, None, :] == inner[:, :, None]) & (
        pair_cols[None, None, :] == out_cols[:, None, None]
    )
    matched = matched & (pair_inner >= 0)[None, None, :] & found[:, :, None]
    matched_int = matched.astype(jnp.int32)
    pair_slot = jnp.sum(matched_int * pair_iota[None, None, :], axis=2)
    weight = (jnp.sum(matched_int, axis=2) > 0).astype(jnp.float32)
    left = panel_vals[panel_slot] * weight[:, :, None, None]
    right = pair_vals[pair_slot]
    return jnp.einsum(
        "tqij,tqjk->tik",
        left,
        right,
        precision=lax.Precision.HIGHEST,
        preferred_element_type=jnp.float32,
    )


def make_pair(first, second, row_span):
    inner = jnp.concatenate([first[1], jnp.where(second[1] >= 0, second[1] + row_span, -1)])
    return (jnp.concatenate([first[0], second[0]]), inner, jnp.concatenate([first[2], second[2]]))


def order_pair(mine, other, is_even, row_span):
    first = tuple((jnp.where(is_even, one, two) for one, two in zip(mine, other)))
    second = tuple((jnp.where(is_even, two, one) for one, two in zip(mine, other)))
    return make_pair(first, second, row_span)


def fetch_panel(tile, row_index, col_count, section):
    root = (row_index // 2 + section) % col_count
    return tuple(from_root(one, "col", root) for one in tile)


def general_body(blocks, block_rows, block_cols):
    tile = (blocks[0, 0], block_rows[0, 0], block_cols[0, 0])
    row_count = lax.axis_size("row")
    col_count = lax.axis_size("col")
    row_span = NBLK // row_count
    row_index = lax.axis_index("row")
    is_even = row_index % 2 == 0
    depth = 2 * ACT
    total = jnp.zeros(blocks.shape[2:], jnp.float32)
    partner = from_partner((tile[0], tile[1], tile[2]), "row", 0)
    current = order_pair(tile, partner, is_even, row_span)
    for section in range(SECTIONS):
        panel = fetch_panel(tile, row_index, col_count, section)
        if section > 0:
            current = shifted((current[0], current[1], current[2]), "row", -2)
        total = total + section_product(panel, current, tile[1], tile[2], depth)
    return total[None, None]


def everything(x, axis):
    return lax.all_to_all(jnp.broadcast_to(x[None], (lax.axis_size(axis),) + x.shape), axis, 0, 0)


def whole_tiles(blocks, block_rows, block_cols):
    tile = (blocks[0, 0], block_rows[0, 0], block_cols[0, 0])
    row_span = NBLK // lax.axis_size(("z", "y"))
    col_count = lax.axis_size("col")
    row_index = lax.axis_index(("z", "y"))
    panels = tuple(everything(one, "col") for one in tile)
    column = tuple(everything(one, ("z", "y")) for one in tile)

    def section(step, total):
        root = (row_index // 2 + step) % col_count
        take = lambda arrays, at: tuple(lax.dynamic_index_in_dim(a, at, 0, False) for a in arrays)
        pair = make_pair(take(column, 2 * root), take(column, 2 * root + 1), row_span)
        return total + section_product(take(panels, root), pair, tile[1], tile[2], 2 * ACT)

    total = lax.fori_loop(0, SECTIONS, section, jnp.zeros(blocks.shape[2:], jnp.float32))
    return total[None, None]


CHIP = 2 * SLOTS
GIVES = (0, 1, 4, 5)


def piece_of(p):
    return p % 2


def group_of(p):
    return p // 2


def bf(x):
    return x.astype(jnp.bfloat16)


def ind(x):
    return bf(jnp.where(x, 1.0, 0.0))


def mm(a, b, transposed=False):
    dims = (((1,), (1 if transposed else 0,)), ((), ()))
    return lax.dot_general(a, b, dims, preferred_element_type=jnp.float32)


def plan_kernel(rows, cols, idx_ref, table_ref, size_ref):
    devices = rows * cols
    plane = 2 * cols
    n = devices * SLOTS
    in_plane = plane * SLOTS
    rb = NBLK // rows
    cb = NBLK // cols
    per_row = cols * SLOTS
    my_plane, my_p = lax.axis_index("z"), lax.axis_index(("y", "col"))
    my_row = 2 * my_plane + lax.axis_index("y")
    my_col = lax.axis_index("col")
    me = my_row * cols + my_col

    sub = lax.broadcasted_iota(jnp.int32, (n, 1), 0)
    lane = lax.broadcasted_iota(jnp.int32, (1, n), 1)
    dev = lax.broadcasted_iota(jnp.int32, (devices, 1), 0)
    dev_r = lax.broadcasted_iota(jnp.int32, (1, devices), 1)
    slot = lax.broadcasted_iota(jnp.int32, (1, SLOTS), 1)
    diagonal = sub == lane

    def as_row(column):
        return jnp.sum(jnp.where(diagonal, column, 0.0), axis=0, keepdims=True)

    def as_column(row):
        return jnp.sum(jnp.where(diagonal, row, 0.0), axis=1, keepdims=True)

    repeat = ind((sub // SLOTS) == dev_r)

    def column(k):
        values = mm(repeat, bf(idx_ref[:, k, :].astype(jnp.float32)))
        return jnp.sum(jnp.where((sub % SLOTS) == slot, values, 0.0), axis=1, keepdims=True)

    up = ((sub // per_row) * rb).astype(jnp.float32)
    along = (((sub // SLOTS) % cols) * cb).astype(jnp.float32)
    row_c, col_c = column(0), column(1)
    row_c = jnp.where(row_c >= 0, row_c + up, -1.0)
    col_c = jnp.where(col_c >= 0, col_c + along, -2.0)
    row_r, col_r = as_row(row_c), as_row(col_c)

    slot_r = (lane % SLOTS).astype(jnp.float32)
    hit = mm(bf(jnp.where(col_c == col_r, 1.0 + 16.0 * slot_r, 0.0)), ind(row_c == row_r))
    product = (row_c == col_r) & (hit > 0)
    product_b = ind(product)

    in_row = (lane // per_row) == (dev // cols)
    in_col = ((lane // SLOTS) % cols) == (dev % cols)
    other = (lane // SLOTS) != dev
    left = in_row & other & (mm(ind(in_col), product_b) > 0)
    right = in_col & other & (mm(ind(in_row), product_b, transposed=True) > 0)
    before = sub < lane
    group_r = group_of((lane // SLOTS) % plane)
    same_group = group_of((sub // SLOTS) % plane) == group_r
    across = left & ((lane // CHIP) != (dev // 2))
    left_at = jnp.where(across, mm(ind(across), ind(before)), -1.0)
    right_at = jnp.where(right, mm(ind(right), ind(before & same_group)), -1.0)

    zed = lax.broadcasted_iota(jnp.int32, (8, 1), 0) - 4
    cross = (mm(ind((dev_r // plane) == zed), ind(right)) > 0) & ((lane // in_plane) != zed)
    together = same_group & ((sub // in_plane) == (lane // in_plane))
    cross_at = jnp.where(cross, mm(ind(cross), ind(before & together)), -1.0)

    left_top = jnp.max(left_at) + 1.0
    same_y = ((lane // per_row) % 2) == (dev // cols) % 2
    right_tops = [jnp.max(jnp.where(same_y == one, right_at, -1.0)) + 1.0 for one in (True, False)]
    step = (lane // in_plane) ^ zed
    cross_tops = [jnp.max(jnp.where(step == m + 1, cross_at, -1.0)) + 1.0 for m in range(rows // 2 - 1)]
    size = jnp.int32(len(SIZES))
    for i, (lmost, rmost, zmost) in reversed(list(enumerate(SIZES))):
        fits = left_top <= lmost
        for top, most in zip(right_tops + cross_tops, rmost + zmost):
            fits = fits & (top <= most)
        size = jnp.where(fits, i, size)
    size_ref[0, 0] = size

    lanes = lax.broadcasted_iota(jnp.int32, (1, BS), 1)
    out_sub = lax.broadcasted_iota(jnp.int32, (8, 1), 0)

    def listed(out, first, at, value, most):
        for k in range(most):
            one = jnp.sum(jnp.where(at == k, value + 1.0, 0.0), axis=1, keepdims=True)
            out = jnp.where((out_sub >= 4) & (lanes == first + k), one, out)
        return out

    out = jnp.zeros((8, BS), jnp.float32)
    zed = out_sub - 4
    mine = (lane // SLOTS) == me
    place = (lane % SLOTS + jnp.where(mine, 0, SLOTS)).astype(jnp.float32)
    to_across = jnp.sum(jnp.where(dev == (me ^ 2), left_at, 0.0), axis=0, keepdims=True)
    out = listed(out, LEFTS, jnp.where((lane // CHIP) == me // 2, to_across, -1.0), place, LMOST)
    here = (lane // CHIP) == me // 2
    out = listed(out, CROSS, jnp.where(here, cross_at, -1.0), place, ZMOST)
    came = jnp.sum(jnp.where(zed == my_plane, cross_at, 0.0), axis=0, keepdims=True)
    away = CHIP + ZMOST * (((lane // in_plane) ^ my_plane) - 1)
    source = jnp.where((lane // in_plane) == my_plane, place, away.astype(jnp.float32) + came)
    partners = jnp.zeros((8, devices), jnp.bool_)
    for g, mask in enumerate(GIVES):
        partners = partners | ((zed == g) & (dev_r == my_plane * plane + (my_p ^ mask)))
    out = listed(out, GIVE, jnp.where(group_r == group_of(my_p), mm(ind(partners), bf(right_at)), -1.0), source, RMOST)

    left_me = jnp.sum(jnp.where(dev == me, left_at, 0.0), axis=0, keepdims=True)
    right_me = jnp.sum(jnp.where(dev == me, right_at, 0.0), axis=0, keepdims=True)
    held_a = jnp.where(here, place, CHIP + left_me)
    other_y = jnp.where((lane // per_row) % 2 == my_row % 2, 0.0, float(RMOST))
    held_b = as_column(jnp.where(mine, slot_r, CHIP + LMOST + other_y + right_me))
    my_product = product & (((sub // SLOTS) % cols) == my_col) & ((lane // per_row) == my_row)
    rank = mm(ind(lane < sub), ind(my_product))
    code = (hit - 1.0) * 256.0 + held_a * 64.0 + held_b + 1.0
    for k in range(2 * ACT):
        one = jnp.sum(jnp.where(my_product & (rank == k), code, 0.0), axis=0, keepdims=True)
        one = sum(one[:, i : i + BS] for i in range(0, n, BS))
        out = jnp.where(out_sub == k, one, out)
    table_ref[...] = out.astype(jnp.int32) - 1


def copy_listed(table_ref, row, first_lane, most, height, sources, to_ref):
    for k in range(most):
        at = table_ref[4 + row, first_lane + k]

        @pl.when(at >= 0)
        def _():
            for ref, first, count, stride, skip in sources:

                @pl.when((at >= first) & (at < first + count))
                def _():
                    here = pl.ds(pl.multiple_of((at - first) * stride + skip, height), height)
                    to_ref[k * height : (k + 1) * height, :] = ref[here, :]


def chip_halves(blocks_ref, other_ref):
    skip = piece_of(lax.axis_index(("y", "col"))) * (BS // 2)
    return [(blocks_ref, 0, SLOTS, BS, skip), (other_ref, SLOTS, SLOTS, BS, skip)]


def cross_kernel(most, table_ref, blocks_ref, other_ref, *outs):
    for m, out_ref in enumerate(outs):
        row = lax.axis_index("z") ^ (m + 1)
        copy_listed(table_ref, row, CROSS, most[m], BS // 2, chip_halves(blocks_ref, other_ref), out_ref)


def left_kernel(most, table_ref, blocks_ref, other_ref, out_ref):
    sources = [(blocks_ref, 0, SLOTS, BS, 0), (other_ref, SLOTS, SLOTS, BS, 0)]
    copy_listed(table_ref, 0, LEFTS, most, BS, sources, out_ref)


def give_kernel(planes, zmost, most, table_ref, blocks_ref, other_ref, *refs):
    sources = chip_halves(blocks_ref, other_ref)
    sources += [(ref, CHIP + m * ZMOST, zmost[m], BS // 2, 0) for m, ref in enumerate(refs[: planes - 1])]
    for g, out_ref in enumerate(refs[planes - 1 :]):
        copy_listed(table_ref, g, GIVE, most[g // 2], BS // 2, sources, out_ref)


def add_products(entries, table_ref, left_ref, first_left, right_ref, first_right, out_ref, wanted):

    def block(held_ref, at):
        x = held_ref[pl.ds(pl.multiple_of(at * BS, BS), BS), :]
        high = bf(x)
        return high, bf(x - high.astype(jnp.float32))

    def one(i, k):
        code = table_ref[k, i]
        a, b = (code // 64) % 64, code % 64

        @pl.when((code >= 0) & wanted(a, b))
        def _():
            a_high, a_low = block(left_ref, a - first_left)
            b_high, b_low = block(right_ref, b - first_right)
            at = pl.ds(pl.multiple_of((code // 4096) * BS, BS), BS)
            out_ref[at, :] += mm(
                jnp.concatenate([a_high, a_high, a_low], axis=1), jnp.concatenate([b_high, b_low, b_high], axis=0)
            )

        if k + 1 < 2 * ACT:

            @pl.when(code >= 0)
            def _():
                one(i, k + 1)

    def entry(i, carry):
        one(i, 0)
        return carry

    lax.fori_loop(*entries, entry, 0)


def first_entry(cols):
    return (2 * lax.axis_index("z") + lax.axis_index("y")) * cols * SLOTS % BS


def chip_entries(cols, cores):
    for core in cores:
        first = first_entry(cols) + (lax.axis_index("col") ^ core) * SLOTS
        yield core, (first, first + SLOTS)


def own_kernel(cols, table_ref, blocks_ref, other_ref, out_ref):
    out_ref[...] = jnp.zeros_like(out_ref)
    wanted = lambda a, b: b < SLOTS
    for core, entries in chip_entries(cols, (0, 1)):
        left_ref = (blocks_ref, other_ref)[core]
        add_products(entries, table_ref, left_ref, core * SLOTS, blocks_ref, 0, out_ref, wanted)


def across_kernel(cols, table_ref, left_ref, blocks_ref, start_ref, out_ref):
    out_ref[...] = start_ref[...]
    wanted = lambda a, b: b < SLOTS
    for _, entries in chip_entries(cols, (2, 3)):
        add_products(entries, table_ref, left_ref, CHIP, blocks_ref, 0, out_ref, wanted)


def product_kernel(cols, rmost, table_ref, blocks_ref, other_ref, start_ref, left_ref, *refs):
    right_refs, (out_ref, held_ref) = refs[: len(GIVES)], refs[len(GIVES) :]
    half = BS // 2
    mine = piece_of(lax.axis_index(("y", "col")))
    for g, ref in enumerate(right_refs):
        for k in range(rmost[g // 2]):
            to = (g // 2 * RMOST + k) * BS + (mine ^ (g % 2)) * half
            held_ref[pl.ds(pl.multiple_of(to, half), half), :] = ref[k * half : (k + 1) * half, :]
    out_ref[...] = start_ref[...]
    wanted = lambda a, b: b >= SLOTS
    for core, entries in chip_entries(cols, range(4)):
        left, first = ((blocks_ref, 0), (other_ref, SLOTS), (left_ref, CHIP), (left_ref, CHIP))[core]
        add_products(entries, table_ref, left, first, held_ref, CHIP + LMOST, out_ref, wanted)


def swapped(x, axis, mask):
    return lax.ppermute(x, axis, [(i, i ^ mask) for i in range(lax.axis_size(axis))])


def packed_body(blocks, block_rows, block_cols):
    planes, cols = lax.axis_size("z"), lax.axis_size("col")
    rows = 2 * planes
    plane = 2 * cols
    devices = rows * cols
    n = devices * SLOTS
    half = BS // 2
    in_plane = ("y", "col")
    flat = blocks.reshape(SLOTS * BS, BS)
    params = pltpu.CompilerParams(vmem_limit_bytes=VMEM_LIMIT)
    vmem = pl.BlockSpec(memory_space=pltpu.VMEM)
    smem = pl.BlockSpec(memory_space=pltpu.SMEM)

    long = pl.CostEstimate(flops=20_000_000_000, bytes_accessed=100_000, transcendentals=0)

    def floats(height):
        return jax.ShapeDtypeStruct((height, BS), jnp.float32)

    def ints(*shape):
        return jax.ShapeDtypeStruct(shape, jnp.int32)

    def call(kernel, name, ins, outs, scratch=(), specs=None, cost=None):
        return pl.pallas_call(
            kernel,
            out_shape=outs,
            in_specs=ins,
            out_specs=[vmem] * len(outs) if specs is None else specs,
            scratch_shapes=scratch,
            compiler_params=params,
            cost_estimate=cost,
            name=name,
        )

    idx = jnp.concatenate([block_rows[0], block_cols[0]])
    idx = jnp.broadcast_to(idx[None], (devices, 2, SLOTS))
    idx, source = lax.optimization_barrier((idx, flat))
    other = swapped(source, in_plane, 1)
    idx = lax.all_to_all(idx, ("z", "y", "col"), 0, 0)
    table, size = call(
        lambda *refs: plan_kernel(rows, cols, *refs),
        "plan",
        [vmem],
        [ints(8, BS), ints(1, 1)],
        specs=[vmem, smem],
        cost=long,
    )(idx)

    def packed(lmost, rmost, zmost):
        crossing = call(
            lambda *refs: cross_kernel(zmost, *refs),
            "cross",
            [smem] + [vmem] * 2,
            [floats(most * half) for most in zmost],
        )(table, flat, other)
        later, *crossing = lax.optimization_barrier((table, *crossing))
        crossed = [swapped(crossing[m], "z", m + 1) for m in reversed(range(planes - 1))][::-1]
        leaving = call(
            lambda *refs: left_kernel(lmost, *refs), "left", [smem] + [vmem] * 2, [floats(lmost * BS)]
        )(later, flat, other)
        later, *leaving = lax.optimization_barrier((later, *leaving))
        own = call(lambda *refs: own_kernel(cols, *refs), "own", [smem] + [vmem] * 2, [floats(SLOTS * BS)])(
            later, flat, other
        )
        later, own = lax.optimization_barrier((later, own[0]))
        lefts = swapped(leaving[0], in_plane, 2)
        giving = call(
            lambda *refs: give_kernel(planes, zmost, rmost, *refs),
            "give",
            [smem] + [vmem] * (2 + planes - 1),
            [floats(rmost[g // 2] * half) for g in range(len(GIVES))],
            cost=long,
        )(later, flat, other, *crossed)
        rights = [swapped(x, in_plane, mask) if mask else x for x, mask in reversed(list(zip(giving, GIVES)))][::-1]
        own = call(
            lambda *refs: across_kernel(cols, *refs), "across", [smem] + [vmem] * 3, [floats(SLOTS * BS)]
        )(later, lefts, flat, own)
        out = call(
            lambda *refs: product_kernel(cols, rmost, *refs),
            "products",
            [smem] + [vmem] * (4 + len(GIVES)),
            [floats(SLOTS * BS)],
            [pltpu.VMEM(((RMOST + rmost[1]) * BS, BS), jnp.float32)],
        )(later, flat, other, *own, lefts, *rights)
        return out[0].reshape(blocks.shape)

    branches = [lambda most=most: packed(*most) for most in SIZES]
    return lax.switch(size[0, 0], branches + [lambda: whole_tiles(blocks, block_rows, block_cols)])


def solution(mesh):
    rows, cols = mesh.devices.shape
    if cols == SECTIONS and rows == 2 * SECTIONS:
        body, row = packed_body, ("z", "y")
        mesh = jax.sharding.Mesh(mesh.devices.reshape(rows // 2, 2, cols), ("z", "y", "col"))
    else:
        body, row = general_body, "row"
    return jax.shard_map(
        body,
        mesh=mesh,
        in_specs=(P(row, "col", None, None, None), P(row, "col", None), P(row, "col", None)),
        out_specs=P(row, "col", None, None, None),
        check_vma=False,
    )
```

```python
import jax
import jax.numpy as jnp
from jax import lax
from jax.experimental import pallas as pl
from jax.experimental.pallas import tpu as pltpu
from jax.sharding import PartitionSpec as P

NBLK = 512
ACT = 2
SECTIONS = 4
BS = 128
SLOTS = 8
SIZES = (
    (4, (3, 2), (4, 2, 2)),
    (4, (3, 2), (3, 2, 3)),
    (4, (3, 2), (3, 3, 2)),
    (4, (3, 3), (3, 3, 3)),
    (5, (4, 4), (5, 4, 4)),
    (8, (8, 8), (8, 8, 8)),
)
LMOST, RMOST, ZMOST = 8, 8, 8
LEFTS, CROSS, GIVE = 0, 16, 32
VMEM_LIMIT = 32 * 1024 * 1024


def from_root(x, axis, root):
    mine = lax.axis_index(axis) == root
    return lax.psum(jnp.where(mine, x, jnp.zeros_like(x)), axis)


def from_partner(x, axis, bit):
    return lax.ppermute(x, axis, [(i, i ^ 1 << bit) for i in range(lax.axis_size(axis))])


def shifted(value, axis, steps):
    count = lax.axis_size(axis)
    pairs = [(source, (source + steps) % count) for source in range(count)]
    return lax.ppermute(value, axis, pairs)


def section_product(panel, pair, out_rows, out_cols, depth):
    panel_vals, panel_rows, panel_cols = panel
    pair_vals, pair_inner, pair_cols = pair
    panel_iota = jnp.arange(panel_rows.shape[0], dtype=jnp.int32)
    pair_iota = jnp.arange(pair_inner.shape[0], dtype=jnp.int32)
    depth_iota = jnp.arange(depth, dtype=jnp.int32)
    panel_live = panel_rows >= 0
    earlier = (
        (panel_rows[None, :] == panel_rows[:, None])
        & panel_live[None, :]
        & (panel_iota[None, :] < panel_iota[:, None])
    )
    within = jnp.sum(earlier.astype(jnp.int32), axis=1)
    picked = (panel_rows[None, None, :] == out_rows[:, None, None]) & (
        within[None, None, :] == depth_iota[None, :, None]
    )
    picked = picked & panel_live[None, None, :] & (out_rows >= 0)[:, None, None]
    picked_int = picked.astype(jnp.int32)
    panel_slot = jnp.sum(picked_int * panel_iota[None, None, :], axis=2)
    found = jnp.sum(picked_int, axis=2) > 0
    inner = jnp.sum(picked_int * panel_cols[None, None, :], axis=2)
    matched = (pair_inner[None, None, :] == inner[:, :, None]) & (
        pair_cols[None, None, :] == out_cols[:, None, None]
    )
    matched = matched & (pair_inner >= 0)[None, None, :] & found[:, :, None]
    matched_int = matched.astype(jnp.int32)
    pair_slot = jnp.sum(matched_int * pair_iota[None, None, :], axis=2)
    weight = (jnp.sum(matched_int, axis=2) > 0).astype(jnp.float32)
    left = panel_vals[panel_slot] * weight[:, :, None, None]
    right = pair_vals[pair_slot]
    return jnp.einsum(
        "tqij,tqjk->tik",
        left,
        right,
        precision=lax.Precision.HIGHEST,
        preferred_element_type=jnp.float32,
    )


def make_pair(first, second, row_span):
    inner = jnp.concatenate([first[1], jnp.where(second[1] >= 0, second[1] + row_span, -1)])
    return (jnp.concatenate([first[0], second[0]]), inner, jnp.concatenate([first[2], second[2]]))


def order_pair(mine, other, is_even, row_span):
    first = tuple((jnp.where(is_even, one, two) for one, two in zip(mine, other)))
    second = tuple((jnp.where(is_even, two, one) for one, two in zip(mine, other)))
    return make_pair(first, second, row_span)


def fetch_panel(tile, row_index, col_count, section):
    root = (row_index // 2 + section) % col_count
    return tuple(from_root(one, "col", root) for one in tile)


def general_body(blocks, block_rows, block_cols):
    tile = (blocks[0, 0], block_rows[0, 0], block_cols[0, 0])
    row_count = lax.axis_size("row")
    col_count = lax.axis_size("col")
    row_span = NBLK // row_count
    row_index = lax.axis_index("row")
    is_even = row_index % 2 == 0
    depth = 2 * ACT
    total = jnp.zeros(blocks.shape[2:], jnp.float32)
    partner = from_partner((tile[0], tile[1], tile[2]), "row", 0)
    current = order_pair(tile, partner, is_even, row_span)
    for section in range(SECTIONS):
        panel = fetch_panel(tile, row_index, col_count, section)
        if section > 0:
            current = shifted((current[0], current[1], current[2]), "row", -2)
        total = total + section_product(panel, current, tile[1], tile[2], depth)
    return total[None, None]


def everything(x, axis):
    return lax.all_to_all(jnp.broadcast_to(x[None], (lax.axis_size(axis),) + x.shape), axis, 0, 0)


def whole_tiles(blocks, block_rows, block_cols):
    tile = (blocks[0, 0], block_rows[0, 0], block_cols[0, 0])
    row_span = NBLK // lax.axis_size(("z", "y"))
    col_count = lax.axis_size("col")
    row_index = lax.axis_index(("z", "y"))
    panels = tuple(everything(one, "col") for one in tile)
    column = tuple(everything(one, ("z", "y")) for one in tile)

    def section(step, total):
        root = (row_index // 2 + step) % col_count
        take = lambda arrays, at: tuple(lax.dynamic_index_in_dim(a, at, 0, False) for a in arrays)
        pair = make_pair(take(column, 2 * root), take(column, 2 * root + 1), row_span)
        return total + section_product(take(panels, root), pair, tile[1], tile[2], 2 * ACT)

    total = lax.fori_loop(0, SECTIONS, section, jnp.zeros(blocks.shape[2:], jnp.float32))
    return total[None, None]


CHIP = 2 * SLOTS
GIVES = (0, 1, 4, 5)


def piece_of(p):
    return p % 2


def group_of(p):
    return p // 2


def bf(x):
    return x.astype(jnp.bfloat16)


def ind(x):
    return bf(jnp.where(x, 1.0, 0.0))


def mm(a, b, transposed=False):
    dims = (((1,), (1 if transposed else 0,)), ((), ()))
    return lax.dot_general(a, b, dims, preferred_element_type=jnp.float32)


def plan_kernel(rows, cols, idx_ref, table_ref, size_ref):
    devices = rows * cols
    plane = 2 * cols
    n = devices * SLOTS
    in_plane = plane * SLOTS
    rb = NBLK // rows
    cb = NBLK // cols
    per_row = cols * SLOTS
    my_plane, my_p = lax.axis_index("z"), lax.axis_index(("y", "col"))
    my_row = 2 * my_plane + lax.axis_index("y")
    my_col = lax.axis_index("col")
    me = my_row * cols + my_col

    sub = lax.broadcasted_iota(jnp.int32, (n, 1), 0)
    lane = lax.broadcasted_iota(jnp.int32, (1, n), 1)
    dev = lax.broadcasted_iota(jnp.int32, (devices, 1), 0)
    dev_r = lax.broadcasted_iota(jnp.int32, (1, devices), 1)
    slot = lax.broadcasted_iota(jnp.int32, (1, SLOTS), 1)
    diagonal = sub == lane

    def as_row(column):
        return jnp.sum(jnp.where(diagonal, column, 0.0), axis=0, keepdims=True)

    def as_column(row):
        return jnp.sum(jnp.where(diagonal, row, 0.0), axis=1, keepdims=True)

    repeat = ind((sub // SLOTS) == dev_r)

    def column(k):
        values = mm(repeat, bf(idx_ref[:, k, :].astype(jnp.float32)))
        return jnp.sum(jnp.where((sub % SLOTS) == slot, values, 0.0), axis=1, keepdims=True)

    up = ((sub // per_row) * rb).astype(jnp.float32)
    along = (((sub // SLOTS) % cols) * cb).astype(jnp.float32)
    row_c, col_c = column(0), column(1)
    row_c = jnp.where(row_c >= 0, row_c + up, -1.0)
    col_c = jnp.where(col_c >= 0, col_c + along, -2.0)
    row_r, col_r = as_row(row_c), as_row(col_c)

    slot_r = (lane % SLOTS).astype(jnp.float32)
    hit = mm(bf(jnp.where(col_c == col_r, 1.0 + 16.0 * slot_r, 0.0)), ind(row_c == row_r))
    product = (row_c == col_r) & (hit > 0)
    product_b = ind(product)

    in_row = (lane // per_row) == (dev // cols)
    in_col = ((lane // SLOTS) % cols) == (dev % cols)
    other = (lane // SLOTS) != dev
    left = in_row & other & (mm(ind(in_col), product_b) > 0)
    right = in_col & other & (mm(ind(in_row), product_b, transposed=True) > 0)
    before = sub < lane
    group_r = group_of((lane // SLOTS) % plane)
    same_group = group_of((sub // SLOTS) % plane) == group_r
    across = left & ((lane // CHIP) != (dev // 2))
    left_at = jnp.where(across, mm(ind(across), ind(before)), -1.0)
    right_at = jnp.where(right, mm(ind(right), ind(before & same_group)), -1.0)

    zed = lax.broadcasted_iota(jnp.int32, (8, 1), 0) - 4
    cross = (mm(ind((dev_r // plane) == zed), ind(right)) > 0) & ((lane // in_plane) != zed)
    together = same_group & ((sub // in_plane) == (lane // in_plane))
    cross_at = jnp.where(cross, mm(ind(cross), ind(before & together)), -1.0)

    left_top = jnp.max(left_at) + 1.0
    same_y = ((lane // per_row) % 2) == (dev // cols) % 2
    right_tops = [jnp.max(jnp.where(same_y == one, right_at, -1.0)) + 1.0 for one in (True, False)]
    step = (lane // in_plane) ^ zed
    cross_tops = [jnp.max(jnp.where(step == m + 1, cross_at, -1.0)) + 1.0 for m in range(rows // 2 - 1)]
    size = jnp.int32(len(SIZES))
    for i, (lmost, rmost, zmost) in reversed(list(enumerate(SIZES))):
        fits = left_top <= lmost
        for top, most in zip(right_tops + cross_tops, rmost + zmost):
            fits = fits & (top <= most)
        size = jnp.where(fits, i, size)
    size_ref[0, 0] = size

    lanes = lax.broadcasted_iota(jnp.int32, (1, BS), 1)
    out_sub = lax.broadcasted_iota(jnp.int32, (8, 1), 0)

    def listed(out, first, at, value, most):
        for k in range(most):
            one = jnp.sum(jnp.where(at == k, value + 1.0, 0.0), axis=1, keepdims=True)
            out = jnp.where((out_sub >= 4) & (lanes == first + k), one, out)
        return out

    out = jnp.zeros((8, BS), jnp.float32)
    zed = out_sub - 4
    mine = (lane // SLOTS) == me
    place = (lane % SLOTS + jnp.where(mine, 0, SLOTS)).astype(jnp.float32)
    to_across = jnp.sum(jnp.where(dev == (me ^ 2), left_at, 0.0), axis=0, keepdims=True)
    out = listed(out, LEFTS, jnp.where((lane // CHIP) == me // 2, to_across, -1.0), place, LMOST)
    here = (lane // CHIP) == me // 2
    out = listed(out, CROSS, jnp.where(here, cross_at, -1.0), place, ZMOST)
    came = jnp.sum(jnp.where(zed == my_plane, cross_at, 0.0), axis=0, keepdims=True)
    away = CHIP + ZMOST * (((lane // in_plane) ^ my_plane) - 1)
    source = jnp.where((lane // in_plane) == my_plane, place, away.astype(jnp.float32) + came)
    partners = jnp.zeros((8, devices), jnp.bool_)
    for g, mask in enumerate(GIVES):
        partners = partners | ((zed == g) & (dev_r == my_plane * plane + (my_p ^ mask)))
    out = listed(out, GIVE, jnp.where(group_r == group_of(my_p), mm(ind(partners), bf(right_at)), -1.0), source, RMOST)

    left_me = jnp.sum(jnp.where(dev == me, left_at, 0.0), axis=0, keepdims=True)
    right_me = jnp.sum(jnp.where(dev == me, right_at, 0.0), axis=0, keepdims=True)
    held_a = jnp.where(here, place, CHIP + left_me)
    other_y = jnp.where((lane // per_row) % 2 == my_row % 2, 0.0, float(RMOST))
    held_b = as_column(jnp.where(mine, slot_r, CHIP + LMOST + other_y + right_me))
    my_product = product & (((sub // SLOTS) % cols) == my_col) & ((lane // per_row) == my_row)
    rank = mm(ind(lane < sub), ind(my_product))
    code = (hit - 1.0) * 256.0 + held_a * 64.0 + held_b + 1.0
    for k in range(2 * ACT):
        one = jnp.sum(jnp.where(my_product & (rank == k), code, 0.0), axis=0, keepdims=True)
        one = sum(one[:, i : i + BS] for i in range(0, n, BS))
        out = jnp.where(out_sub == k, one, out)
    table_ref[...] = out.astype(jnp.int32) - 1


def copy_listed(table_ref, row, first_lane, most, height, sources, to_ref):
    for k in range(most):
        at = table_ref[4 + row, first_lane + k]

        @pl.when(at >= 0)
        def _():
            for ref, first, count, stride, skip in sources:

                @pl.when((at >= first) & (at < first + count))
                def _():
                    here = pl.ds(pl.multiple_of((at - first) * stride + skip, height), height)
                    to_ref[k * height : (k + 1) * height, :] = ref[here, :]


def chip_halves(blocks_ref, other_ref):
    skip = piece_of(lax.axis_index(("y", "col"))) * (BS // 2)
    return [(blocks_ref, 0, SLOTS, BS, skip), (other_ref, SLOTS, SLOTS, BS, skip)]


def cross_kernel(most, table_ref, blocks_ref, other_ref, *outs):
    for m, out_ref in enumerate(outs):
        row = lax.axis_index("z") ^ (m + 1)
        copy_listed(table_ref, row, CROSS, most[m], BS // 2, chip_halves(blocks_ref, other_ref), out_ref)


def left_kernel(most, table_ref, blocks_ref, other_ref, out_ref):
    sources = [(blocks_ref, 0, SLOTS, BS, 0), (other_ref, SLOTS, SLOTS, BS, 0)]
    copy_listed(table_ref, 0, LEFTS, most, BS, sources, out_ref)


def give_kernel(planes, zmost, most, table_ref, blocks_ref, other_ref, *refs):
    sources = chip_halves(blocks_ref, other_ref)
    sources += [(ref, CHIP + m * ZMOST, zmost[m], BS // 2, 0) for m, ref in enumerate(refs[: planes - 1])]
    for g, out_ref in enumerate(refs[planes - 1 :]):
        copy_listed(table_ref, g, GIVE, most[g // 2], BS // 2, sources, out_ref)


def add_products(entries, table_ref, left_ref, first_left, right_ref, first_right, out_ref, wanted):

    def block(held_ref, at):
        x = held_ref[pl.ds(pl.multiple_of(at * BS, BS), BS), :]
        high = bf(x)
        return high, bf(x - high.astype(jnp.float32))

    def one(i, k):
        code = table_ref[k, i]
        a, b = (code // 64) % 64, code % 64

        @pl.when((code >= 0) & wanted(a, b))
        def _():
            a_high, a_low = block(left_ref, a - first_left)
            b_high, b_low = block(right_ref, b - first_right)
            at = pl.ds(pl.multiple_of((code // 4096) * BS, BS), BS)
            out_ref[at, :] += mm(
                jnp.concatenate([a_high, a_high, a_low], axis=1), jnp.concatenate([b_high, b_low, b_high], axis=0)
            )

        if k + 1 < 2 * ACT:

            @pl.when(code >= 0)
            def _():
                one(i, k + 1)

    def entry(i, carry):
        one(i, 0)
        return carry

    lax.fori_loop(*entries, entry, 0)


def first_entry(cols):
    return (2 * lax.axis_index("z") + lax.axis_index("y")) * cols * SLOTS % BS


def chip_entries(cols, cores):
    for core in cores:
        first = first_entry(cols) + (lax.axis_index("col") ^ core) * SLOTS
        yield core, (first, first + SLOTS)


def own_kernel(cols, table_ref, blocks_ref, other_ref, out_ref):
    out_ref[...] = jnp.zeros_like(out_ref)
    wanted = lambda a, b: b < SLOTS
    for core, entries in chip_entries(cols, (0, 1)):
        left_ref = (blocks_ref, other_ref)[core]
        add_products(entries, table_ref, left_ref, core * SLOTS, blocks_ref, 0, out_ref, wanted)


def across_kernel(cols, table_ref, left_ref, blocks_ref, start_ref, out_ref):
    out_ref[...] = start_ref[...]
    wanted = lambda a, b: b < SLOTS
    for _, entries in chip_entries(cols, (2, 3)):
        add_products(entries, table_ref, left_ref, CHIP, blocks_ref, 0, out_ref, wanted)


def product_kernel(cols, rmost, table_ref, blocks_ref, other_ref, start_ref, left_ref, *refs):
    right_refs, (out_ref, held_ref) = refs[: len(GIVES)], refs[len(GIVES) :]
    half = BS // 2
    mine = piece_of(lax.axis_index(("y", "col")))
    for g, ref in enumerate(right_refs):
        for k in range(rmost[g // 2]):
            to = (g // 2 * RMOST + k) * BS + (mine ^ (g % 2)) * half
            held_ref[pl.ds(pl.multiple_of(to, half), half), :] = ref[k * half : (k + 1) * half, :]
    out_ref[...] = start_ref[...]
    wanted = lambda a, b: b >= SLOTS
    for core, entries in chip_entries(cols, range(4)):
        left, first = ((blocks_ref, 0), (other_ref, SLOTS), (left_ref, CHIP), (left_ref, CHIP))[core]
        add_products(entries, table_ref, left, first, held_ref, CHIP + LMOST, out_ref, wanted)


def swapped(x, axis, mask):
    return lax.ppermute(x, axis, [(i, i ^ mask) for i in range(lax.axis_size(axis))])


def packed_body(blocks, block_rows, block_cols):
    planes, cols = lax.axis_size("z"), lax.axis_size("col")
    rows = 2 * planes
    plane = 2 * cols
    devices = rows * cols
    n = devices * SLOTS
    half = BS // 2
    in_plane = ("y", "col")
    flat = blocks.reshape(SLOTS * BS, BS)
    params = pltpu.CompilerParams(vmem_limit_bytes=VMEM_LIMIT)
    vmem = pl.BlockSpec(memory_space=pltpu.VMEM)
    smem = pl.BlockSpec(memory_space=pltpu.SMEM)

    long = pl.CostEstimate(flops=20_000_000_000, bytes_accessed=100_000, transcendentals=0)

    def floats(height):
        return jax.ShapeDtypeStruct((height, BS), jnp.float32)

    def ints(*shape):
        return jax.ShapeDtypeStruct(shape, jnp.int32)

    def call(kernel, name, ins, outs, scratch=(), specs=None, cost=None):
        return pl.pallas_call(
            kernel,
            out_shape=outs,
            in_specs=ins,
            out_specs=[vmem] * len(outs) if specs is None else specs,
            scratch_shapes=scratch,
            compiler_params=params,
            cost_estimate=cost,
            name=name,
        )

    idx = jnp.concatenate([block_rows[0], block_cols[0]])
    idx = jnp.broadcast_to(idx[None], (devices, 2, SLOTS))
    idx, source = lax.optimization_barrier((idx, flat))
    other = swapped(source, in_plane, 1)
    idx = lax.all_to_all(idx, ("z", "y", "col"), 0, 0)
    table, size = call(
        lambda *refs: plan_kernel(rows, cols, *refs),
        "plan",
        [vmem],
        [ints(8, BS), ints(1, 1)],
        specs=[vmem, smem],
        cost=long,
    )(idx)

    def packed(lmost, rmost, zmost):
        crossing = call(
            lambda *refs: cross_kernel(zmost, *refs),
            "cross",
            [smem] + [vmem] * 2,
            [floats(most * half) for most in zmost],
        )(table, flat, other)
        later, *crossing = lax.optimization_barrier((table, *crossing))
        crossed = [swapped(crossing[m], "z", m + 1) for m in reversed(range(planes - 1))][::-1]
        leaving = call(
            lambda *refs: left_kernel(lmost, *refs), "left", [smem] + [vmem] * 2, [floats(lmost * BS)]
        )(later, flat, other)
        later, *leaving = lax.optimization_barrier((later, *leaving))
        own = call(lambda *refs: own_kernel(cols, *refs), "own", [smem] + [vmem] * 2, [floats(SLOTS * BS)])(
            later, flat, other
        )
        later, own = lax.optimization_barrier((later, own[0]))
        lefts = swapped(leaving[0], in_plane, 2)
        giving = call(
            lambda *refs: give_kernel(planes, zmost, rmost, *refs),
            "give",
            [smem] + [vmem] * (2 + planes - 1),
            [floats(rmost[g // 2] * half) for g in range(len(GIVES))],
            cost=long,
        )(later, flat, other, *crossed)
        rights = [swapped(x, in_plane, mask) if mask else x for x, mask in reversed(list(zip(giving, GIVES)))][::-1]
        own = call(
            lambda *refs: across_kernel(cols, *refs), "across", [smem] + [vmem] * 3, [floats(SLOTS * BS)]
        )(later, lefts, flat, own)
        out = call(
            lambda *refs: product_kernel(cols, rmost, *refs),
            "products",
            [smem] + [vmem] * (4 + len(GIVES)),
            [floats(SLOTS * BS)],
            [pltpu.VMEM(((RMOST + rmost[1]) * BS, BS), jnp.float32)],
        )(later, flat, other, *own, lefts, *rights)
        return out[0].reshape(blocks.shape)

    branches = [lambda most=most: packed(*most) for most in SIZES]
    return lax.switch(size[0, 0], branches + [lambda: whole_tiles(blocks, block_rows, block_cols)])


def solution(mesh):
    rows, cols = mesh.devices.shape
    if cols == SECTIONS and rows == 2 * SECTIONS:
        body, row = packed_body, ("z", "y")
        mesh = jax.sharding.Mesh(mesh.devices.reshape(rows // 2, 2, cols), ("z", "y", "col"))
    else:
        body, row = general_body, "row"
    return jax.shard_map(
        body,
        mesh=mesh,
        in_specs=(P(row, "col", None, None, None), P(row, "col", None), P(row, "col", None)),
        out_specs=P(row, "col", None, None, None),
        check_vma=False,
    )
```
